32 devices in a mesh: dp: 8 (over z, x), blk: 4 (over y, core).
Axes of the slice: x: 2, y: 2, z: 4, core: 2. Of those that a mesh axis runs over, the one named last changes fastest.
Arguments:
- tokens: bfloat16 [62976, 512], P(('dp', 'blk')), may hold values from -6 to 6
- sides: int32 [32], P(('dp', 'blk')), may hold values from 5 to 9, as said below
- cpe_weight: bfloat16 [9, 512], replicated, may hold values from -2 to 2
- cpe_bias: bfloat16 [512], replicated, may hold values from -2 to 2
- norm1_gain: bfloat16 [512], replicated, may hold values from 0.5 to 1.5
- norm1_shift: bfloat16 [512], replicated, may hold values from -2 to 2
- w_qkv: bfloat16 [512, 1536], replicated, may hold values from -0.375 to 0.375
- query_bias: bfloat16 [512], replicated, may hold values from -2 to 2
- value_bias: bfloat16 [512], replicated, may hold values from -2 to 2
- crpe_small: bfloat16 [9, 128], replicated, may hold values from -1 to 1
- crpe_middle: bfloat16 [25, 192], replicated, may hold values from -0.625 to 0.625
- crpe_large: bfloat16 [49, 192], replicated, may hold values from -0.4375 to 0.4375
- crpe_bias: bfloat16 [512], replicated, may hold values from -2 to 2
- w_proj: bfloat16 [512, 512], replicated, may hold values from -0.375 to 0.375
- proj_bias: bfloat16 [512], replicated, may hold values from -2 to 2
- norm2_gain: bfloat16 [512], replicated, may hold values from 0.5 to 1.5
- norm2_shift: bfloat16 [512], replicated, may hold values from -2 to 2
- w_fc1: bfloat16 [512, 2048], P(None, 'blk'), may hold values from -0.25 to 0.25
- fc1_bias: bfloat16 [2048], P('blk'), may hold values from -2 to 2
- w_fc2: bfloat16 [2048, 512], P('blk'), may hold values from -0.1875 to 0.1875
- fc2_bias: bfloat16 [512], replicated, may hold values from -2 to 2
- cotangent: bfloat16 [62976, 512], P(('dp', 'blk')), may hold values from -6 to 6
Outputs:
- output: bfloat16 [62976, 512], P(('dp', 'blk'))
- grad_tokens: bfloat16 [62976, 512], P(('dp', 'blk'))
- grad_cpe_weight: float32 [9, 512], replicated
- grad_cpe_bias: float32 [512], replicated
- grad_norm1_gain: float32 [512], replicated
- grad_norm1_shift: float32 [512], replicated
- grad_w_qkv: float32 [512, 1536], replicated
- grad_query_bias: float32 [512], replicated
- grad_value_bias: float32 [512], replicated
- grad_crpe_small: float32 [9, 128], replicated
- grad_crpe_middle: float32 [25, 192], replicated
- grad_crpe_large: float32 [49, 192], replicated
- grad_crpe_bias: float32 [512], replicated
- grad_w_proj: float32 [512, 512], replicated
- grad_proj_bias: float32 [512], replicated
- grad_norm2_gain: float32 [512], replicated
- grad_norm2_shift: float32 [512], replicated
- grad_w_fc1: float32 [512, 2048], P(None, 'blk')
- grad_fc1_bias: float32 [2048], P('blk')
- grad_w_fc2: float32 [2048, 512], P('blk')
- grad_fc2_bias: float32 [512], replicated
The draws below stay inside these ranges and needn't reach their ends.
Inputs may be any that keep to these rules, and one draw needn't show every extreme that they name: Every image of batch group g has a patch grid of sides[g] x sides[g] cells, sides[g] odd; in every draw some group has 9 and some group 5.
All inputs are finite; a program needn't handle non-finite values.
Results may differ from the reference program's by a relative error of at most 0.014.
Values may be sent and summed in bfloat16 or wider, within the bound.
No kernel may reach another device: no remote copies, remote signals or barrier semaphores. Data moves between devices by JAX's collectives and lax.ppermute only.
A program may use at most 512 MiB of HBM per device.

```python
import jax
import jax.numpy as jnp
from jax import lax

C = 512
HEADS = 8
FF = 2048
HD = 64
GRID = 9
SLOT = 82
IMGS = 24
GROUPS = 32
ROWS = 62976
N_DP = 8
N_BLK = 4


def draw_sides(key, part):
    key = jax.random.fold_in(key, 11)
    picks = jax.random.randint(jax.random.fold_in(key, 1), (GROUPS,), 0, 3)
    order = jax.random.permutation(jax.random.fold_in(key, 2), GROUPS)
    picks = jnp.where(order == 0, 2, picks)
    picks = jnp.where(order == 1, 0, picks)
    return (5 + 2 * picks).astype(jnp.int32)


def steps_of(key, shape, pieces, least, high):
    level, own = 1.0, jax.random.fold_in(key, 6)
    for position, blocks in pieces:
        heights = jnp.exp(jax.random.uniform(jax.random.fold_in(own, position), (blocks,), jnp.float32, least / len(pieces), high / len(pieces)))
        level = level * jnp.repeat(heights, shape[position] // blocks).reshape([-1 if axis == position else 1 for axis in range(len(shape))])
    return level


def bell_draw(key, extent, deviation, bound, cuts=(), held_as=jnp.bfloat16):
    values = jax.random.normal(key, extent, jnp.float32) * deviation
    if len(cuts) > 0:
        values = steps_of(key, extent, cuts, -0.22, 0.18) * values
    return jnp.clip(values, min=-bound, max=bound).astype(held_as)


def setup_inputs(seed: int = 0) -> dict:
    arg_keys = jax.random.split(jax.random.key(seed), 23)
    return {
        "tokens": bell_draw(arg_keys[0], (ROWS, C), 1.0, 6.0, ((0, 32),)),
        "sides": draw_sides(jax.random.fold_in(arg_keys[22], 71), 0),
        "cpe_weight": bell_draw(arg_keys[2], (9, C), 9 ** -0.5, 2.0),
        "cpe_bias": bell_draw(arg_keys[3], (C,), 0.3, 2.0),
        "norm1_gain": jnp.clip(1.0 + 0.1 * jax.random.normal(arg_keys[4], (C,), jnp.float32), 0.5, 1.5).astype(jnp.bfloat16),
        "norm1_shift": bell_draw(arg_keys[5], (C,), 0.3, 2.0),
        "w_qkv": bell_draw(arg_keys[6], (C, 3 * C), (C // 2) ** -0.5, 0.375),
        "query_bias": bell_draw(arg_keys[7], (C,), 0.3, 2.0),
        "value_bias": bell_draw(arg_keys[8], (C,), 0.3, 2.0),
        "crpe_small": bell_draw(arg_keys[9], (9, 2 * HD), 36 ** -0.5, 1.0),
        "crpe_middle": bell_draw(arg_keys[10], (25, 3 * HD), 100 ** -0.5, 0.625),
        "crpe_large": bell_draw(arg_keys[11], (49, 3 * HD), 196 ** -0.5, 0.4375),
        "crpe_bias": bell_draw(arg_keys[12], (C,), 0.3, 2.0),
        "w_proj": bell_draw(arg_keys[13], (C, C), (C // 2) ** -0.5, 0.375),
        "proj_bias": bell_draw(arg_keys[14], (C,), 0.3, 2.0),
        "norm2_gain": jnp.clip(1.0 + 0.1 * jax.random.normal(arg_keys[15], (C,), jnp.float32), 0.5, 1.5).astype(jnp.bfloat16),
        "norm2_shift": bell_draw(arg_keys[16], (C,), 0.3, 2.0),
        "w_fc1": bell_draw(arg_keys[17], (C, FF), C ** -0.5, 0.25, ((1, 4),)),
        "fc1_bias": bell_draw(arg_keys[18], (FF,), 0.3, 2.0, ((0, 4),)),
        "w_fc2": bell_draw(arg_keys[19], (FF, C), (FF // 2) ** -0.5, 0.1875, ((0, 4),)),
        "fc2_bias": bell_draw(arg_keys[20], (C,), 0.3, 2.0),
        "cotangent": bell_draw(arg_keys[21], (ROWS, C), 1.0, 6.0, ((0, 32),)),
    }


epsilon = 1e-06
highest = lax.Precision.HIGHEST

@jax.custom_vjp
def low(v):
    return lax.optimization_barrier(v.astype(jnp.bfloat16)).astype(jnp.float32)

@jax.custom_vjp
def low_back(v):
    return v

def low_keep(v):
    return (low(v), None)

def low_pass(kept, grad):
    return (grad,)

def back_keep(v):
    return (v, None)

def back_low(kept, grad):
    return (low(grad),)
low.defvjp(low_keep, low_pass)
low_back.defvjp(back_keep, back_low)

def valid_rows(grid_side):
    positions = jnp.arange(GRID * GRID + 1, dtype=jnp.int32)
    cell_row = (positions - 1) // GRID
    cell_col = (positions - 1) % GRID
    inside = (positions == 0) | (cell_row < grid_side) & (cell_col < grid_side)
    return jnp.where(inside, 1.0, 0.0).astype(jnp.float32)

def depthwise(grid_cells, kernel, kernel_size):
    margin = kernel_size // 2
    padded = jnp.pad(grid_cells, ((0, 0), (margin, margin), (margin, margin), (0, 0)))
    summed = jnp.zeros_like(grid_cells)
    for row_tap in range(kernel_size):
        for col_tap in range(kernel_size):
            summed = summed + padded[:, row_tap:row_tap + GRID, col_tap:col_tap + GRID, :] * kernel[row_tap * kernel_size + col_tap]
    return summed

def layer_norm(values, norm_gain, norm_shift):
    average = lax.optimization_barrier(jnp.mean(values, -1, keepdims=True))
    centered = values - average
    variance = lax.optimization_barrier(jnp.mean(centered * centered, -1, keepdims=True))
    return centered * lax.rsqrt(variance + epsilon) * norm_gain + norm_shift

def assemble_kernel(small_kernel, middle_kernel, large_kernel):
    first_part = jnp.pad(small_kernel.reshape(3, 3, -1), ((2, 2), (2, 2), (0, 0)))
    second_part = jnp.pad(middle_kernel.reshape(5, 5, -1), ((1, 1), (1, 1), (0, 0)))
    third_part = large_kernel.reshape(7, 7, -1)
    return jnp.concatenate([first_part, second_part, third_part], 2).reshape(49, -1)

def front_part(values, valid_mask, cpe_kernel, cpe_shift, norm_gain, norm_shift):
    images, slots, channels = values.shape
    grid_cells = values[:, 1:, :].reshape(images, GRID, GRID, channels)
    convolved = (depthwise(grid_cells, cpe_kernel, 3) + cpe_shift).reshape(images, GRID * GRID, channels)
    class_rows = jnp.zeros((images, 1, channels), values.dtype)
    after_cpe = values + jnp.concatenate([class_rows, convolved], 1) * valid_mask
    return (after_cpe, layer_norm(after_cpe, norm_gain, norm_shift))

def mix_part(projected, valid_mask, small_kernel, middle_kernel, large_kernel, crpe_shift):
    images, slots, triple = projected.shape
    channels = triple // 3
    head_size = channels // HEADS
    queries = projected[..., :channels]
    key_part = projected[..., channels:2 * channels]
    value_rows = projected[..., 2 * channels:] * valid_mask
    masked = jnp.where(valid_mask > 0, key_part, -1e+30)
    highest_key = lax.optimization_barrier(jnp.max(masked, 1, keepdims=True))
    weights = jnp.exp(masked - highest_key) * valid_mask
    weights = weights / lax.optimization_barrier(jnp.sum(weights, 1, keepdims=True))
    query_heads = queries.reshape(images, slots, HEADS, head_size)
    weight_heads = weights.reshape(images, slots, HEADS, head_size)
    value_heads = value_rows.reshape(images, slots, HEADS, head_size)
    context = jnp.einsum('nshc,nshd->nhcd', weight_heads, value_heads, precision=highest)
    factor = jnp.einsum('nshc,nhcd->nshd', query_heads, context, precision=highest).reshape(images, slots, channels)
    kernel = assemble_kernel(small_kernel, middle_kernel, large_kernel)
    value_grid = value_rows[:, 1:, :].reshape(images, GRID, GRID, channels)
    convolved = (depthwise(value_grid, kernel, 7) + crpe_shift).reshape(images, GRID * GRID, channels)
    class_rows = jnp.zeros((images, 1, channels), projected.dtype)
    relative = jnp.concatenate([class_rows, queries[:, 1:, :] * convolved], 1)
    return factor * head_size ** (-0.5) + relative

def forward(values, valid_mask, params):
    cpe_kernel, cpe_shift, gain_one, shift_one, qkv_matrix, query_shift, value_shift, small_kernel, middle_kernel, large_kernel, crpe_shift, proj_matrix, proj_shift, gain_two, shift_two, fc1_matrix, fc1_shift, fc2_matrix, fc2_shift = params
    masked_in = values * valid_mask
    after_cpe, normed = front_part(masked_in, valid_mask, cpe_kernel, cpe_shift, gain_one, shift_one)
    normed = low(normed)
    zeros_row = jnp.zeros_like(query_shift)
    projected = jnp.einsum('nsc,ck->nsk', normed, qkv_matrix, precision=highest) + jnp.concatenate([query_shift, zeros_row, value_shift])
    projected = low_back(projected)
    attended = low(mix_part(projected, valid_mask, small_kernel, middle_kernel, large_kernel, crpe_shift))
    branch = low_back(jnp.einsum('nsc,cd->nsd', attended, proj_matrix, precision=highest) + proj_shift)
    second = after_cpe + branch
    normed_two = low(layer_norm(second, gain_two, shift_two))
    hidden_in = low_back(jnp.einsum('nsc,cf->nsf', normed_two, fc1_matrix, precision=highest) + fc1_shift)
    hidden = low(jax.nn.gelu(hidden_in, approximate=False))
    mlp_out = low_back(jnp.einsum('nsf,fc->nsc', hidden, fc2_matrix, precision=highest) + fc2_shift)
    return (second + mlp_out) * valid_mask

def reference(tokens, sides, cpe_weight, cpe_bias, norm1_gain, norm1_shift, w_qkv, query_bias, value_bias, crpe_small, crpe_middle, crpe_large, crpe_bias, w_proj, proj_bias, norm2_gain, norm2_shift, w_fc1, fc1_bias, w_fc2, fc2_bias, cotangent):
    params = (cpe_weight.astype(jnp.float32), cpe_bias.astype(jnp.float32), norm1_gain.astype(jnp.float32), norm1_shift.astype(jnp.float32), w_qkv.astype(jnp.float32), query_bias.astype(jnp.float32), value_bias.astype(jnp.float32), crpe_small.astype(jnp.float32), crpe_middle.astype(jnp.float32), crpe_large.astype(jnp.float32), crpe_bias.astype(jnp.float32), w_proj.astype(jnp.float32), proj_bias.astype(jnp.float32), norm2_gain.astype(jnp.float32), norm2_shift.astype(jnp.float32), w_fc1.astype(jnp.float32), fc1_bias.astype(jnp.float32), w_fc2.astype(jnp.float32), fc2_bias.astype(jnp.float32))
    channels = tokens.shape[1]
    group_count = N_DP * N_BLK
    stacked = tokens.astype(jnp.float32).reshape(group_count, IMGS, SLOT, channels)
    cot_stack = cotangent.astype(jnp.float32).reshape(group_count, IMGS, SLOT, channels)

    def device_step(totals, device_item):
        values, cot_values, grid_side = device_item
        valid_mask = valid_rows(grid_side)[None, :, None]

        def inner(value_in, param_in):
            return forward(value_in, valid_mask, param_in)
        result, pull_back = jax.vjp(inner, values, params)
        grad_values, grad_params = pull_back(cot_values)
        totals = jax.tree.map(jnp.add, totals, grad_params)
        return (totals, (result.astype(jnp.bfloat16), grad_values.astype(jnp.bfloat16)))
    zero_grads = jax.tree.map(jnp.zeros_like, params)
    grads, (results, grad_rows) = lax.scan(device_step, zero_grads, (stacked, cot_stack, sides))
    return (results.reshape(-1, channels), grad_rows.reshape(-1, channels), grads[0], grads[1], grads[2], grads[3], grads[4], grads[5], grads[6], grads[7], grads[8], grads[9], grads[10], grads[11], grads[12], grads[13], grads[14], grads[15], grads[16], grads[17], grads[18])
```

```python
import functools
import math

import jax
import jax.numpy as jnp
from jax import lax
from jax.experimental import pallas as pl
from jax.experimental.pallas import tpu as pltpu
from jax.sharding import PartitionSpec as P

HEADS = 8
GRID = 9
CELLS = GRID * GRID
SLOT = CELLS + 1
LANES = 128
EPSILON = 1e-6
SLOT_PAD = 96
TILE = 256
BAND = 128
MLP_TILE = 1024
KERNEL_SIZES = (3, 5, 7, 7)
PIECE = 256
VMEM_BYTES = 62 * 1024 * 1024

F32 = jnp.float32
BF16 = jnp.bfloat16

SMALL_ROWS = (56, 58, 49, 50, 64, 65, 66)
CPE_B, GAIN1, SHIFT1, QUERY_B, VALUE_B, CRPE_B, PROJ_B = range(7)
GAIN2, SHIFT2, FC2_B = range(3)


def dot(left, right):
    return lax.dot_general(left, right, (((1,), (0,)), ((), ())), preferred_element_type=F32)


def dot_nt(left, right):
    return lax.dot_general(left, right, (((1,), (1,)), ((), ())), preferred_element_type=F32)


def dot_tn(left, right):
    return lax.dot_general(left, right, (((0,), (0,)), ((), ())), preferred_element_type=F32)


class Copies:
    def __init__(self, sems):
        self.sems, self.count, self.open = sems, 0, []

    def start(self, source, target):
        copy = pltpu.make_async_copy(source, target, self.sems.at[self.count])
        self.count += 1
        copy.start()
        self.open.append(copy)
        return copy

    def finish(self):
        for copy in self.open:
            copy.wait()


def loop(count, body, unroll=1):
    def step(index, carry):
        body(index)
        return carry

    lax.fori_loop(0, count, step, 0, unroll=unroll)


def rows_at(start, count, multiple=8):
    return pl.ds(pl.multiple_of(start, multiple), count)


def lanes_of(block):
    return slice(block * LANES, (block + 1) * LANES)


def fold_rows(values):
    count, lanes = values.shape
    return jnp.sum(values.reshape(count // 8, 8, lanes), 0)


def fill_mask(side, mask_ref, images):
    mask_ref[SLOT * images :, :] = jnp.zeros_like(mask_ref[SLOT * images :, :])

    def body(slot):
        row = slot // GRID
        col = slot - row * GRID
        inside = (slot == CELLS) | ((row < side) & (col < side))
        level = jnp.where(inside, 1.0, 0.0).astype(F32)
        mask_ref[rows_at(slot * images, images), :] = jnp.full((images, LANES), level, F32)

    loop(SLOT, body)


def spread(rows_ref, blocks_ref, blocks):
    total = rows_ref.shape[0]

    def body(step):
        at = rows_at(step * 48, 48, 16)
        values = rows_ref[at, :].astype(F32)
        for block in range(blocks):
            blocks_ref[block, at, :] = values[:, lanes_of(block)]

    loop(total // 48, body)


def unspread(blocks_ref, rows_ref, blocks):
    total = rows_ref.shape[0]

    def body(step):
        at = rows_at(step * 48, 48, 16)
        values = [blocks_ref[block, at, :] for block in range(blocks)]
        rows_ref[at, :] = jnp.concatenate(values, 1).astype(BF16)

    loop(total // 48, body)


def natural_slot(slot):
    return jnp.where(slot == CELLS, 0, slot + 1)


def fill_table(vectors, table_ref):
    for row, ref in enumerate(vectors):
        table_ref[row : row + 1, :] = ref[...].astype(F32).reshape(1, -1)


def fill_taps(table, taps_ref, count, blocks):
    for tap in range(count):
        for block in range(blocks):
            taps_ref[block, tap] = jnp.broadcast_to(table[tap : tap + 1, lanes_of(block)], (8, LANES))


def centred(size):
    inset = (7 - size) // 2
    return [(a + inset) * 7 + b + inset for a in range(size) for b in range(size)]


def lane_picker(width, offset, channels):
    lane = lax.broadcasted_iota(jnp.int32, (width, channels), 0)
    channel = lax.broadcasted_iota(jnp.int32, (width, channels), 1)
    return jnp.where(channel == lane + offset, 1.0, 0.0).astype(BF16)


def assemble_taps(kernels, work_ref, table_ref):
    channels = table_ref.shape[1]
    table_ref[...] = jnp.zeros_like(table_ref)
    offset = 0
    for size, kernel_ref in zip((3, 5, 7), kernels):
        width = kernel_ref.shape[1]
        work_ref[0 : size * size, :] = dot(kernel_ref[...], lane_picker(width, offset, channels))
        for tap, place in enumerate(centred(size)):
            table_ref[place : place + 1, :] += work_ref[tap : tap + 1, :]
        offset += width


def correlate(source_ref, taps_ref, size, span, images, block, sub, emit, turned=False):
    margin, inset = size // 2, (span - size) // 2

    def load(cell):
        return source_ref[block, rows_at(cell * images + sub * 8, 8), :]

    for row in range(GRID):
        totals = [None] * GRID
        for a in range(size):
            from_row = row + a - margin
            if not 0 <= from_row < GRID:
                continue
            cells = [load(from_row * GRID + col) for col in range(GRID)]
            for b in range(size):
                tap = (a + inset) * span + b + inset
                weight = taps_ref[block, span * span - 1 - tap if turned else tap]
                for col in range(GRID):
                    from_col = col + b - margin
                    if 0 <= from_col < GRID:
                        term = cells[from_col] * weight
                        totals[col] = term if totals[col] is None else totals[col] + term
        for col in range(GRID):
            emit(row * GRID + col, totals[col])


def tap_sums(grad_ref, source_ref, sums_ref, size, span, images, block, sub):
    margin, inset = size // 2, (span - size) // 2

    def load(ref, cell):
        return ref[block, rows_at(cell * images + sub * 8, 8), :]

    for a in range(size):
        totals = [None] * size
        for row in range(GRID):
            from_row = row + a - margin
            if not 0 <= from_row < GRID:
                continue
            grads = [load(grad_ref, row * GRID + col) for col in range(GRID)]
            cells = [load(source_ref, from_row * GRID + col) for col in range(GRID)]
            for b in range(size):
                part = None
                for col in range(GRID):
                    from_col = col + b - margin
                    if 0 <= from_col < GRID:
                        term = grads[col] * cells[from_col]
                        part = term if part is None else part + term
                totals[b] = part if totals[b] is None else totals[b] + part
        for b in range(size):
            tap = (a + inset) * span + b + inset
            sums_ref[block, tap] += totals[b]


def by_block(images, body, before=None):
    subs = images // 8
    first = 0
    while first < len(KERNEL_SIZES):
        size = KERNEL_SIZES[first]
        count = 1
        while first + count < len(KERNEL_SIZES) and KERNEL_SIZES[first + count] == size:
            count += 1

        for block in range(first, first + count):
            if before is not None:
                before(block)

        def step(index, first=first, size=size):
            body(size, first + index // subs, index % subs)

        loop(count * subs, step)
        first += count


def row_sums(value):
    high = value.astype(BF16)
    low = (value - high.astype(F32)).astype(BF16)
    return dot(jnp.concatenate([high, low], 1), jnp.ones((2 * LANES, LANES), BF16))


def row_means(blocks):
    return row_sums(sum(blocks[1:], blocks[0])) * (1.0 / (len(blocks) * LANES))


def norm_parts(blocks):
    mean = row_means(blocks)
    centered = [value - mean for value in blocks]
    inverse = lax.rsqrt(row_means([value * value for value in centered]) + EPSILON)
    return [value * inverse for value in centered], inverse


def norm_forward(source_ref, table_ref, gain_row, shift_row, normed_ref, turned_ref, blocks):
    gains = table_ref[gain_row : gain_row + 1, :]
    shifts = table_ref[shift_row : shift_row + 1, :]

    def body(step):
        at = rows_at(step * BAND, BAND, BAND)
        parts, _ = norm_parts([source_ref[block, at, :] for block in range(blocks)])
        out = [
            parts[block] * gains[:, lanes_of(block)] + shifts[:, lanes_of(block)]
            for block in range(blocks)
        ]
        normed_ref[at, :] = jnp.concatenate(out, 1).astype(BF16)

    loop(source_ref.shape[1] // BAND, body, unroll=2)
    transpose_rows(normed_ref, turned_ref)


def transpose_rows(rows_ref, turned_ref):
    width = rows_ref.shape[1]

    def body(step):
        at = rows_at(step * TILE, TILE, TILE)
        turned_ref[0:width, at] = rows_ref[at, :].T

    loop(rows_ref.shape[0] // TILE, body)


def norm_backward(source_ref, grad_at, direct_at, table_ref, gain_row, emit, blocks, total):
    gains = table_ref[gain_row : gain_row + 1, :]

    def body(step, sums):
        at = rows_at(step * BAND, BAND, BAND)
        parts, inverse = norm_parts([source_ref[block, at, :] for block in range(blocks)])
        grads = [grad_at(block, at) for block in range(blocks)]
        scaled = [grads[block] * gains[:, lanes_of(block)] for block in range(blocks)]
        product = [grads[block] * parts[block] for block in range(blocks)]
        crossed = [scaled[block] * parts[block] for block in range(blocks)]
        mean, cross = row_means(scaled), row_means(crossed)
        out = [
            direct_at(block, at) + inverse * (scaled[block] - mean - parts[block] * cross)
            for block in range(blocks)
        ]
        emit(at, out)
        gain_sums = [sums[0][block] + fold_rows(product[block]) for block in range(blocks)]
        shift_sums = [sums[1][block] + fold_rows(grads[block]) for block in range(blocks)]
        return (gain_sums, shift_sums)

    zero = [jnp.zeros((8, LANES), F32) for _ in range(blocks)]
    return lax.fori_loop(0, total // BAND, body, (zero, zero), unroll=2)


def total_row(parts):
    return jnp.concatenate([jnp.sum(part, 0, keepdims=True) for part in parts], 1)


def head_mask():
    row = lax.broadcasted_iota(jnp.int32, (LANES, LANES), 0)
    col = lax.broadcasted_iota(jnp.int32, (LANES, LANES), 1)
    size = LANES // 2
    return jnp.where((row < size) == (col < size), size ** (-0.5), 0.0).astype(F32)


def front_kernel(
    side_ref, tokens_ref, cpe_ref, small_ref, middle_ref, large_ref, qkv_ref, proj_ref,
    cpe_bias_ref, gain_ref, shift_ref, query_bias_ref, value_bias_ref, crpe_bias_ref, proj_bias_ref,
    crpe_ref, input_out, position_out, query_out, weight_out, value_out, convolved_out, normed_t_out, context_out, attended_t_out, second_out,
    input_ref, position_ref, query_ref, weight_ref, value_ref, convolved_ref, normed_t_ref, context_ref, attended_t_ref, second_ref,
    mask_ref, work_ref, normed_ref, cpe_taps_ref, crpe_taps_ref, crpe_work_ref, table_ref, sems,
):
    fill_table(
        (cpe_bias_ref, gain_ref, shift_ref, query_bias_ref, value_bias_ref, crpe_bias_ref, proj_bias_ref), table_ref
    )
    out = Copies(sems)
    rows, channels = tokens_ref.shape
    blocks = channels // LANES
    images = rows // SLOT
    padded = normed_ref.shape[0]
    held = SLOT_PAD * images
    fill_mask(side_ref[0], mask_ref, images)
    assemble_taps((small_ref, middle_ref, large_ref), crpe_work_ref, crpe_ref)
    fill_taps(cpe_ref[...].astype(F32), cpe_taps_ref, 9, blocks)
    fill_taps(crpe_ref, crpe_taps_ref, 49, blocks)
    spread(tokens_ref, work_ref, blocks)

    def arrange(slot):
        at = rows_at(slot * images, images)
        mask = mask_ref[at, :]
        for block in range(blocks):
            values = work_ref[block, pl.ds(natural_slot(slot), images, stride=SLOT), :]
            input_ref[block, at, :] = values * mask

    loop(SLOT, arrange)
    for ref in (input_ref, position_ref, convolved_ref):
        ref[:, rows:padded, :] = jnp.zeros((blocks, padded - rows, LANES), F32)
    position_ref[:, CELLS * images : rows, :] = input_ref[:, CELLS * images : rows, :]
    convolved_ref[:, CELLS * images : rows, :] = jnp.zeros((blocks, images, LANES), F32)

    subs = images // 8

    def position(index):
        block, sub = index // subs, index % subs
        bias = table_row(table_ref, CPE_B, block)

        def emit(cell, total):
            at = rows_at(cell * images + sub * 8, 8)
            position_ref[block, at, :] = input_ref[block, at, :] + mask_ref[at, :] * (total + bias)

        correlate(input_ref, cpe_taps_ref, 3, 3, images, block, sub, emit)

    loop(blocks * subs, position)
    out.start(input_ref, input_out)
    out.start(position_ref, position_out)
    norm_forward(position_ref, table_ref, GAIN1, SHIFT1, normed_ref, normed_t_ref, blocks)
    normed_t_ref[channels:, :] = jnp.ones_like(normed_t_ref[channels:, :])
    out.start(normed_t_ref, normed_t_out)

    def project(step):
        at = rows_at(step * TILE, TILE, TILE)
        normed = normed_ref[at, :]
        mask = mask_ref[at, :]
        query = dot(normed, qkv_ref[:, :channels]) + table_ref[QUERY_B : QUERY_B + 1, :]
        for block in range(blocks):
            query_ref[block, at, :] = query[:, lanes_of(block)]
        key = dot(normed, qkv_ref[:, channels : 2 * channels])
        for block in range(blocks):
            weight_ref[block, at, :] = key[:, lanes_of(block)]
        value = dot(normed, qkv_ref[:, 2 * channels :]) + table_ref[VALUE_B : VALUE_B + 1, :]
        for block in range(blocks):
            value_ref[block, at, :] = value[:, lanes_of(block)] * mask

    loop(padded // TILE, project)
    for ref in (query_ref, value_ref):
        ref[:, padded:held, :] = jnp.zeros((blocks, held - padded, LANES), F32)
    weight_ref[:, rows:held, :] = jnp.zeros((blocks, held - rows, LANES), F32)
    out.start(query_ref, query_out)
    out.start(value_ref, value_out)

    def convolve(size, block, sub):
        bias = table_row(table_ref, CRPE_B, block)

        def emit(cell, total):
            convolved_ref[block, rows_at(cell * images + sub * 8, 8), :] = total + bias

        correlate(value_ref, crpe_taps_ref, size, 7, images, block, sub, emit)

    by_block(images, convolve)
    out.start(convolved_ref, convolved_out)

    def soften(index):
        block, sub = index // subs, index % subs
        top = None
        for slot in range(SLOT):
            at = rows_at(slot * images + sub * 8, 8)
            key = jnp.where(mask_ref[at, :] > 0, weight_ref[block, at, :], -1e30)
            top = key if top is None else jnp.maximum(top, key)
        total = None
        for slot in range(SLOT):
            at = rows_at(slot * images + sub * 8, 8)
            mask = mask_ref[at, :]
            key = jnp.where(mask > 0, weight_ref[block, at, :], -1e30)
            level = jnp.exp(key - top) * mask
            weight_ref[block, at, :] = level
            total = level if total is None else total + level
        inverse = 1.0 / total
        for slot in range(SLOT):
            at = rows_at(slot * images + sub * 8, 8)
            weight_ref[block, at, :] = weight_ref[block, at, :] * inverse

    loop(blocks * subs, soften)
    out.start(weight_ref, weight_out)
    heads = head_mask()

    def attend(image):
        at = pl.ds(image, SLOT_PAD, stride=images)
        for block in range(blocks):
            weight = weight_ref[block, at, :].astype(BF16)
            value = value_ref[block, at, :].astype(BF16)
            query = query_ref[block, at, :].astype(BF16)
            context = (dot_tn(weight, value) * heads).astype(BF16)
            context_ref[image, block] = context
            work_ref[block, at, :] = dot(query, context)

    loop(images, attend, unroll=4)
    out.start(context_ref, context_out)

    def finish(step):
        at = rows_at(step * TILE, TILE, TILE)
        attended = jnp.concatenate(
            [
                work_ref[block, at, :] + query_ref[block, at, :] * convolved_ref[block, at, :]
                for block in range(blocks)
            ],
            1,
        ).astype(BF16)
        attended_t_ref[:, at] = attended.T
        branch = dot(attended, proj_ref[...]) + table_ref[PROJ_B : PROJ_B + 1, :]
        for block in range(blocks):
            second_ref[block, at, :] = position_ref[block, at, :] + branch[:, lanes_of(block)]

    half = padded // TILE // 2
    loop(half, finish)
    part = slice(0, half * TILE)
    out.start(second_ref.at[:, part], second_out.at[:, part])
    loop(padded // TILE - half, lambda step: finish(step + half))
    part = slice(half * TILE, padded)
    out.start(second_ref.at[:, part], second_out.at[:, part])
    out.start(attended_t_ref, attended_t_out)
    out.finish()


def table_row(table_ref, row, block):
    return table_ref[row : row + 1, pl.ds(pl.multiple_of(block * LANES, LANES), LANES)]


def gelu_parts(value):
    size = 1.0 + (0.3275911 / math.sqrt(2.0)) * jnp.abs(value)
    part = pl.reciprocal(size, approx=True)
    part = part * (2.0 - size * part)
    level = jnp.exp2(value * value * (-0.5 / math.log(2.0)))
    poly = 0.5 * 1.061405429
    for term in (-1.453152027, 1.421413741, -0.284496736, 0.254829592):
        poly = poly * part + 0.5 * term
    tail = poly * part * level
    return jnp.where(value >= 0, 1.0 - tail, tail), level * (1.0 / math.sqrt(2.0 * math.pi))


def mlp_kernel(
    side_ref, cot_ref, second_in, fc_in, gain_ref, shift_ref, fc2_bias_ref, own_ref, second_bias_ref,
    third_bias_ref, fourth_bias_ref,
    out_ref, grad_out, grad_fc_keep, grad_fc_send, small_ref,
    second_ref, fc_ref, grad_ref, grad_fc_ref,
    mask_ref, work_ref, cot_rows_ref, cot_t_ref, normed_ref, normed_t_ref, hidden_ref, pre_ref, hidden_two_ref, pre_two_ref, mlp_ref, back_ref,
    table_ref, bias_ref, sems,
):
    fill_table((gain_ref, shift_ref, fc2_bias_ref), table_ref)
    fill_table((own_ref, second_bias_ref, third_bias_ref, fourth_bias_ref), bias_ref)
    copies = Copies(sems)
    got_second = copies.start(second_in, second_ref)
    got_fc = copies.start(fc_in, fc_ref)
    rows, channels = cot_ref.shape
    blocks = channels // LANES
    images = rows // SLOT
    padded = normed_ref.shape[0]
    owners, _, units = fc_ref.shape
    fill_mask(side_ref[0], mask_ref, images)
    mine, half_x, half_z = side_ref[1], side_ref[2] & 1, (side_ref[2] >> 1) & 1
    spread(cot_ref, work_ref, blocks)
    cot_rows_ref[rows:padded, :] = jnp.zeros((padded - rows, channels), BF16)

    def arrange(step, sums):
        at = rows_at(step * (2 * images), 2 * images, 16)
        mask = mask_ref[at, :]
        parts = []
        for block in range(blocks):
            pair = [
                work_ref[block, pl.ds(natural_slot(2 * step + one), images, stride=SLOT), :]
                for one in range(2)
            ]
            parts.append(jnp.concatenate(pair, 0) * mask)
        cot_rows_ref[at, :] = jnp.concatenate(parts, 1).astype(BF16)
        return [sums[block] + fold_rows(parts[block]) for block in range(blocks)]

    zero = [jnp.zeros((8, LANES), F32) for _ in range(blocks)]
    bias_sums = lax.fori_loop(0, SLOT // 2, arrange, zero)
    transpose_rows(cot_rows_ref, cot_t_ref)
    got_second.wait()
    norm_forward(second_ref, table_ref, GAIN2, SHIFT2, normed_ref, normed_t_ref, blocks)
    normed_t_ref[channels:, :] = jnp.ones_like(normed_t_ref[channels:, :])
    half = units // 2
    got_fc.wait()

    full = padded // MLP_TILE
    wide = units // full
    ends = 1
    rows_half = MLP_TILE // ends

    def weights(slot, held, step):
        cols = pl.ds(pl.multiple_of(step * wide, wide), wide)
        hidden_ref, pre_ref = held
        for which, (left_ref, right_ref) in enumerate(((normed_t_ref, pre_ref), (cot_t_ref, hidden_ref))):
            for end in range(2):
                last = left_ref.shape[0] if end else PIECE
                grad = dot(left_ref[end * PIECE : last, :], right_ref[:, cols]).astype(BF16)
                place = ((half_x ^ which) << 1) | (half_z ^ end)
                grad_fc_ref[slot, place, 0:PIECE, cols] = grad[0:PIECE]
                if last > channels:
                    first = (half_x << 1) | half_z
                    grad_fc_ref[slot, first, PIECE:, cols] = grad[PIECE:]
                yield

    def part(slot, held, before):
        owner = mine ^ ((slot >> 1) | ((slot & 1) << 1))
        hidden_ref, pre_ref = held

        def tile(step):
            beside = iter(()) if before is None else weights(slot - 1, before, step)
            for end in range(ends):
                at = rows_at(step * MLP_TILE + end * rows_half, rows_half, rows_half)
                normed = normed_ref[at, :]
                cot = cot_rows_ref[at, :]
                mlp, back = None, None
                for piece in range(2):
                    cols = slice(piece * half, (piece + 1) * half)
                    first = fc_ref[owner, 0:channels, cols]
                    second = fc_ref[owner, channels + piece * half : channels + (piece + 1) * half, :]
                    value = dot(normed, first) + bias_ref[slot : slot + 1, cols]
                    grad = dot_nt(cot, second)
                    next(beside, None)
                    next(beside, None)
                    level, density = gelu_parts(value)
                    hidden = (value * level).astype(BF16)
                    pre = (grad * (level + value * density)).astype(BF16)
                    hidden_ref[at, cols] = hidden
                    pre_ref[at, cols] = pre
                    more_mlp, more_back = dot(hidden, second), dot_nt(pre, first)
                    mlp = more_mlp if mlp is None else mlp + more_mlp
                    back = more_back if back is None else back + more_back
                if slot == 0:
                    mlp_ref[at, :] = mlp
                    back_ref[at, :] = back
                else:
                    mlp_ref[at, :] += mlp
                    back_ref[at, :] += back

        loop(full, tile)

    def last_weights(step):
        for _ in weights(owners - 1, held[(owners - 1) % 2], step):
            pass

    held = (hidden_ref, pre_ref), (hidden_two_ref, pre_two_ref)
    targets = [(grad_fc_keep if slot < owners // 2 else grad_fc_send).at[slot % (owners // 2)] for slot in range(owners)]
    for slot in range(owners + 1):
        if slot < owners:
            part(slot, held[slot % 2], held[(slot - 1) % 2] if slot else None)
        else:
            loop(full, last_weights)
        if slot:
            copies.start(grad_fc_ref.at[slot - 1], targets[slot - 1])

    def grad_at(block, at):
        return back_ref[at, lanes_of(block)]

    def direct_at(block, at):
        return cot_rows_ref[at, lanes_of(block)].astype(F32)

    def emit(at, out):
        for block in range(blocks):
            grad_ref[block, at, :] = out[block]

    gain_sums, shift_sums = norm_backward(
        second_ref, grad_at, direct_at, table_ref, GAIN2, emit, blocks, padded
    )
    copies.start(grad_ref, grad_out)
    fc2_bias = table_ref[FC2_B : FC2_B + 1, :]

    def result(slot):
        at = rows_at(slot * images, images)
        mask = mask_ref[at, :]
        for block in range(blocks):
            total = second_ref[block, at, :] + mlp_ref[at, lanes_of(block)] + fc2_bias[:, lanes_of(block)]
            work_ref[block, pl.ds(natural_slot(slot), images, stride=SLOT), :] = total * mask

    loop(SLOT, result)
    unspread(work_ref, out_ref, blocks)

    small_ref[...] = jnp.zeros_like(small_ref)
    small_ref[0:1, :] = total_row(gain_sums)
    small_ref[1:2, :] = total_row(shift_sums)
    small_ref[2:3, :] = total_row(bias_sums)
    for copy in copies.open[2:]:
        copy.wait()


def branch_kernel(
    proj_ref, grad_in, attended_t_in,
    back_out, grad_proj_ref, small_ref,
    grad_ref, attended_t_ref, back_ref, branch_ref, sems,
):
    copies = Copies(sems)
    padded, channels = branch_ref.shape
    blocks = channels // LANES
    held = back_ref.shape[1]
    half = padded // 2
    halves = slice(0, half), slice(half, padded)
    got = [copies.start(grad_in.at[:, part], grad_ref.at[:, part]) for part in halves]
    got_attended = copies.start(attended_t_in, attended_t_ref)
    back_ref[:, padded:held, :] = jnp.zeros((blocks, held - padded, LANES), F32)
    sent = [copies.start(back_ref.at[:, padded:held], back_out.at[:, padded:held])]

    def branch(step, total):
        at = rows_at(step * TILE, TILE, TILE)
        parts = [grad_ref[block, at, :] for block in range(blocks)]
        low = jnp.concatenate(parts, 1).astype(BF16)
        branch_ref[at, :] = low
        back = dot_nt(low, proj_ref[...])
        for block in range(blocks):
            back_ref[block, at, :] = back[:, lanes_of(block)]
        return total + fold_rows(low.astype(F32))

    total = jnp.zeros((8, channels), F32)
    for end, part in enumerate(halves):
        got[end].wait()
        total = lax.fori_loop(end * half // TILE, (end + 1) * half // TILE, branch, total)
        sent.append(copies.start(back_ref.at[:, part], back_out.at[:, part]))
    got_attended.wait()
    grad_proj_ref[...] = dot(attended_t_ref[...], branch_ref[...]).astype(BF16)
    small_ref[...] = total
    for copy in sent:
        copy.wait()


def mix_kernel(
    side_ref, small_mlp_ref, small_branch_ref, crpe_ref, grad_proj_ref,
    back_in, query_in, weight_in, value_in, convolved_in, normed_t_in, context_in,
    keep_ref, send_ref, projected_out,
    total_ref, back_ref, query_ref, weight_ref, value_ref, convolved_ref, normed_t_ref, context_ref, projected_ref,
    mask_ref, small_ref, edge_ref, turned_ref, crpe_taps_ref, level_ref, sems,
):
    copies = Copies(sems)
    pairs = (back_in, back_ref), (query_in, query_ref), (convolved_in, convolved_ref)
    first = [
        [copies.start(source.at[block], target.at[block]) for source, target in pairs] for block in range(back_ref.shape[0])
    ]
    pairs = (weight_in, weight_ref), (value_in, value_ref), (context_in, context_ref), (normed_t_in, normed_t_ref)
    then = [copies.start(*pair) for pair in pairs]
    blocks, padded, _ = edge_ref.shape
    channels = blocks * LANES
    held = query_ref.shape[1]
    images = held // SLOT_PAD
    rows = images * SLOT
    subs = images // 8
    fill_mask(side_ref[0], mask_ref, images)
    fill_taps(crpe_ref, crpe_taps_ref, 49, blocks)
    turned_ref[:, CELLS * images :, :] = jnp.zeros((blocks, padded - CELLS * images, LANES), F32)
    bias_sums = []

    def arrived(block):
        for copy in first[block]:
            copy.wait()

        def edges(step, total):
            at = rows_at(step * (9 * images), 9 * images)
            back = back_ref[block, at, :]
            edge = back * query_ref[block, at, :]
            edge_ref[block, at, :] = edge
            convolved_ref[block, at, :] = back * convolved_ref[block, at, :]
            return total + fold_rows(edge)

        bias_sums.append(lax.fori_loop(0, CELLS // 9, edges, jnp.zeros((8, LANES), F32)))

    def convolve(size, block, sub):
        def emit(cell, total):
            turned_ref[block, rows_at(cell * images + sub * 8, 8), :] = total

        correlate(edge_ref, crpe_taps_ref, size, 7, images, block, sub, emit, turned=True)

    by_block(images, convolve, arrived)
    for copy in then:
        copy.wait()
    heads = head_mask()

    def attend(image):
        at = pl.ds(image, SLOT_PAD, stride=images)
        for block in range(blocks):
            weight = weight_ref[block, at, :].astype(BF16)
            value = value_ref[block, at, :].astype(BF16)
            query = query_ref[block, at, :].astype(BF16)
            back = back_ref[block, at, :].astype(BF16)
            context = context_ref[image, block]
            grad = (dot_tn(query, back) * heads).astype(BF16)
            query_ref[block, at, :] = dot_nt(back, context)
            back_ref[block, at, :] = dot_nt(value, grad)
            value_ref[block, at, :] = dot(weight, grad)

    loop(images, attend, unroll=4)

    def levels(index):
        block, sub = index // subs, index % subs
        total = None
        for slot in range(SLOT):
            at = rows_at(slot * images + sub * 8, 8)
            term = weight_ref[block, at, :] * back_ref[block, at, :]
            total = term if total is None else total + term
        level_ref[block, rows_at(sub * 8, 8), :] = total

    loop(blocks * subs, levels)
    projected_ref[rows:padded, :] = jnp.zeros((padded - rows, 3 * channels), BF16)

    def gather(step):
        at = rows_at(step * (2 * images), 2 * images, 16)
        mask = mask_ref[at, :]
        parts = [[], [], []]
        for block in range(blocks):
            level = level_ref[block]
            level = jnp.concatenate([level, level], 0)
            parts[0].append(query_ref[block, at, :] + convolved_ref[block, at, :])
            parts[1].append(weight_ref[block, at, :] * (back_ref[block, at, :] - level))
            parts[2].append((value_ref[block, at, :] + turned_ref[block, at, :]) * mask)
        for which in range(3):
            cols = slice(which * channels, (which + 1) * channels)
            projected_ref[at, cols] = jnp.concatenate(parts[which], 1).astype(BF16)

    loop(SLOT // 2, gather)
    sent = copies.start(projected_ref, projected_out)
    small_ref[...] = jnp.zeros_like(small_ref)
    index = ((side_ref[1] & 1) << 2) | ((side_ref[2] & 1) << 1) | (side_ref[1] >> 1)

    def place(matrix, grad):
        for end in range(channels // PIECE):
            piece = matrix * (channels // PIECE) + end
            total_ref[piece ^ index, 0:PIECE, :] = grad[end * PIECE : (end + 1) * PIECE]

    for which in range(3):
        cols = slice(which * channels, (which + 1) * channels)
        grad = dot(normed_t_ref[...], projected_ref[:, cols])
        place(which, grad[0:channels].astype(BF16))
        small_ref[56 + which : 57 + which, :] = grad[channels : channels + 1]
    place(3, grad_proj_ref[...])
    small_ref[49:50, :] = total_row(bias_sums)
    small_ref[50:51, :] = jnp.sum(small_branch_ref[...], 0, keepdims=True)
    small_ref[64:72, :] = small_mlp_ref[...]
    for piece in range(total_ref.shape[0]):
        total_ref[piece ^ index, PIECE:, :] = small_ref[piece * 16 : (piece + 1) * 16, :].astype(BF16)
    out = [copies.start(total_ref.at[4:8], send_ref), copies.start(total_ref.at[0:4], keep_ref)]
    for copy in [sent] + out:
        copy.wait()


def taps_kernel(
    back_in, query_in, value_in,
    small_ref,
    back_ref, query_ref, value_ref, sums_ref, sems,
):
    copies = Copies(sems)
    blocks, cells, _ = back_ref.shape
    images = cells // CELLS
    part = slice(0, cells)
    pairs = (back_in, back_ref), (query_in, query_ref), (value_in, value_ref)
    got = [
        [copies.start(source.at[block, part], target.at[block]) for source, target in pairs] for block in range(blocks)
    ]
    sums_ref[...] = jnp.zeros_like(sums_ref)

    def arrived(block):
        for copy in got[block]:
            copy.wait()

        def edges(step):
            at = rows_at(step * (9 * images), 9 * images)
            back_ref[block, at, :] = back_ref[block, at, :] * query_ref[block, at, :]

        loop(CELLS // 9, edges)

    def taps(size, block, sub):
        tap_sums(back_ref, value_ref, sums_ref, size, 7, images, block, sub)

    by_block(images, taps, arrived)
    small_ref[...] = jnp.zeros_like(small_ref)
    for block in range(blocks):
        small_ref[0:49, lanes_of(block)] = jnp.sum(sums_ref[block], 1)


def norm_half(copies, first, base, operands, grad_out, projected_ref, position_ref, grad_ref, normed_ref, table_ref):
    qkv_ref, gain_ref, projected_in, position_in, grad_in = operands
    fill_table((gain_ref,), table_ref)
    padded, channels = normed_ref.shape
    blocks = channels // LANES
    half = padded // 2
    got_halves = [
        copies.start(projected_in.at[pl.ds(first + end * half, half)], projected_ref.at[pl.ds(end * half, half)])
        for end in range(2)
    ]
    source, target = pl.ds(first, padded), pl.ds(base, padded)
    got = [
        copies.start(position_in.at[:, source], position_ref),
        copies.start(grad_in.at[:, source], grad_ref.at[:, target]),
    ]

    def project(step):
        at = rows_at(step * TILE, TILE, TILE)
        normed_ref[at, :] = dot_nt(projected_ref[at, :], qkv_ref[...])

    got_halves[0].wait()
    loop(half // TILE, project)
    got_halves[1].wait()
    loop(half // TILE, lambda step: project(step + half // TILE))
    for copy in got:
        copy.wait()

    def grad_at(block, at):
        return normed_ref[at, lanes_of(block)]

    def moved(at):
        return rows_at(base + at.start, at.size, BAND)

    def direct_at(block, at):
        return grad_ref[block, moved(at), :]

    def emit_norm(at, out):
        for block in range(blocks):
            grad_ref[block, moved(at), :] = out[block]

    sums = norm_backward(position_ref, grad_at, direct_at, table_ref, 0, emit_norm, blocks, padded)
    return copies.start(grad_ref.at[:, target], grad_out), sums


def norm_first_kernel(
    qkv_ref, gain_ref, projected_in, position_in, grad_in,
    grad_out, small_ref,
    projected_ref, position_ref, grad_ref, normed_ref, table_ref, sems,
):
    operands = qkv_ref, gain_ref, projected_in, position_in, grad_in
    sent, (gain_sums, shift_sums) = norm_half(
        Copies(sems), 0, 0, operands, grad_out, projected_ref, position_ref, grad_ref, normed_ref, table_ref
    )
    small_ref[...] = jnp.zeros_like(small_ref)
    small_ref[0:1, :] = total_row(gain_sums)
    small_ref[1:2, :] = total_row(shift_sums)
    sent.wait()


def norm_last_kernel(
    first, qkv_ref, gain_ref, projected_in, position_in, grad_in, grad_first_in, input_in, small_first_ref, small_taps_ref,
    grad_out, small_ref,
    projected_ref, position_ref, grad_ref, normed_ref, table_ref, input_ref, sums_ref, work_ref, sems,
):
    copies = Copies(sems)
    blocks, cells, _ = input_ref.shape
    images = cells // CELLS
    subs = images // 8
    got = copies.start(grad_first_in, grad_ref.at[:, 0:first]), copies.start(input_in.at[:, 0:cells], input_ref)
    operands = qkv_ref, gain_ref, projected_in, position_in, grad_in
    sent, (gain_sums, shift_sums) = norm_half(
        copies, first, first, operands, grad_out, projected_ref, position_ref, grad_ref, normed_ref, table_ref
    )
    sums_ref[...] = jnp.zeros_like(sums_ref)
    work_ref[...] = jnp.zeros_like(work_ref)
    work_ref[0:56, :] = small_taps_ref[...]
    work_ref[57:58, :] = total_row(gain_sums) + small_first_ref[0:1, :]
    work_ref[58:59, :] = total_row(shift_sums) + small_first_ref[1:2, :]
    for copy in got:
        copy.wait()

    def colsum(step, sums):
        at = rows_at(step * (9 * images), 9 * images)
        return [sums[block] + fold_rows(grad_ref[block, at, :]) for block in range(blocks)]

    zero = [jnp.zeros((8, LANES), F32) for _ in range(blocks)]
    work_ref[56:57, :] = total_row(lax.fori_loop(0, GRID, colsum, zero))

    def taps(index):
        tap_sums(grad_ref, input_ref, sums_ref, 3, 3, images, index // subs, index % subs)

    loop(blocks * subs, taps)
    for block in range(blocks):
        work_ref[64:73, lanes_of(block)] = jnp.sum(sums_ref[block], 1)
    small_ref[...] = work_ref[...].astype(BF16)
    sent.wait()


def back_kernel(
    side_ref, cpe_ref, first_in, second_in,
    tokens_ref,
    grad_ref, mask_ref, work_ref, result_ref, taps_ref, sems,
):
    copies = Copies(sems)
    half = first_in.shape[1]
    got = copies.start(first_in, grad_ref.at[:, 0:half]), copies.start(second_in, grad_ref.at[:, half : 2 * half])
    rows, channels = tokens_ref.shape
    blocks = channels // LANES
    images = rows // SLOT
    subs = images // 8
    fill_mask(side_ref[0], mask_ref, images)
    fill_taps(cpe_ref[...].astype(F32), taps_ref, 9, blocks)
    for copy in got:
        copy.wait()

    def convolve(index):
        block, sub = index // subs, index % subs

        def emit(cell, total):
            at = rows_at(cell * images + sub * 8, 8)
            result_ref[block, at, :] = (grad_ref[block, at, :] + total) * mask_ref[at, :]

        correlate(grad_ref, taps_ref, 3, 3, images, block, sub, emit, turned=True)

    loop(blocks * subs, convolve)
    result_ref[:, CELLS * images : rows, :] = grad_ref[:, CELLS * images : rows, :]

    def arrange(slot):
        at = rows_at(slot * images, images)
        for block in range(blocks):
            work_ref[block, pl.ds(natural_slot(slot), images, stride=SLOT), :] = result_ref[block, at, :]

    loop(SLOT, arrange, unroll=2)
    unspread(work_ref, tokens_ref, blocks)


def finish_fc_kernel(
    side_ref, first_ref, second_ref, third_ref, fourth_ref,
    fc1_ref, fc2_ref, bias_ref,
    held_ref,
):
    index = ((side_ref[2] & 1) << 1) | ((side_ref[2] >> 1) & 1)
    for place, piece in enumerate((first_ref, second_ref, third_ref, fourth_ref)):
        held_ref[place ^ index] = piece[...]
    for end in range(2):
        fc1_ref[end * PIECE : (end + 1) * PIECE, :] = held_ref[end, 0:PIECE, :].astype(F32)
        fc2_ref[:, end * PIECE : (end + 1) * PIECE] = held_ref[2 + end, 0:PIECE, :].astype(F32).T
    bias_ref[...] = held_ref[0, PIECE:, :].astype(F32)[0:1].reshape(bias_ref.shape)


def finish_small_kernel(
    small_ref,
    cpe_ref, cpe_bias_ref, gain_ref, shift_ref, crpe_small_ref, crpe_middle_ref, crpe_large_ref,
    work_ref,
):
    small = small_ref[...]
    work_ref[...] = small.astype(F32)
    cpe_ref[...] = work_ref[64:73, :]
    for row, ref in enumerate((cpe_bias_ref, gain_ref, shift_ref)):
        ref[...] = work_ref[56 + row : 57 + row, :].reshape(ref.shape)
    channels = small.shape[1]
    offset = 0
    for size, ref in zip((3, 5, 7), (crpe_small_ref, crpe_middle_ref, crpe_large_ref)):
        width = ref.shape[1]
        taps = dot_nt(small, lane_picker(width, offset, channels))
        for tap, place in enumerate(centred(size)):
            ref[tap : tap + 1, :] = taps[place : place + 1, :]
        offset += width


def finish_kernel(side_ref, *refs):
    pieces, (qkv_ref, proj_ref), rows, (held_ref, small_ref) = refs[:8], refs[8:10], refs[10:-2], refs[-2:]
    index = ((side_ref[1] & 1) << 2) | ((side_ref[2] & 1) << 1) | (side_ref[1] >> 1)
    for place, piece in enumerate(pieces):
        held_ref[place ^ index] = piece[...]
    channels = proj_ref.shape[1]
    for piece in range(8):
        matrix, end = piece // 2, piece % 2
        at = slice(end * PIECE, (end + 1) * PIECE)
        values = held_ref[piece, 0:PIECE, :].astype(F32)
        if matrix < 3:
            qkv_ref[at, matrix * channels : (matrix + 1) * channels] = values
        else:
            proj_ref[at, :] = values
        small_ref[piece * 16 : (piece + 1) * 16, :] = held_ref[piece, PIECE:, :].astype(F32)
    for row, ref in zip(SMALL_ROWS, rows):
        ref[...] = small_ref[row : row + 1, :].reshape(ref.shape)


def add(*terms):
    return sum(term.astype(F32) for term in terms).astype(BF16)


def exchange(values, across_dp, across_blk):
    owners, parts = lax.axis_size("blk"), lax.axis_size("dp")
    flip = across_dp * owners + across_blk
    return lax.ppermute(values, ("dp", "blk"), [(at, at ^ flip) for at in range(parts * owners)])


def together(*values):
    return lax.optimization_barrier(values)


def shape(dims, dtype):
    return jax.ShapeDtypeStruct(dims, dtype)


def call(body, outs, scratch, cost, *operands):
    vmem, smem, hbm = (pl.BlockSpec(memory_space=space) for space in (pltpu.VMEM, pltpu.SMEM, pl.ANY))

    def place(value):
        return hbm if isinstance(value, Held) else smem if value.dtype == jnp.int32 else vmem

    def plain(values):
        return [value.array if isinstance(value, Held) else value for value in values]

    return pl.pallas_call(
        body,
        out_shape=plain(outs),
        in_specs=[place(value) for value in operands],
        out_specs=[place(value) for value in outs],
        scratch_shapes=[
            pltpu.SemaphoreType.DMA((item,)) if isinstance(item, int) else pltpu.VMEM(*item) for item in scratch
        ],
        compiler_params=pltpu.CompilerParams(vmem_limit_bytes=VMEM_BYTES),
        cost_estimate=pl.CostEstimate(flops=cost, bytes_accessed=30_000_000, transcendentals=0),
    )(*plain(operands))


class Held:
    def __init__(self, array):
        self.array = array


def shards(
    tokens, sides, cpe_weight, cpe_bias, norm1_gain, norm1_shift, w_qkv, query_bias, value_bias,
    crpe_small, crpe_middle, crpe_large, crpe_bias, w_proj, proj_bias, norm2_gain, norm2_shift,
    w_fc1, fc1_bias, w_fc2, fc2_bias, cotangent,
):
    rows, channels = tokens.shape
    blocks = channels // LANES
    images = rows // SLOT
    padded = -(-rows // TILE) * TILE
    held = SLOT_PAD * images
    units = w_fc1.shape[1]
    owners = lax.axis_size("blk")

    fc_all = lax.all_gather(jnp.concatenate([w_fc1, w_fc2], 0), "blk", axis=0, tiled=False)
    biases = [fc1_bias] + [exchange(fc1_bias, 0, flip) for flip in (2, 1, 3)]
    scalars = jnp.stack([sides[0], lax.axis_index("blk"), lax.axis_index("dp")]).astype(jnp.int32)
    block_rows = (blocks, padded, LANES)
    block_held = (blocks, held, LANES)
    block_cells = (blocks, CELLS * images, LANES)
    contexts = (images, blocks, LANES, LANES), BF16
    front = [
        (block_rows, F32), (block_rows, F32), (block_held, F32), (block_held, F32), (block_held, F32),
        (block_rows, F32), ((channels + 16, padded), BF16), contexts, ((channels, padded), BF16), (block_rows, F32),
    ]
    crpe, inputs, position, query, weight, value, convolved, normed_t, context, attended_t, second = call(
        front_kernel,
        [shape((56, channels), F32)] + [Held(shape(*item)) for item in front],
        front + [
            ((padded, LANES), F32), (block_held, F32), ((padded, channels), BF16),
            ((blocks, 9, 8, LANES), F32), ((blocks, 49, 8, LANES), F32), ((56, channels), F32), ((8, channels), F32), 11,
        ],
        40_000_000_000,
        scalars, tokens, cpe_weight, crpe_small, crpe_middle, crpe_large, w_qkv, w_proj,
        cpe_bias, norm1_gain, norm1_shift, query_bias, value_bias, crpe_bias, proj_bias,
    )
    pieces = (owners // 2, 4, PIECE + 16, units)
    output, grad_second, fc_keep, fc_send, small_mlp = call(
        mlp_kernel,
        [
            shape((rows, channels), BF16), Held(shape(block_rows, F32)), Held(shape(pieces, BF16)), Held(shape(pieces, BF16)),
            shape((8, channels), F32),
        ],
        [
            (block_rows, F32), (fc_all.shape, BF16), (block_rows, F32),
            ((owners, 4, PIECE + 16, units), BF16),
            ((padded, LANES), F32), ((blocks, rows, LANES), F32),
            ((padded, channels), BF16), ((channels, padded), BF16),
            ((padded, channels), BF16), ((channels + 16, padded), BF16),
            ((padded, units), BF16), ((padded, units), BF16), ((padded, units), BF16), ((padded, units), BF16),
            ((padded, channels), F32), ((padded, channels), F32), ((8, channels), F32), ((8, units), F32), 4 + owners,
        ],
        60_000_000_000,
        scalars, cotangent, Held(second), Held(fc_all), norm2_gain, norm2_shift, fc2_bias, *biases,
    )
    fc_far = exchange(fc_send, 0, 1)
    back, grad_proj, small_branch = call(
        branch_kernel,
        [Held(shape(block_held, F32)), shape((channels, channels), BF16), shape((8, channels), F32)],
        [(block_rows, F32), ((channels, padded), BF16), (block_held, F32), ((padded, channels), BF16), 6],
        10_000_000_000,
        w_proj, Held(grad_second), Held(attended_t),
    )

    def half_of(side, end):
        part = slice(2 * end, 2 * end + 2)
        return add(fc_keep[side, part], fc_far[side, part])

    back, fc_y, fc_x, fc_yx, fc_own = together(back, half_of(1, 0), half_of(0, 1), half_of(1, 1), half_of(0, 0))
    fc_far = exchange(fc_y, 0, 2), exchange(fc_x, 1, 0), exchange(fc_yx, 1, 2)
    total_keep, total_send, projected = call(
        mix_kernel,
        [Held(shape((4, PIECE + 16, channels), BF16))] * 2 + [Held(shape((padded, 3 * channels), BF16))],
        [
            ((8, PIECE + 16, channels), BF16),
            (block_held, F32), (block_held, F32), (block_held, F32), (block_held, F32), (block_rows, F32),
            ((channels + 16, padded), BF16), contexts, ((padded, 3 * channels), BF16),
            ((padded, LANES), F32), ((128, channels), F32), (block_rows, F32), (block_rows, F32),
            ((blocks, 49, 8, LANES), F32), ((blocks, images, LANES), F32), 7 + 3 * blocks,
        ],
        50_000_000_000,
        scalars, small_mlp, small_branch, crpe, grad_proj,
        Held(back), Held(query), Held(weight), Held(value), Held(convolved), Held(normed_t), Held(context),
    )
    total_far = exchange(total_send, 0, 1)

    def end_of(end):
        return add(fc_own[end], *(far[end] for far in fc_far))

    projected, fc_other, fc_own = together(projected, end_of(1), end_of(0))
    fc_far = exchange(fc_other, 2, 0)

    block_half = (blocks, padded // 2, LANES)
    norm_outs = [Held(shape(block_half, F32)), shape((8, channels), F32)]
    norm_scratch = [((padded // 2, 3 * channels), BF16), (block_half, F32)]
    norm_more = [((padded // 2, channels), F32), ((8, channels), F32)]
    grad_first, small_first = call(
        norm_first_kernel, norm_outs, norm_scratch + [(block_half, F32)] + norm_more + [5], 8_000_000_000,
        w_qkv, norm1_gain, Held(projected), Held(position), Held(grad_second),
    )
    sums = [add(total_keep[piece], total_far[piece]) for piece in range(4)]
    back, grad_first, fc_own, *sums = together(back, grad_first, add(fc_own, fc_far), *sums)
    own = sums[0]
    total_far = exchange(sums[1], 0, 2), exchange(sums[2], 1, 0), exchange(sums[3], 1, 2)
    bits = [1 << bit for bit in range(1, lax.axis_size("dp").bit_length() - 1)]
    fc_bits = [bit for bit in bits if bit > 2]
    fc_far = exchange(fc_own, fc_bits[0], 0)
    (small_taps,) = call(
        taps_kernel,
        [shape((56, channels), F32)],
        [(block_cells, F32), (block_cells, F32), (block_cells, F32), ((blocks, 49, 8, LANES), F32), 3 * blocks],
        15_000_000_000,
        Held(back), Held(query), Held(value),
    )
    fc_own = add(fc_own, fc_far)
    for bit in fc_bits[1:]:
        fc_own = add(fc_own, exchange(fc_own, bit, 0))
    projected, small_taps, fc_own, own = together(projected, small_taps, fc_own, add(own, *total_far))
    total_far = exchange(own, bits[0], 0)
    fc_other, fc_third = exchange(fc_own, 2, 0), exchange(fc_own, 1, 0)
    grad_last, small_back = call(
        functools.partial(norm_last_kernel, padded // 2),
        [norm_outs[0], shape((80, channels), BF16)],
        norm_scratch + [(block_rows, F32)] + norm_more
        + [(block_cells, F32), ((blocks, 9, 8, LANES), F32), ((80, channels), F32), 7],
        12_000_000_000,
        w_qkv, norm1_gain, Held(projected), Held(position), Held(grad_second), Held(grad_first), Held(inputs),
        small_first, small_taps,
    )
    grad_last, fc_other, own = together(grad_last, fc_other, add(own, total_far))
    total_far = exchange(own, bits[1], 0)
    fc_fourth = exchange(fc_other, 1, 0)
    small_far = exchange(small_back, 0, 1)
    (grad_tokens,) = call(
        back_kernel,
        [shape((rows, channels), BF16)],
        [
            (block_rows, F32), ((padded, LANES), F32), ((blocks, rows, LANES), F32),
            (block_rows, F32), ((blocks, 9, 8, LANES), F32), 2,
        ],
        12_000_000_000,
        scalars, cpe_weight, Held(grad_first), Held(grad_last),
    )
    grad_tokens, small_back, small_far, fc_third, fc_fourth, own, total_far = together(
        grad_tokens, small_back, small_far, fc_third, fc_fourth, own, total_far
    )
    small = add(small_back, small_far)
    own = add(own, total_far)
    for bit in bits[2:]:
        own = add(own, exchange(own, bit, 0))
    near = [own, exchange(own, 0, 2), exchange(own, 1, 0)]
    near.append(exchange(near[1], 1, 0))
    fc1, fc2, fc1_sums = call(
        finish_fc_kernel,
        [shape((channels, units), F32), shape((units, channels), F32), shape((units,), F32)],
        [((4, PIECE + 16, units), BF16)],
        3_000_000_000,
        scalars, fc_own, fc_other, fc_third, fc_fourth,
    )
    total_pieces = near + [exchange(piece, 0, 1) for piece in near]
    flips = (0, 2), (1, 0), (1, 2)
    small_y, small_x, small_yx = (exchange(small, *flip) for flip in flips)
    small = ((small.astype(F32) + small_y.astype(F32)) + (small_x.astype(F32) + small_yx.astype(F32))).astype(BF16)
    for bit in bits:
        small = add(small, exchange(small, bit, 0))
    row = shape((channels,), F32)
    cpe, cpe_sums, gain_one, shift_one, taps_small, taps_middle, taps_large = call(
        finish_small_kernel,
        [
            shape(cpe_weight.shape, F32), row, row, row,
            shape(crpe_small.shape, F32), shape(crpe_middle.shape, F32), shape(crpe_large.shape, F32),
        ],
        [((80, channels), F32)],
        1_000_000,
        small,
    )
    grad_qkv, grad_proj, query_sums, value_sums, crpe_sums, proj_sums, gain_two, shift_two, fc2_sums = call(
        finish_kernel,
        [shape((channels, 3 * channels), F32), shape((channels, channels), F32)] + [row] * len(SMALL_ROWS),
        [((8, PIECE + 16, channels), BF16), ((128, channels), F32)],
        1_000_000,
        scalars, *total_pieces,
    )
    return (
        output, grad_tokens, cpe, cpe_sums, gain_one, shift_one, grad_qkv, query_sums, value_sums,
        taps_small, taps_middle, taps_large, crpe_sums, grad_proj, proj_sums, gain_two, shift_two,
        fc1, fc1_sums, fc2, fc2_sums,
    )


def solution(mesh):
    split, whole = P(("dp", "blk"), None), P()
    fc1, fc1_bias, fc2 = P(None, "blk"), P("blk"), P("blk", None)
    return jax.shard_map(
        shards,
        mesh=mesh,
        in_specs=(split, P(("dp", "blk"))) + (whole,) * 15 + (fc1, fc1_bias, fc2, whole, split),
        out_specs=(split, split) + (whole,) * 15 + (fc1, fc1_bias, fc2, whole),
        check_vma=False,
    )
```

```python
import functools
import math

import jax
import jax.numpy as jnp
from jax import lax
from jax.experimental import pallas as pl
from jax.experimental.pallas import tpu as pltpu
from jax.sharding import PartitionSpec as P

HEADS = 8
GRID = 9
CELLS = GRID * GRID
SLOT = CELLS + 1
LANES = 128
EPSILON = 1e-6
SLOT_PAD = 96
TILE = 256
BAND = 128
MLP_TILE = 1024
KERNEL_SIZES = (3, 5, 7, 7)
PIECE = 256
VMEM_BYTES = 62 * 1024 * 1024

F32 = jnp.float32
BF16 = jnp.bfloat16

SMALL_ROWS = (56, 58, 49, 50, 64, 65, 66)
CPE_B, GAIN1, SHIFT1, QUERY_B, VALUE_B, CRPE_B, PROJ_B = range(7)
GAIN2, SHIFT2, FC2_B = range(3)


def dot(left, right):
    return lax.dot_general(left, right, (((1,), (0,)), ((), ())), preferred_element_type=F32)


def dot_nt(left, right):
    return lax.dot_general(left, right, (((1,), (1,)), ((), ())), preferred_element_type=F32)


def dot_tn(left, right):
    return lax.dot_general(left, right, (((0,), (0,)), ((), ())), preferred_element_type=F32)


class Copies:
    def __init__(self, sems):
        self.sems, self.count, self.open = sems, 0, []

    def start(self, source, target):
        assert self.count < self.sems.shape[0]
        copy = pltpu.make_async_copy(source, target, self.sems.at[self.count])
        self.count += 1
        copy.start()
        self.open.append(copy)
        return copy

    def wait(self, copy):
        copy.wait()
        self.open = [other for other in self.open if other is not copy]

    def finish(self):
        for copy in self.open:
            copy.wait()


def loop(count, body, unroll=1):
    def step(index, carry):
        body(index)
        return carry

    lax.fori_loop(0, count, step, 0, unroll=unroll)


def rows_at(start, count, multiple=8):
    return pl.ds(pl.multiple_of(start, multiple), count)


def lanes_of(block):
    return slice(block * LANES, (block + 1) * LANES)


def fold_rows(values):
    count, lanes = values.shape
    return jnp.sum(values.reshape(count // 8, 8, lanes), 0)


def fill_mask(side, mask_ref, images):
    mask_ref[SLOT * images :, :] = jnp.zeros_like(mask_ref[SLOT * images :, :])

    def body(slot):
        row = slot // GRID
        col = slot - row * GRID
        inside = (slot == CELLS) | ((row < side) & (col < side))
        level = jnp.where(inside, 1.0, 0.0).astype(F32)
        mask_ref[rows_at(slot * images, images), :] = jnp.full((images, LANES), level, F32)

    loop(SLOT, body, unroll=2)


def spread(rows_ref, blocks_ref, blocks):
    total = rows_ref.shape[0]

    def body(step):
        at = rows_at(step * 48, 48, 16)
        values = rows_ref[at, :].astype(F32)
        for block in range(blocks):
            blocks_ref[block, at, :] = values[:, lanes_of(block)]

    loop(total // 48, body)


def unspread(blocks_ref, rows_ref, blocks):
    total = rows_ref.shape[0]

    def body(step):
        at = rows_at(step * 48, 48, 16)
        values = [blocks_ref[block, at, :] for block in range(blocks)]
        rows_ref[at, :] = jnp.concatenate(values, 1).astype(BF16)

    loop(total // 48, body)


def natural_slot(slot):
    return jnp.where(slot == CELLS, 0, slot + 1)


def fill_table(vectors, table_ref):
    for row, ref in enumerate(vectors):
        table_ref[row : row + 1, :] = ref[...].astype(F32).reshape(1, -1)


def fill_taps(table, taps_ref, count, blocks):
    for tap in range(count):
        for block in range(blocks):
            taps_ref[block, tap] = jnp.broadcast_to(table[tap : tap + 1, lanes_of(block)], (8, LANES))


def centred(size):
    inset = (7 - size) // 2
    return [(a + inset) * 7 + b + inset for a in range(size) for b in range(size)]


def lane_picker(width, offset, channels):
    lane = lax.broadcasted_iota(jnp.int32, (width, channels), 0)
    channel = lax.broadcasted_iota(jnp.int32, (width, channels), 1)
    return jnp.where(channel == lane + offset, 1.0, 0.0).astype(BF16)


def assemble_taps(kernels, work_ref, table_ref):
    channels = table_ref.shape[1]
    table_ref[...] = jnp.zeros_like(table_ref)
    offset = 0
    for size, kernel_ref in zip((3, 5, 7), kernels):
        width = kernel_ref.shape[1]
        work_ref[0 : size * size, :] = dot(kernel_ref[...], lane_picker(width, offset, channels))
        for tap, place in enumerate(centred(size)):
            table_ref[place : place + 1, :] += work_ref[tap : tap + 1, :]
        offset += width


def correlate(source_ref, taps_ref, size, span, images, block, sub, emit, turned=False, beside=()):
    margin, inset = size // 2, (span - size) // 2
    beside = iter(beside)

    def load(cell):
        return source_ref[block, rows_at(cell * images + sub * 8, 8), :]

    for row in range(GRID):
        totals = [None] * GRID
        for a in range(size):
            from_row = row + a - margin
            if not 0 <= from_row < GRID:
                continue
            cells = [load(from_row * GRID + col) for col in range(GRID)]
            for b in range(size):
                tap = (a + inset) * span + b + inset
                weight = taps_ref[block, span * span - 1 - tap if turned else tap]
                for col in range(GRID):
                    from_col = col + b - margin
                    if 0 <= from_col < GRID:
                        term = cells[from_col] * weight
                        totals[col] = term if totals[col] is None else totals[col] + term
        for col in range(GRID):
            emit(row * GRID + col, totals[col])
        next(beside, None)
        next(beside, None)
    for _ in beside:
        pass


def tap_sums(grad_ref, source_ref, sums_ref, size, span, images, block, sub):
    margin, inset = size // 2, (span - size) // 2

    def load(ref, cell):
        return ref[block, rows_at(cell * images + sub * 8, 8), :]

    for a in range(size):
        totals = [None] * size
        for row in range(GRID):
            from_row = row + a - margin
            if not 0 <= from_row < GRID:
                continue
            grads = [load(grad_ref, row * GRID + col) for col in range(GRID)]
            cells = [load(source_ref, from_row * GRID + col) for col in range(GRID)]
            for b in range(size):
                part = None
                for col in range(GRID):
                    from_col = col + b - margin
                    if 0 <= from_col < GRID:
                        term = grads[col] * cells[from_col]
                        part = term if part is None else part + term
                totals[b] = part if totals[b] is None else totals[b] + part
        for b in range(size):
            tap = (a + inset) * span + b + inset
            sums_ref[block, tap] += totals[b]


def by_block(images, body, before=None, beside=None):
    subs = images // 8
    first = 0
    while first < len(KERNEL_SIZES):
        size = KERNEL_SIZES[first]
        count = 1
        while first + count < len(KERNEL_SIZES) and KERNEL_SIZES[first + count] == size:
            count += 1
        for block in range(first, first + count):
            if before is not None:
                before(block)
        last = beside is not None and first + count == len(KERNEL_SIZES)
        share = images // (count * subs)

        def step(index, first=first, size=size, last=last, share=share):
            if last:
                work = (part for one in range(share) for part in beside(index * share + one))
                body(size, first + index // subs, index % subs, work)
            else:
                body(size, first + index // subs, index % subs)

        loop(count * subs, step)
        first += count


def row_sums(value):
    high = value.astype(BF16)
    low = (value - high.astype(F32)).astype(BF16)
    return dot(jnp.concatenate([high, low], 1), jnp.ones((2 * LANES, LANES), BF16))


def row_means(blocks):
    return row_sums(sum(blocks[1:], blocks[0])) * (1.0 / (len(blocks) * LANES))


def norm_parts(blocks):
    mean = row_means(blocks)
    centered = [value - mean for value in blocks]
    inverse = lax.rsqrt(row_means([value * value for value in centered]) + EPSILON)
    return [value * inverse for value in centered], inverse


def norm_forward(source_ref, table_ref, gain_row, shift_row, normed_ref, turned_ref, parts_ref, inverse_ref, keep=None):
    blocks = source_ref.shape[0]
    gains = table_ref[gain_row : gain_row + 1, :]
    shifts = table_ref[shift_row : shift_row + 1, :]

    def body(step):
        at = rows_at(step * BAND, BAND, BAND)
        source = [source_ref[block, at, :] for block in range(blocks)]
        if keep is not None:
            keep(at, source)
        parts, inverse = norm_parts(source)
        inverse_ref[at, :] = inverse
        for block in range(blocks):
            parts_ref[block, at, :] = parts[block]
        out = [
            parts[block] * gains[:, lanes_of(block)] + shifts[:, lanes_of(block)]
            for block in range(blocks)
        ]
        normed_ref[at, :] = jnp.concatenate(out, 1).astype(BF16)

    loop(source_ref.shape[1] // BAND, body, unroll=2)
    transpose_rows(normed_ref, turned_ref)


def transpose_rows(rows_ref, turned_ref):
    width = rows_ref.shape[1]

    def body(step):
        at = rows_at(step * TILE, TILE, TILE)
        turned_ref[0:width, at] = rows_ref[at, :].T

    loop(rows_ref.shape[0] // TILE, body)


def norm_backward(parts_ref, inverse_ref, grad_at, direct_at, table_ref, gain_row, emit, blocks, total):
    gains = table_ref[gain_row : gain_row + 1, :]

    def body(step, sums):
        at = rows_at(step * BAND, BAND, BAND)
        parts, inverse = [parts_ref[block, at, :] for block in range(blocks)], inverse_ref[at, :]
        grads = [grad_at(block, at) for block in range(blocks)]
        scaled = [grads[block] * gains[:, lanes_of(block)] for block in range(blocks)]
        product = [grads[block] * parts[block] for block in range(blocks)]
        crossed = [product[block] * gains[:, lanes_of(block)] for block in range(blocks)]
        mean, cross = row_means(scaled), row_means(crossed)
        out = [
            direct_at(block, at) + inverse * (scaled[block] - mean - parts[block] * cross)
            for block in range(blocks)
        ]
        emit(at, out)
        gain_sums = [sums[0][block] + fold_rows(product[block]) for block in range(blocks)]
        shift_sums = [sums[1][block] + fold_rows(grads[block]) for block in range(blocks)]
        return (gain_sums, shift_sums)

    zero = [jnp.zeros((8, LANES), F32) for _ in range(blocks)]
    return lax.fori_loop(0, total // BAND, body, (zero, zero), unroll=2)


def total_row(parts):
    return jnp.concatenate([jnp.sum(part, 0, keepdims=True) for part in parts], 1)


def head_mask():
    row = lax.broadcasted_iota(jnp.int32, (LANES, LANES), 0)
    col = lax.broadcasted_iota(jnp.int32, (LANES, LANES), 1)
    size = LANES // 2
    return jnp.where((row < size) == (col < size), size ** (-0.5), 0.0).astype(F32)


def pack_kernel(bias_ref, fc1_ref, fc2_ref, packed_ref):
    channels = fc1_ref.shape[0]
    packed_ref[0:channels, :] = fc1_ref[...]
    packed_ref[channels : 2 * channels, :] = fc2_ref[...]
    rest = packed_ref.at[2 * channels :, :]
    rest[...] = jnp.broadcast_to(bias_ref[...].reshape(1, -1), rest.shape)


def front_kernel(
    side_ref, tokens_ref, cpe_ref, small_ref, middle_ref, large_ref, qkv_ref, proj_ref,
    cpe_bias_ref, gain_ref, shift_ref, query_bias_ref, value_bias_ref, crpe_bias_ref, proj_bias_ref,
    crpe_ref, mask_out, input_out, parts_out, inverse_out, query_out, weight_out, value_out, convolved_out, normed_t_out, context_out, attended_t_out, second_out,
    input_ref, inverse_ref, query_ref, weight_ref, value_ref, convolved_ref, normed_t_ref, context_ref, attended_t_ref,
    second_ref, position_ref, mask_ref, work_ref, normed_ref, cpe_taps_ref, crpe_taps_ref, crpe_work_ref, table_ref, sems,
):
    fill_table(
        (cpe_bias_ref, gain_ref, shift_ref, query_bias_ref, value_bias_ref, crpe_bias_ref, proj_bias_ref), table_ref
    )
    out = Copies(sems)
    rows, channels = tokens_ref.shape
    blocks = channels // LANES
    images = rows // SLOT
    padded = normed_ref.shape[0]
    held = SLOT_PAD * images
    fill_mask(side_ref[0], mask_ref, images)
    assemble_taps((small_ref, middle_ref, large_ref), crpe_work_ref, crpe_ref)
    fill_taps(cpe_ref[...].astype(F32), cpe_taps_ref, 9, blocks)
    fill_taps(crpe_ref, crpe_taps_ref, 49, blocks)
    spread(tokens_ref, work_ref, blocks)

    def arrange(slot):
        at = rows_at(slot * images, images)
        mask = mask_ref[at, :]
        for block in range(blocks):
            values = work_ref[block, pl.ds(natural_slot(slot), images, stride=SLOT), :]
            input_ref[block, at, :] = values * mask

    out.start(mask_ref, mask_out)
    loop(SLOT, arrange, unroll=2)
    for ref in (input_ref, position_ref, convolved_ref):
        ref[:, rows:padded, :] = jnp.zeros((blocks, padded - rows, LANES), F32)
    position_ref[:, CELLS * images : rows, :] = input_ref[:, CELLS * images : rows, :]
    convolved_ref[:, CELLS * images : rows, :] = jnp.zeros((blocks, images, LANES), F32)

    subs = images // 8

    def position(index):
        block, sub = index // subs, index % subs
        bias = table_row(table_ref, CPE_B, block)

        def emit(cell, total):
            at = rows_at(cell * images + sub * 8, 8)
            position_ref[block, at, :] = input_ref[block, at, :] + mask_ref[at, :] * (total + bias)

        correlate(input_ref, cpe_taps_ref, 3, 3, images, block, sub, emit)

    loop(blocks * subs, position)
    out.start(input_ref, input_out)
    norm_forward(
        position_ref, table_ref, GAIN1, SHIFT1, normed_ref, normed_t_ref, second_ref, inverse_ref
    )
    sent_parts = out.start(second_ref, parts_out)
    out.start(inverse_ref, inverse_out)
    normed_t_ref[channels:, :] = jnp.ones_like(normed_t_ref[channels:, :])
    out.start(normed_t_ref, normed_t_out)

    def project(step):
        at = rows_at(step * TILE, TILE, TILE)
        normed = normed_ref[at, :]
        mask = mask_ref[at, :]
        query = dot(normed, qkv_ref[:, :channels]) + table_ref[QUERY_B : QUERY_B + 1, :]
        for block in range(blocks):
            query_ref[block, at, :] = query[:, lanes_of(block)]
        key = dot(normed, qkv_ref[:, channels : 2 * channels])
        for block in range(blocks):
            weight_ref[block, at, :] = key[:, lanes_of(block)]
        value = dot(normed, qkv_ref[:, 2 * channels :]) + table_ref[VALUE_B : VALUE_B + 1, :]
        for block in range(blocks):
            value_ref[block, at, :] = value[:, lanes_of(block)] * mask

    loop(padded // TILE, project)
    for ref in (query_ref, value_ref):
        ref[:, padded:held, :] = jnp.zeros((blocks, held - padded, LANES), F32)
    weight_ref[:, rows:held, :] = jnp.zeros((blocks, held - rows, LANES), F32)
    out.start(query_ref, query_out)
    out.start(value_ref, value_out)

    def soften(index):
        block, sub = index // subs, index % subs
        top = None
        for slot in range(SLOT):
            at = rows_at(slot * images + sub * 8, 8)
            key = jnp.where(mask_ref[at, :] > 0, weight_ref[block, at, :], -1e30)
            top = key if top is None else jnp.maximum(top, key)
        total = None
        for slot in range(SLOT):
            at = rows_at(slot * images + sub * 8, 8)
            mask = mask_ref[at, :]
            key = jnp.where(mask > 0, weight_ref[block, at, :], -1e30)
            level = jnp.exp(key - top) * mask
            weight_ref[block, at, :] = level
            total = level if total is None else total + level
        inverse = 1.0 / total
        for slot in range(SLOT):
            at = rows_at(slot * images + sub * 8, 8)
            weight_ref[block, at, :] = weight_ref[block, at, :] * inverse

    loop(blocks * subs, soften)
    out.start(weight_ref, weight_out)
    heads = head_mask()

    def attend(image):
        at = pl.ds(image, SLOT_PAD, stride=images)
        for block in range(blocks):
            weight = weight_ref[block, at, :].astype(BF16)
            value = value_ref[block, at, :].astype(BF16)
            query = query_ref[block, at, :].astype(BF16)
            context = (dot_tn(weight, value) * heads).astype(BF16)
            context_ref[image, block] = context
            work_ref[block, at, :] = dot(query, context)
            yield

    def convolve(size, block, sub, beside=()):
        bias = table_row(table_ref, CRPE_B, block)

        def emit(cell, total):
            convolved_ref[block, rows_at(cell * images + sub * 8, 8), :] = total + bias

        correlate(value_ref, crpe_taps_ref, size, 7, images, block, sub, emit, beside=beside)

    by_block(images, convolve, beside=attend)
    out.start(convolved_ref, convolved_out)
    out.start(context_ref, context_out)
    out.wait(sent_parts)

    def finish(step):
        at = rows_at(step * TILE, TILE, TILE)
        attended = jnp.concatenate(
            [
                work_ref[block, at, :] + query_ref[block, at, :] * convolved_ref[block, at, :]
                for block in range(blocks)
            ],
            1,
        ).astype(BF16)
        attended_t_ref[:, at] = attended.T
        branch = dot(attended, proj_ref[...]) + table_ref[PROJ_B : PROJ_B + 1, :]
        for block in range(blocks):
            second_ref[block, at, :] = position_ref[block, at, :] + branch[:, lanes_of(block)]

    half = padded // TILE // 2
    loop(half, finish)
    part = slice(0, half * TILE)
    out.start(second_ref.at[:, part], second_out.at[:, part])
    loop(padded // TILE - half, lambda step: finish(step + half))
    part = slice(half * TILE, padded)
    out.start(second_ref.at[:, part], second_out.at[:, part])
    out.start(attended_t_ref, attended_t_out)
    out.finish()


def table_row(table_ref, row, block):
    return table_ref[row : row + 1, pl.ds(pl.multiple_of(block * LANES, LANES), LANES)]


def gelu_parts(value):
    level = 0.5 + 0.5 * lax.erf(value * math.sqrt(0.5))
    return level, jnp.exp2(value * value * (-0.5 / math.log(2.0))) * (1.0 / math.sqrt(2.0 * math.pi))


def mlp_kernel(
    side_ref, cot_ref, mask_ref, second_in, fc_in, gain_ref, shift_ref, fc2_bias_ref,
    result_out, grad_out, grad_fc_keep, grad_fc_send, small_ref,
    second_ref, fc_ref, grad_ref, grad_fc_ref,
    work_ref, cot_rows_ref, cot_t_ref, normed_ref, normed_t_ref, hidden_ref, pre_ref, hidden_two_ref, pre_two_ref, mlp_ref, back_ref,
    table_ref, result_ref, inverse_ref, sems,
):
    fill_table((gain_ref, shift_ref, fc2_bias_ref), table_ref)
    copies = Copies(sems)
    got_second = copies.start(second_in, second_ref)
    got_fc = copies.start(fc_in, fc_ref)
    rows, channels = cot_ref.shape
    blocks = channels // LANES
    images = rows // SLOT
    padded = normed_ref.shape[0]
    owners, _, units = fc_ref.shape
    mine, half_x, half_z = side_ref[1], side_ref[2] & 1, (side_ref[2] >> 1) & 1
    spread(cot_ref, work_ref, blocks)
    cot_rows_ref[rows:padded, :] = jnp.zeros((padded - rows, channels), BF16)

    def arrange(step, sums):
        at = rows_at(step * (2 * images), 2 * images, 16)
        mask = mask_ref[at, :]
        parts = []
        for block in range(blocks):
            pair = [
                work_ref[block, pl.ds(natural_slot(2 * step + one), images, stride=SLOT), :]
                for one in range(2)
            ]
            parts.append(jnp.concatenate(pair, 0) * mask)
        cot_rows_ref[at, :] = jnp.concatenate(parts, 1).astype(BF16)
        return [sums[block] + fold_rows(parts[block]) for block in range(blocks)]

    zero = [jnp.zeros((8, LANES), F32) for _ in range(blocks)]
    bias_sums = lax.fori_loop(0, SLOT // 2, arrange, zero)
    transpose_rows(cot_rows_ref, cot_t_ref)
    got_second.wait()
    fc2_bias = table_ref[FC2_B : FC2_B + 1, :]

    def keep(at, second):
        for block in range(blocks):
            mlp_ref[at, lanes_of(block)] = second[block] + fc2_bias[:, lanes_of(block)]

    norm_forward(
        second_ref, table_ref, GAIN2, SHIFT2, normed_ref, normed_t_ref, second_ref, inverse_ref, keep
    )
    normed_t_ref[channels:, :] = jnp.ones_like(normed_t_ref[channels:, :])
    half = units // 2
    got_fc.wait()

    full = padded // MLP_TILE
    wide = units // full
    ends = 2
    rows_half = MLP_TILE // ends

    def weights(slot, held, step):
        cols = pl.ds(pl.multiple_of(step * wide, wide), wide)
        hidden_ref, pre_ref = held
        for which, (left_ref, right_ref) in enumerate(((normed_t_ref, pre_ref), (cot_t_ref, hidden_ref))):
            grad = dot(left_ref[...], right_ref[:, cols]).astype(BF16)
            for end in range(2):
                place = ((half_x ^ which) << 1) | (half_z ^ end)
                grad_fc_ref[slot, place, 0:PIECE, cols] = grad[end * PIECE : (end + 1) * PIECE]
            if which == 0:
                grad_fc_ref[slot, (half_x << 1) | half_z, PIECE:, cols] = grad[channels:]
            yield

    def part(slot, held, before):
        owner = mine ^ ((slot >> 1) | ((slot & 1) << 1))
        hidden_ref, pre_ref = held

        def tile(step):
            beside = iter(()) if before is None else weights(slot - 1, before, step)
            for end in range(ends):
                at = rows_at(step * MLP_TILE + end * rows_half, rows_half, rows_half)
                normed = normed_ref[at, :]
                cot = cot_rows_ref[at, :]
                mlp, back = None, None
                for piece in range(2):
                    cols = slice(piece * half, (piece + 1) * half)
                    first = fc_ref[owner, 0:channels, cols]
                    second = fc_ref[owner, channels + piece * half : channels + (piece + 1) * half, :]
                    bias = fc_ref[owner, 2 * channels :, cols].astype(F32)[0:1]
                    values, grads = dot(normed, first), dot_nt(cot, second)
                    if piece == 0:
                        next(beside, None)
                    values = values + bias
                    level, density = gelu_parts(values)
                    hidden = (values * level).astype(BF16)
                    pre = (grads * (level + values * density)).astype(BF16)
                    hidden_ref[at, cols] = hidden
                    pre_ref[at, cols] = pre
                    more_mlp, more_back = dot(hidden, second), dot_nt(pre, first)
                    mlp = more_mlp if mlp is None else mlp + more_mlp
                    back = more_back if back is None else back + more_back
                if slot == 0:
                    back_ref[at, :] = back
                else:
                    back_ref[at, :] += back
                if slot < owners - 1:
                    mlp_ref[at, :] += mlp
                else:
                    result_ref[at, :] = (mlp_ref[at, :] + mlp).astype(BF16)

        loop(full, tile)

    def last_weights(step):
        for _ in weights(owners - 1, held[(owners - 1) % 2], step):
            pass

    held = (hidden_ref, pre_ref), (hidden_two_ref, pre_two_ref)
    targets = [(grad_fc_keep if slot < owners // 2 else grad_fc_send).at[slot % (owners // 2)] for slot in range(owners)]
    for slot in range(owners + 1):
        if slot < owners:
            part(slot, held[slot % 2], held[(slot - 1) % 2] if slot else None)
        else:
            loop(full, last_weights)
        if slot:
            copies.start(grad_fc_ref.at[slot - 1], targets[slot - 1])

    def grad_at(block, at):
        return back_ref[at, lanes_of(block)]

    def direct_at(block, at):
        return cot_rows_ref[at, lanes_of(block)].astype(F32)

    def emit(at, out):
        for block in range(blocks):
            grad_ref[block, at, :] = out[block]

    gain_sums, shift_sums = norm_backward(
        second_ref, inverse_ref, grad_at, direct_at, table_ref, GAIN2, emit, blocks, padded
    )
    copies.start(grad_ref, grad_out)
    copies.start(result_ref, result_out)
    small_ref[...] = jnp.zeros_like(small_ref)
    small_ref[0:1, :] = total_row(gain_sums)
    small_ref[1:2, :] = total_row(shift_sums)
    small_ref[2:3, :] = total_row(bias_sums)
    for copy in copies.open[2:]:
        copy.wait()


def result_kernel(result_ref, mask_ref, out_ref, work_ref):
    rows, channels = out_ref.shape
    blocks = channels // LANES
    images = rows // SLOT

    def arrange(step):
        at = rows_at(step * (2 * images), 2 * images, 16)
        values = result_ref[at, :].astype(F32)
        mask = mask_ref[at, :]
        for block in range(blocks):
            masked = values[:, lanes_of(block)] * mask
            for one in range(2):
                to = pl.ds(natural_slot(2 * step + one), images, stride=SLOT)
                work_ref[block, to, :] = masked[one * images : (one + 1) * images]

    loop(SLOT // 2, arrange)
    unspread(work_ref, out_ref, blocks)


def branch_kernel(
    proj_ref, grad_in, attended_t_in,
    back_out, grad_proj_ref, small_ref,
    grad_ref, attended_t_ref, back_ref, branch_ref, sems,
):
    copies = Copies(sems)
    padded, channels = branch_ref.shape
    blocks = channels // LANES
    held = back_ref.shape[1]
    half = padded // 2
    halves = slice(0, half), slice(half, padded)
    got = [copies.start(grad_in.at[:, part], grad_ref.at[:, part]) for part in halves]
    got_attended = copies.start(attended_t_in, attended_t_ref)
    back_ref[:, padded:held, :] = jnp.zeros((blocks, held - padded, LANES), F32)
    sent = [copies.start(back_ref.at[:, padded:held], back_out.at[:, padded:held])]

    total = jnp.zeros((8, channels), F32)
    step = half // 2
    for end, part in enumerate(halves):
        got[end].wait()
        for first in range(end * half, (end + 1) * half, step):
            at = slice(first, first + step)
            low = jnp.concatenate([grad_ref[block, at, :] for block in range(blocks)], 1).astype(BF16)
            branch_ref[at, :] = low
            total += fold_rows(low.astype(F32))
            back = dot_nt(low, proj_ref[...])
            for block in range(blocks):
                back_ref[block, at, :] = back[:, lanes_of(block)]
        sent.append(copies.start(back_ref.at[:, part], back_out.at[:, part]))
    got_attended.wait()
    grad_proj_ref[...] = dot(attended_t_ref[...], branch_ref[...]).astype(BF16)
    small_ref[...] = total
    for copy in sent:
        copy.wait()


def mix_kernel(
    side_ref, small_mlp_ref, small_branch_ref, crpe_ref, grad_proj_ref,
    back_in, query_in, weight_in, value_in, convolved_in, normed_t_in, context_in, mask_in,
    keep_ref, send_ref, projected_out,
    total_ref, back_ref, query_ref, weight_ref, value_ref, convolved_ref, normed_t_ref, context_ref, projected_ref,
    mask_ref, small_ref, edge_ref, turned_ref, crpe_taps_ref, sems,
):
    copies = Copies(sems)
    pairs = (back_in, back_ref), (query_in, query_ref), (convolved_in, convolved_ref)
    first = [
        [copies.start(source.at[block], target.at[block]) for source, target in pairs] for block in range(back_ref.shape[0])
    ]
    pairs = (weight_in, weight_ref), (value_in, value_ref), (context_in, context_ref), (mask_in, mask_ref)
    pairs += ((normed_t_in, normed_t_ref),)
    then = [copies.start(*pair) for pair in pairs]
    blocks, padded, _ = edge_ref.shape
    channels = blocks * LANES
    held = query_ref.shape[1]
    images = held // SLOT_PAD
    rows = images * SLOT
    subs = images // 8
    fill_taps(crpe_ref, crpe_taps_ref, 49, blocks)
    turned_ref[:, CELLS * images :, :] = jnp.zeros((blocks, padded - CELLS * images, LANES), F32)
    bias_sums = []

    def arrived(block):
        for copy in first[block]:
            copy.wait()

        def edges(step, total):
            at = rows_at(step * (9 * images), 9 * images)
            back = back_ref[block, at, :]
            edge = back * query_ref[block, at, :]
            edge_ref[block, at, :] = edge
            convolved_ref[block, at, :] = back * convolved_ref[block, at, :]
            return total + fold_rows(edge)

        bias_sums.append(lax.fori_loop(0, CELLS // 9, edges, jnp.zeros((8, LANES), F32)))

    def convolve(size, block, sub):
        def emit(cell, total):
            turned_ref[block, rows_at(cell * images + sub * 8, 8), :] = total

        correlate(edge_ref, crpe_taps_ref, size, 7, images, block, sub, emit, turned=True)

    by_block(images, convolve, arrived)
    for copy in then:
        copy.wait()
    heads = head_mask()

    def attend(image):
        at = pl.ds(image, SLOT_PAD, stride=images)
        for block in range(blocks):
            weight = weight_ref[block, at, :]
            low = weight.astype(BF16)
            value = value_ref[block, at, :].astype(BF16)
            query = query_ref[block, at, :].astype(BF16)
            back = back_ref[block, at, :].astype(BF16)
            context = context_ref[image, block]
            grad = (dot_tn(query, back) * heads).astype(BF16)
            query_ref[block, at, :] = dot_nt(back, context)
            key = dot_nt(value, grad)
            back_ref[block, at, :] = weight * (key - jnp.sum(weight * key, 0, keepdims=True))
            value_ref[block, at, :] = dot(low, grad)

    loop(images, attend, unroll=4)
    projected_ref[rows:padded, :] = jnp.zeros((padded - rows, 3 * channels), BF16)

    def gather(step):
        at = rows_at(step * (2 * images), 2 * images, 16)
        mask = mask_ref[at, :]
        parts = [[], [], []]
        for block in range(blocks):
            parts[0].append(query_ref[block, at, :] + convolved_ref[block, at, :])
            parts[1].append(back_ref[block, at, :])
            parts[2].append((value_ref[block, at, :] + turned_ref[block, at, :]) * mask)
        for which in range(3):
            cols = slice(which * channels, (which + 1) * channels)
            projected_ref[at, cols] = jnp.concatenate(parts[which], 1).astype(BF16)

    loop(SLOT // 2, gather)
    sent = copies.start(projected_ref, projected_out)
    small_ref[...] = jnp.zeros_like(small_ref)
    index = ((side_ref[1] & 1) << 2) | ((side_ref[2] & 1) << 1) | (side_ref[1] >> 1)

    def place(matrix, grad):
        for end in range(channels // PIECE):
            piece = matrix * (channels // PIECE) + end
            total_ref[piece ^ index, 0:PIECE, :] = grad[end * PIECE : (end + 1) * PIECE]

    for which in range(3):
        cols = slice(which * channels, (which + 1) * channels)
        grad = dot(normed_t_ref[...], projected_ref[:, cols])
        place(which, grad[0:channels].astype(BF16))
        small_ref[56 + which : 57 + which, :] = grad[channels : channels + 1]
    place(3, grad_proj_ref[...])
    small_ref[49:50, :] = total_row(bias_sums)
    small_ref[50:51, :] = jnp.sum(small_branch_ref[...], 0, keepdims=True)
    small_ref[64:72, :] = small_mlp_ref[...]
    for piece in range(total_ref.shape[0]):
        total_ref[piece ^ index, PIECE:, :] = small_ref[piece * 16 : (piece + 1) * 16, :].astype(BF16)
    out = [copies.start(total_ref.at[4:8], send_ref), copies.start(total_ref.at[0:4], keep_ref)]
    for copy in [sent] + out:
        copy.wait()


def taps_kernel(
    back_in, query_in, value_in,
    small_ref,
    back_ref, query_ref, value_ref, sums_ref, sems,
):
    copies = Copies(sems)
    blocks, cells, _ = back_ref.shape
    images = cells // CELLS
    part = slice(0, cells)
    pairs = (back_in, back_ref), (query_in, query_ref), (value_in, value_ref)
    got = [
        [copies.start(source.at[block, part], target.at[block]) for source, target in pairs] for block in range(blocks)
    ]
    sums_ref[...] = jnp.zeros_like(sums_ref)

    def arrived(block):
        for copy in got[block]:
            copy.wait()

        def edges(step):
            at = rows_at(step * (9 * images), 9 * images)
            back_ref[block, at, :] = back_ref[block, at, :] * query_ref[block, at, :]

        loop(CELLS // 9, edges)

    def taps(size, block, sub):
        tap_sums(back_ref, value_ref, sums_ref, size, 7, images, block, sub)

    by_block(images, taps, arrived)
    small_ref[...] = jnp.zeros_like(small_ref)
    for block in range(blocks):
        small_ref[0:49, lanes_of(block)] = jnp.sum(sums_ref[block], 1)


def norm_half(
    copies, first, base, operands, grad_out, projected_ref, parts_ref, inverse_ref, grad_ref, normed_ref, table_ref
):
    qkv_ref, gain_ref, projected_in, parts_in, inverse_in, grad_in = operands
    fill_table((gain_ref,), table_ref)
    padded, channels = normed_ref.shape
    blocks = channels // LANES
    half = padded // 2
    got_halves = [
        copies.start(projected_in.at[pl.ds(first + end * half, half)], projected_ref.at[pl.ds(end * half, half)])
        for end in range(2)
    ]
    source, target = pl.ds(first, padded), pl.ds(base, padded)
    got = [
        copies.start(parts_in.at[:, source], parts_ref),
        copies.start(inverse_in.at[source], inverse_ref),
        copies.start(grad_in.at[:, source], grad_ref.at[:, target]),
    ]

    for end in range(2):
        got_halves[end].wait()
        at = slice(end * half, (end + 1) * half)
        normed_ref[at, :] = dot_nt(projected_ref[at, :], qkv_ref[...])
    for copy in got:
        copy.wait()

    def grad_at(block, at):
        return normed_ref[at, lanes_of(block)]

    def moved(at):
        return rows_at(base + at.start, at.size, BAND)

    def direct_at(block, at):
        return grad_ref[block, moved(at), :]

    def emit_norm(at, out):
        for block in range(blocks):
            grad_ref[block, moved(at), :] = out[block]

    sums = norm_backward(parts_ref, inverse_ref, grad_at, direct_at, table_ref, 0, emit_norm, blocks, padded)
    return copies.start(grad_ref.at[:, target], grad_out), sums


def norm_first_kernel(
    qkv_ref, gain_ref, projected_in, parts_in, inverse_in, grad_in,
    grad_out, small_ref,
    projected_ref, parts_ref, inverse_ref, grad_ref, normed_ref, table_ref, sems,
):
    operands = qkv_ref, gain_ref, projected_in, parts_in, inverse_in, grad_in
    sent, (gain_sums, shift_sums) = norm_half(
        Copies(sems), 0, 0, operands, grad_out, projected_ref, parts_ref, inverse_ref, grad_ref, normed_ref,
        table_ref,
    )
    small_ref[...] = jnp.zeros_like(small_ref)
    small_ref[0:1, :] = total_row(gain_sums)
    small_ref[1:2, :] = total_row(shift_sums)
    sent.wait()


def norm_last_kernel(
    first, qkv_ref, gain_ref, projected_in, parts_in, inverse_in, grad_in, grad_first_in, input_in, small_first_ref,
    small_taps_ref,
    grad_out, small_ref,
    projected_ref, parts_ref, inverse_ref, grad_ref, normed_ref, table_ref, input_ref, sums_ref, work_ref, sems,
):
    copies = Copies(sems)
    blocks, cells, _ = input_ref.shape
    images = cells // CELLS
    subs = images // 8
    got = copies.start(grad_first_in, grad_ref.at[:, 0:first]), copies.start(input_in.at[:, 0:cells], input_ref)
    operands = qkv_ref, gain_ref, projected_in, parts_in, inverse_in, grad_in
    sent, (gain_sums, shift_sums) = norm_half(
        copies, first, first, operands, grad_out, projected_ref, parts_ref, inverse_ref, grad_ref, normed_ref,
        table_ref,
    )
    sums_ref[...] = jnp.zeros_like(sums_ref)
    work_ref[...] = jnp.zeros_like(work_ref)
    work_ref[0:56, :] = small_taps_ref[...]
    work_ref[57:58, :] = total_row(gain_sums) + small_first_ref[0:1, :]
    work_ref[58:59, :] = total_row(shift_sums) + small_first_ref[1:2, :]
    for copy in got:
        copy.wait()

    def colsum(step, sums):
        at = rows_at(step * (9 * images), 9 * images)
        return [sums[block] + fold_rows(grad_ref[block, at, :]) for block in range(blocks)]

    zero = [jnp.zeros((8, LANES), F32) for _ in range(blocks)]
    work_ref[56:57, :] = total_row(lax.fori_loop(0, GRID, colsum, zero))

    def taps(index):
        tap_sums(grad_ref, input_ref, sums_ref, 3, 3, images, index // subs, index % subs)

    loop(blocks * subs, taps)
    for block in range(blocks):
        work_ref[64:73, lanes_of(block)] = jnp.sum(sums_ref[block], 1)
    small_ref[...] = work_ref[...].astype(BF16)
    sent.wait()


def back_kernel(
    mask_ref, cpe_ref, first_in, second_in,
    tokens_ref,
    grad_ref, work_ref, result_ref, taps_ref, sems,
):
    copies = Copies(sems)
    half = first_in.shape[1]
    got = copies.start(first_in, grad_ref.at[:, 0:half]), copies.start(second_in, grad_ref.at[:, half : 2 * half])
    rows, channels = tokens_ref.shape
    blocks = channels // LANES
    images = rows // SLOT
    subs = images // 8
    fill_taps(cpe_ref[...].astype(F32), taps_ref, 9, blocks)
    for copy in got:
        copy.wait()

    def convolve(index):
        block, sub = index // subs, index % subs

        def emit(cell, total):
            at = rows_at(cell * images + sub * 8, 8)
            result_ref[block, at, :] = (grad_ref[block, at, :] + total) * mask_ref[at, :]

        correlate(grad_ref, taps_ref, 3, 3, images, block, sub, emit, turned=True)

    loop(blocks * subs, convolve)
    result_ref[:, CELLS * images : rows, :] = grad_ref[:, CELLS * images : rows, :]

    def arrange(slot):
        at = rows_at(slot * images, images)
        for block in range(blocks):
            work_ref[block, pl.ds(natural_slot(slot), images, stride=SLOT), :] = result_ref[block, at, :]

    loop(SLOT, arrange, unroll=2)
    unspread(work_ref, tokens_ref, blocks)


def finish_fc_kernel(
    side_ref, first_ref, second_ref, third_ref, fourth_ref,
    fc1_ref, fc2_ref, bias_ref,
    held_ref,
):
    index = ((side_ref[2] & 1) << 1) | ((side_ref[2] >> 1) & 1)
    for place, piece in enumerate((first_ref, second_ref, third_ref, fourth_ref)):
        held_ref[place ^ index] = piece[...]
    for end in range(2):
        fc1_ref[end * PIECE : (end + 1) * PIECE, :] = held_ref[end, 0:PIECE, :].astype(F32)
        fc2_ref[:, end * PIECE : (end + 1) * PIECE] = held_ref[2 + end, 0:PIECE, :].astype(F32).T
    bias_ref[...] = held_ref[0, PIECE:, :].astype(F32)[0:1].reshape(bias_ref.shape)


def finish_small_kernel(
    small_ref,
    cpe_ref, cpe_bias_ref, gain_ref, shift_ref, crpe_small_ref, crpe_middle_ref, crpe_large_ref,
    work_ref,
):
    small = small_ref[...]
    work_ref[...] = small.astype(F32)
    cpe_ref[...] = work_ref[64:73, :]
    for row, ref in enumerate((cpe_bias_ref, gain_ref, shift_ref)):
        ref[...] = work_ref[56 + row : 57 + row, :].reshape(ref.shape)
    channels = small.shape[1]
    offset = 0
    for size, ref in zip((3, 5, 7), (crpe_small_ref, crpe_middle_ref, crpe_large_ref)):
        width = ref.shape[1]
        taps = dot_nt(small, lane_picker(width, offset, channels))
        for tap, place in enumerate(centred(size)):
            ref[tap : tap + 1, :] = taps[place : place + 1, :]
        offset += width


def finish_kernel(side_ref, *refs):
    pieces, (qkv_out, proj_out), rows = refs[:8], refs[8:10], refs[10:-5]
    held_ref, small_ref, qkv_ref, proj_ref, sems = refs[-5:]
    copies = Copies(sems)
    index = ((side_ref[1] & 1) << 2) | ((side_ref[2] & 1) << 1) | (side_ref[1] >> 1)
    for place, piece in enumerate(pieces):
        held_ref[place ^ index] = piece[...]
    channels = proj_ref.shape[1]
    for piece in range(8):
        matrix, end = piece // 2, piece % 2
        at = slice(end * PIECE, (end + 1) * PIECE)
        cols = slice(matrix * channels, (matrix + 1) * channels)
        values = held_ref[piece, 0:PIECE, :].astype(F32)
        if matrix < 3:
            qkv_ref[at, cols] = values
            copies.start(qkv_ref.at[at, cols], qkv_out.at[at, cols])
        else:
            proj_ref[at, :] = values
            copies.start(proj_ref.at[at], proj_out.at[at])
        small_ref[piece * 16 : (piece + 1) * 16, :] = held_ref[piece, PIECE:, :].astype(F32)
    for row, ref in zip(SMALL_ROWS, rows):
        ref[...] = small_ref[row : row + 1, :].reshape(ref.shape)
    copies.finish()


def add(*terms):
    return sum(term.astype(F32) for term in terms).astype(BF16)


def exchange(values, across_dp, across_blk):
    owners, parts = lax.axis_size("blk"), lax.axis_size("dp")
    flip = across_dp * owners + across_blk
    return lax.ppermute(values, ("dp", "blk"), [(at, at ^ flip) for at in range(parts * owners)])


def together(*values):
    return lax.optimization_barrier(values)


def shape(dims, dtype):
    return jax.ShapeDtypeStruct(dims, dtype)


def call(body, outs, scratch, cost, *operands):
    vmem, smem, hbm = (pl.BlockSpec(memory_space=space) for space in (pltpu.VMEM, pltpu.SMEM, pl.ANY))

    def place(value):
        return hbm if isinstance(value, Held) else smem if value.dtype == jnp.int32 else vmem

    def plain(values):
        return [value.array if isinstance(value, Held) else value for value in values]

    return pl.pallas_call(
        body,
        out_shape=plain(outs),
        in_specs=[place(value) for value in operands],
        out_specs=[place(value) for value in outs],
        scratch_shapes=[
            pltpu.SemaphoreType.DMA((item,)) if isinstance(item, int) else pltpu.VMEM(*item) for item in scratch
        ],
        compiler_params=pltpu.CompilerParams(vmem_limit_bytes=VMEM_BYTES),
        cost_estimate=pl.CostEstimate(flops=cost, bytes_accessed=cost // 1000, transcendentals=0),
    )(*plain(operands))


class Held:
    def __init__(self, array):
        self.array = array


def shards(
    tokens, sides, cpe_weight, cpe_bias, norm1_gain, norm1_shift, w_qkv, query_bias, value_bias,
    crpe_small, crpe_middle, crpe_large, crpe_bias, w_proj, proj_bias, norm2_gain, norm2_shift,
    w_fc1, fc1_bias, w_fc2, fc2_bias, cotangent,
):
    rows, channels = tokens.shape
    blocks = channels // LANES
    images = rows // SLOT
    padded = -(-rows // TILE) * TILE
    held = SLOT_PAD * images
    units = w_fc1.shape[1]
    owners = lax.axis_size("blk")

    (packed,) = call(
        pack_kernel, [shape((2 * channels + 16, units), BF16)], [], 1_000_000, fc1_bias, w_fc1, w_fc2
    )
    fc_all = lax.all_gather(packed, "blk", axis=0, tiled=False)
    scalars = jnp.stack([sides[0], lax.axis_index("blk"), lax.axis_index("dp")]).astype(jnp.int32)
    block_rows = (blocks, padded, LANES)
    block_held = (blocks, held, LANES)
    block_cells = (blocks, CELLS * images, LANES)
    contexts = (images, blocks, LANES, LANES), BF16
    front = [
        (block_rows, F32), (block_rows, F32), ((padded, LANES), F32), (block_held, F32), (block_held, F32), (block_held, F32),
        (block_rows, F32), ((channels + 16, padded), BF16), contexts, ((channels, padded), BF16), (block_rows, F32),
    ]
    crpe, mask, inputs, parts, inverse, query, weight, value, convolved, normed_t, context, attended_t, second = call(
        front_kernel,
        [shape((56, channels), F32), Held(shape((padded, LANES), F32))] + [Held(shape(*item)) for item in front],
        front[:1] + front[2:] + [
            (block_rows, F32), ((padded, LANES), F32), (block_held, F32), ((padded, channels), BF16),
            ((blocks, 9, 8, LANES), F32), ((blocks, 49, 8, LANES), F32), ((56, channels), F32), ((8, channels), F32), 13,
        ],
        40_000_000_000,
        scalars, tokens, cpe_weight, crpe_small, crpe_middle, crpe_large, w_qkv, w_proj,
        cpe_bias, norm1_gain, norm1_shift, query_bias, value_bias, crpe_bias, proj_bias,
    )
    pieces = (owners // 2, 4, PIECE + 16, units)
    result, grad_second, fc_keep, fc_send, small_mlp = call(
        mlp_kernel,
        [
            Held(shape((padded, channels), BF16)), Held(shape(block_rows, F32)), Held(shape(pieces, BF16)),
            Held(shape(pieces, BF16)),
            shape((8, channels), F32),
        ],
        [
            (block_rows, F32), (fc_all.shape, BF16), (block_rows, F32),
            ((owners, 4, PIECE + 16, units), BF16),
            ((blocks, rows, LANES), F32),
            ((padded, channels), BF16), ((channels, padded), BF16),
            ((padded, channels), BF16), ((channels + 16, padded), BF16),
            ((padded, units), BF16), ((padded, units), BF16), ((padded, units), BF16), ((padded, units), BF16),
            ((padded, channels), F32), ((padded, channels), F32), ((8, channels), F32), ((padded, channels), BF16), ((padded, LANES), F32), 4 + owners,
        ],
        60_000_000_000,
        scalars, cotangent, mask, Held(second), Held(fc_all), norm2_gain, norm2_shift, fc2_bias,
    )
    fc_far = exchange(fc_send, 0, 1)
    back, grad_proj, small_branch = call(
        branch_kernel,
        [Held(shape(block_held, F32)), shape((channels, channels), BF16), shape((8, channels), F32)],
        [(block_rows, F32), ((channels, padded), BF16), (block_held, F32), ((padded, channels), BF16), 6],
        10_000_000_000,
        w_proj, Held(grad_second), Held(attended_t),
    )

    def half_of(side, end):
        part = slice(2 * end, 2 * end + 2)
        return add(fc_keep[side, part], fc_far[side, part])

    back, fc_y, fc_x, fc_yx, fc_own = together(back, half_of(1, 0), half_of(0, 1), half_of(1, 1), half_of(0, 0))
    fc_far = exchange(fc_y, 0, 2), exchange(fc_x, 1, 0), exchange(fc_yx, 1, 2)
    total_keep, total_send, projected = call(
        mix_kernel,
        [Held(shape((4, PIECE + 16, channels), BF16))] * 2 + [Held(shape((padded, 3 * channels), BF16))],
        [
            ((8, PIECE + 16, channels), BF16),
            (block_held, F32), (block_held, F32), (block_held, F32), (block_held, F32), (block_rows, F32),
            ((channels + 16, padded), BF16), contexts, ((padded, 3 * channels), BF16),
            ((padded, LANES), F32), ((128, channels), F32), (block_rows, F32), (block_rows, F32),
            ((blocks, 49, 8, LANES), F32), 8 + 3 * blocks,
        ],
        50_000_000_000,
        scalars, small_mlp, small_branch, crpe, grad_proj,
        Held(back), Held(query), Held(weight), Held(value), Held(convolved), Held(normed_t), Held(context),
        Held(mask),
    )
    projected, total_keep, total_send, *fc_far = together(projected, total_keep, total_send, *fc_far)
    total_far = exchange(total_send, 0, 1)
    bits = [1 << bit for bit in range(1, lax.axis_size("dp").bit_length() - 1)]
    fc_bits = [bit for bit in bits if bit > 2]

    def end_of(end):
        return add(fc_own[end], *(far[end] for far in fc_far))

    fc_other, fc_own = end_of(1), end_of(0)
    sums = [add(total_keep[piece], total_far[piece]) for piece in range(4)]
    projected, fc_own, fc_other, *sums = together(projected, fc_own, fc_other, *sums)
    fc_far = exchange(fc_other, 2, 0)
    total_far = exchange(sums[1], 0, 2), exchange(sums[2], 1, 0), exchange(sums[3], 1, 2)
    block_half = (blocks, padded // 2, LANES)
    norm_outs = [Held(shape(block_half, F32)), shape((8, channels), F32)]
    norm_scratch = [((padded // 2, 3 * channels), BF16), (block_half, F32), ((padded // 2, LANES), F32)]
    norm_more = [((padded // 2, channels), F32), ((8, channels), F32)]
    grad_first, small_first = call(
        norm_first_kernel, norm_outs, norm_scratch + [(block_half, F32)] + norm_more + [6], 8_000_000_000,
        w_qkv, norm1_gain, Held(projected), Held(parts), Held(inverse), Held(grad_second),
    )
    back, grad_first, fc_own, own = together(back, grad_first, add(fc_own, fc_far), add(sums[0], *total_far))
    total_far = exchange(own, bits[0], 0)
    fc_far = exchange(fc_own, fc_bits[0], 0)
    (small_taps,) = call(
        taps_kernel,
        [shape((56, channels), F32)],
        [(block_cells, F32), (block_cells, F32), (block_cells, F32), ((blocks, 49, 8, LANES), F32), 3 * blocks],
        15_000_000_000,
        Held(back), Held(query), Held(value),
    )
    fc_own = add(fc_own, fc_far)
    for bit in fc_bits[1:]:
        fc_own = add(fc_own, exchange(fc_own, bit, 0))
    projected, small_taps, fc_own, own = together(projected, small_taps, fc_own, add(own, total_far))
    total_far = exchange(own, bits[1], 0)
    fc_other, fc_third = exchange(fc_own, 2, 0), exchange(fc_own, 1, 0)
    grad_last, small_back = call(
        functools.partial(norm_last_kernel, padded // 2),
        [norm_outs[0], shape((80, channels), BF16)],
        norm_scratch + [(block_rows, F32)] + norm_more
        + [(block_cells, F32), ((blocks, 9, 8, LANES), F32), ((80, channels), F32), 8],
        12_000_000_000,
        w_qkv, norm1_gain, Held(projected), Held(parts), Held(inverse), Held(grad_second), Held(grad_first), Held(inputs),
        small_first, small_taps,
    )
    own = add(own, total_far)
    for bit in bits[2:]:
        own = add(own, exchange(own, bit, 0))
    grad_last, small_back, result, fc_other, fc_third, own = together(
        grad_last, small_back, result, fc_other, fc_third, own
    )
    near = [own, exchange(own, 0, 2), exchange(own, 1, 0), exchange(own, 1, 2)]
    small_far, fc_fourth = exchange(small_back, 0, 1), exchange(fc_other, 1, 0)
    (output,) = call(
        result_kernel, [shape((rows, channels), BF16)], [((blocks, rows, LANES), F32)], 1_000_000,
        result, mask,
    )
    output, small, small_far, fc_fourth = together(output, small_back, small_far, fc_fourth)
    small, grad_last = together(add(small, small_far), grad_last)
    small_far = exchange(small, 0, 2)
    (grad_tokens,) = call(
        back_kernel,
        [shape((rows, channels), BF16)],
        [
            (block_rows, F32), ((blocks, rows, LANES), F32),
            (block_rows, F32), ((blocks, 9, 8, LANES), F32), 2,
        ],
        1_000_000,
        mask, cpe_weight, Held(grad_first), Held(grad_last),
    )
    grad_tokens, small, small_far, *near = together(grad_tokens, small, small_far, *near)
    total_pieces = near + [exchange(piece, 0, 1) for piece in near]
    small = add(small, small_far)
    small_far = exchange(small, 1, 0)
    small, fc_own = together(small, fc_own)
    fc1, fc2, fc1_sums = call(
        finish_fc_kernel,
        [shape((channels, units), F32), shape((units, channels), F32), shape((units,), F32)],
        [((4, PIECE + 16, units), BF16)],
        1_000_000,
        scalars, fc_own, fc_other, fc_third, fc_fourth,
    )
    fc1, small, small_far, *total_pieces = together(fc1, small, small_far, *total_pieces)
    small = add(small, small_far)
    small_far = [exchange(small, flip, 0) for flip in (bits[0], bits[1], bits[0] | bits[1])]
    row = shape((channels,), F32)
    grad_qkv, grad_proj, query_sums, value_sums, crpe_sums, proj_sums, gain_two, shift_two, fc2_sums = call(
        finish_kernel,
        [Held(shape((channels, 3 * channels), F32)), Held(shape((channels, channels), F32))] + [row] * len(SMALL_ROWS),
        [
            ((8, PIECE + 16, channels), BF16), ((128, channels), F32),
            ((channels, 3 * channels), F32), ((channels, channels), F32), 8,
        ],
        1_000_000,
        scalars, *total_pieces,
    )
    grad_qkv, small, *small_far = together(grad_qkv, small, *small_far)
    terms = [term.astype(F32) for term in (small, *small_far)]
    small = ((terms[0] + terms[1]) + (terms[2] + terms[3])).astype(BF16)
    for bit in bits[2:]:
        small = add(small, exchange(small, bit, 0))
    cpe, cpe_sums, gain_one, shift_one, taps_small, taps_middle, taps_large = call(
        finish_small_kernel,
        [
            shape(cpe_weight.shape, F32), row, row, row,
            shape(crpe_small.shape, F32), shape(crpe_middle.shape, F32), shape(crpe_large.shape, F32),
        ],
        [((80, channels), F32)],
        1_000_000,
        small,
    )
    return (
        output, grad_tokens, cpe, cpe_sums, gain_one, shift_one, grad_qkv, query_sums, value_sums,
        taps_small, taps_middle, taps_large, crpe_sums, grad_proj, proj_sums, gain_two, shift_two,
        fc1, fc1_sums, fc2, fc2_sums,
    )


def solution(mesh):
    split, whole = P(("dp", "blk"), None), P()
    fc1, fc1_bias, fc2 = P(None, "blk"), P("blk"), P("blk", None)
    return jax.shard_map(
        shards,
        mesh=mesh,
        in_specs=(split, P(("dp", "blk"))) + (whole,) * 15 + (fc1, fc1_bias, fc2, whole, split),
        out_specs=(split, split) + (whole,) * 15 + (fc1, fc1_bias, fc2, whole),
        check_vma=False,
    )
```

```python
import functools
import math

import jax
import jax.numpy as jnp
from jax import lax
from jax.experimental import pallas as pl
from jax.experimental.pallas import tpu as pltpu
from jax.sharding import PartitionSpec as P

HEADS = 8
GRID = 9
CELLS = GRID * GRID
SLOT = CELLS + 1
LANES = 128
EPSILON = 1e-6
SLOT_PAD = 96
TILE = 256
BAND = 128
MLP_TILE = 512
KERNEL_SIZES = (3, 5, 7, 7)
PIECE = 256
VMEM_BYTES = 62 * 1024 * 1024

F32 = jnp.float32
BF16 = jnp.bfloat16

SMALL_ROWS = (56, 58, 49, 50, 64, 65, 66)
CPE_B, GAIN1, SHIFT1, QUERY_B, VALUE_B, CRPE_B, PROJ_B = range(7)
GAIN2, SHIFT2, FC2_B = range(3)


def dot(left, right):
    return lax.dot_general(left, right, (((1,), (0,)), ((), ())), preferred_element_type=F32)


def dot_nt(left, right):
    return lax.dot_general(left, right, (((1,), (1,)), ((), ())), preferred_element_type=F32)


def dot_tn(left, right):
    return lax.dot_general(left, right, (((0,), (0,)), ((), ())), preferred_element_type=F32)


class Copies:
    def __init__(self, sems):
        self.sems, self.count, self.open = sems, 0, []

    def start(self, source, target):
        assert self.count < self.sems.shape[0]
        copy = pltpu.make_async_copy(source, target, self.sems.at[self.count])
        self.count += 1
        copy.start()
        self.open.append(copy)
        return copy

    def wait(self, copy):
        copy.wait()
        self.open = [other for other in self.open if other is not copy]

    def finish(self):
        for copy in self.open:
            copy.wait()


def loop(count, body, unroll=1):
    def step(index, carry):
        body(index)
        return carry

    lax.fori_loop(0, count, step, 0, unroll=unroll)


def rows_at(start, count, multiple=8):
    return pl.ds(pl.multiple_of(start, multiple), count)


def lanes_of(block):
    return slice(block * LANES, (block + 1) * LANES)


def fold_rows(values):
    count, lanes = values.shape
    return jnp.sum(values.reshape(count // 8, 8, lanes), 0)


def fill_mask(side, mask_ref, images):
    mask_ref[SLOT * images :, :] = jnp.zeros_like(mask_ref[SLOT * images :, :])

    def body(slot):
        row = slot // GRID
        col = slot - row * GRID
        inside = (slot == CELLS) | ((row < side) & (col < side))
        level = jnp.where(inside, 1.0, 0.0).astype(F32)
        mask_ref[rows_at(slot * images, images), :] = jnp.full((images, LANES), level, F32)

    loop(SLOT, body, unroll=2)


def spread(rows_ref, blocks_ref, blocks):
    total = rows_ref.shape[0]

    def body(step):
        at = rows_at(step * 48, 48, 16)
        values = rows_ref[at, :].astype(F32)
        for block in range(blocks):
            blocks_ref[block, at, :] = values[:, lanes_of(block)]

    loop(total // 48, body)


def unspread(blocks_ref, rows_ref, blocks):
    total = rows_ref.shape[0]

    def body(step):
        at = rows_at(step * 48, 48, 16)
        values = [blocks_ref[block, at, :] for block in range(blocks)]
        rows_ref[at, :] = jnp.concatenate(values, 1).astype(BF16)

    loop(total // 48, body)


def natural_slot(slot):
    return jnp.where(slot == CELLS, 0, slot + 1)


def fill_table(vectors, table_ref):
    for row, ref in enumerate(vectors):
        table_ref[row : row + 1, :] = ref[...].astype(F32).reshape(1, -1)


def fill_taps(table, taps_ref, count, blocks):
    for tap in range(count):
        for block in range(blocks):
            taps_ref[block, tap] = jnp.broadcast_to(table[tap : tap + 1, lanes_of(block)], (8, LANES))


def centred(size):
    inset = (7 - size) // 2
    return [(a + inset) * 7 + b + inset for a in range(size) for b in range(size)]


def lane_picker(width, offset, channels):
    lane = lax.broadcasted_iota(jnp.int32, (width, channels), 0)
    channel = lax.broadcasted_iota(jnp.int32, (width, channels), 1)
    return jnp.where(channel == lane + offset, 1.0, 0.0).astype(BF16)


def assemble_taps(kernels, work_ref, table_ref):
    channels = table_ref.shape[1]
    table_ref[...] = jnp.zeros_like(table_ref)
    offset = 0
    for size, kernel_ref in zip((3, 5, 7), kernels):
        width = kernel_ref.shape[1]
        work_ref[0 : size * size, :] = dot(kernel_ref[...], lane_picker(width, offset, channels))
        for tap, place in enumerate(centred(size)):
            table_ref[place : place + 1, :] += work_ref[tap : tap + 1, :]
        offset += width


def correlate(source_ref, taps_ref, size, span, images, block, sub, emit, turned=False, beside=()):
    margin, inset = size // 2, (span - size) // 2
    beside = iter(beside)

    def load(cell):
        return source_ref[block, rows_at(cell * images + sub * 8, 8), :]

    for row in range(GRID):
        totals = [None] * GRID
        for a in range(size):
            from_row = row + a - margin
            if not 0 <= from_row < GRID:
                continue
            cells = [load(from_row * GRID + col) for col in range(GRID)]
            for b in range(size):
                tap = (a + inset) * span + b + inset
                weight = taps_ref[block, span * span - 1 - tap if turned else tap]
                for col in range(GRID):
                    from_col = col + b - margin
                    if 0 <= from_col < GRID:
                        term = cells[from_col] * weight
                        totals[col] = term if totals[col] is None else totals[col] + term
        for col in range(GRID):
            emit(row * GRID + col, totals[col])
        next(beside, None)
        next(beside, None)
    for _ in beside:
        pass


def tap_sums(grad_ref, source_ref, sums_ref, size, span, images, block, sub):
    margin, inset = size // 2, (span - size) // 2

    def load(ref, cell):
        return ref[block, rows_at(cell * images + sub * 8, 8), :]

    for a in range(size):
        totals = [None] * size
        for row in range(GRID):
            from_row = row + a - margin
            if not 0 <= from_row < GRID:
                continue
            grads = [load(grad_ref, row * GRID + col) for col in range(GRID)]
            cells = [load(source_ref, from_row * GRID + col) for col in range(GRID)]
            for b in range(size):
                part = None
                for col in range(GRID):
                    from_col = col + b - margin
                    if 0 <= from_col < GRID:
                        term = grads[col] * cells[from_col]
                        part = term if part is None else part + term
                totals[b] = part if totals[b] is None else totals[b] + part
        for b in range(size):
            tap = (a + inset) * span + b + inset
            sums_ref[block, tap] += totals[b]


def by_block(images, body, before=None, beside=None):
    subs = images // 8
    first = 0
    while first < len(KERNEL_SIZES):
        size = KERNEL_SIZES[first]
        count = 1
        while first + count < len(KERNEL_SIZES) and KERNEL_SIZES[first + count] == size:
            count += 1
        for block in range(first, first + count):
            if before is not None:
                before(block)
        last = beside is not None and first + count == len(KERNEL_SIZES)
        share = images // (count * subs)

        def step(index, first=first, size=size, last=last, share=share):
            if last:
                work = (part for one in range(share) for part in beside(index * share + one))
                body(size, first + index // subs, index % subs, work)
            else:
                body(size, first + index // subs, index % subs)

        loop(count * subs, step)
        first += count


def row_sums(value):
    high = value.astype(BF16)
    low = (value - high.astype(F32)).astype(BF16)
    return dot(jnp.concatenate([high, low], 1), jnp.ones((2 * LANES, LANES), BF16))


def row_means(blocks):
    return row_sums(sum(blocks[1:], blocks[0])) * (1.0 / (len(blocks) * LANES))


def norm_parts(blocks):
    mean = row_means(blocks)
    centered = [value - mean for value in blocks]
    inverse = lax.rsqrt(row_means([value * value for value in centered]) + EPSILON)
    return [value * inverse for value in centered], inverse


def norm_forward(source_ref, table_ref, gain_row, shift_row, normed_ref, turned_ref, parts_ref, inverse_ref, keep=None):
    blocks = source_ref.shape[0]
    gains = table_ref[gain_row : gain_row + 1, :]
    shifts = table_ref[shift_row : shift_row + 1, :]

    def body(step):
        at = rows_at(step * BAND, BAND, BAND)
        source = [source_ref[block, at, :] for block in range(blocks)]
        if keep is not None:
            keep(at, source)
        parts, inverse = norm_parts(source)
        inverse_ref[at, :] = inverse
        for block in range(blocks):
            parts_ref[block, at, :] = parts[block]
        out = [
            parts[block] * gains[:, lanes_of(block)] + shifts[:, lanes_of(block)]
            for block in range(blocks)
        ]
        normed_ref[at, :] = jnp.concatenate(out, 1).astype(BF16)

    loop(source_ref.shape[1] // BAND, body, unroll=2)
    transpose_rows(normed_ref, turned_ref)


def transpose_rows(rows_ref, turned_ref):
    width = rows_ref.shape[1]

    def body(step):
        at = rows_at(step * TILE, TILE, TILE)
        turned_ref[0:width, at] = rows_ref[at, :].T

    loop(rows_ref.shape[0] // TILE, body)


def norm_backward(parts_ref, inverse_ref, grad_at, direct_at, table_ref, gain_row, emit, blocks, total):
    gains = table_ref[gain_row : gain_row + 1, :]

    def body(step, sums):
        at = rows_at(step * BAND, BAND, BAND)
        parts, inverse = [parts_ref[block, at, :] for block in range(blocks)], inverse_ref[at, :]
        grads = [grad_at(block, at) for block in range(blocks)]
        scaled = [grads[block] * gains[:, lanes_of(block)] for block in range(blocks)]
        product = [grads[block] * parts[block] for block in range(blocks)]
        crossed = [product[block] * gains[:, lanes_of(block)] for block in range(blocks)]
        mean, cross = row_means(scaled), row_means(crossed)
        out = [
            direct_at(block, at) + inverse * (scaled[block] - mean - parts[block] * cross)
            for block in range(blocks)
        ]
        emit(at, out)
        gain_sums = [sums[0][block] + fold_rows(product[block]) for block in range(blocks)]
        shift_sums = [sums[1][block] + fold_rows(grads[block]) for block in range(blocks)]
        return (gain_sums, shift_sums)

    zero = [jnp.zeros((8, LANES), F32) for _ in range(blocks)]
    return lax.fori_loop(0, total // BAND, body, (zero, zero), unroll=2)


def total_row(parts):
    return jnp.concatenate([jnp.sum(part, 0, keepdims=True) for part in parts], 1)


def head_mask():
    row = lax.broadcasted_iota(jnp.int32, (LANES, LANES), 0)
    col = lax.broadcasted_iota(jnp.int32, (LANES, LANES), 1)
    size = LANES // 2
    return jnp.where((row < size) == (col < size), size ** (-0.5), 0.0).astype(F32)


def pack_kernel(bias_ref, fc1_ref, fc2_ref, packed_ref):
    channels = fc1_ref.shape[0]
    packed_ref[0:channels, :] = fc1_ref[...]
    packed_ref[channels : 2 * channels, :] = fc2_ref[...]
    rest = packed_ref.at[2 * channels :, :]
    rest[...] = jnp.broadcast_to(bias_ref[...].reshape(1, -1), rest.shape)


def front_kernel(
    side_ref, tokens_ref, cpe_ref, small_ref, middle_ref, large_ref, qkv_ref, proj_ref,
    cpe_bias_ref, gain_ref, shift_ref, query_bias_ref, value_bias_ref, crpe_bias_ref, proj_bias_ref,
    crpe_ref, mask_out, input_out, parts_out, inverse_out, query_out, weight_out, value_out, convolved_out, normed_t_out, context_out, attended_t_out, second_out,
    input_ref, inverse_ref, query_ref, weight_ref, value_ref, convolved_ref, normed_t_ref, context_ref, attended_t_ref,
    second_ref, position_ref, mask_ref, work_ref, normed_ref, cpe_taps_ref, crpe_taps_ref, crpe_work_ref, table_ref, sems,
):
    fill_table(
        (cpe_bias_ref, gain_ref, shift_ref, query_bias_ref, value_bias_ref, crpe_bias_ref, proj_bias_ref), table_ref
    )
    out = Copies(sems)
    rows, channels = tokens_ref.shape
    blocks = channels // LANES
    images = rows // SLOT
    padded = normed_ref.shape[0]
    held = SLOT_PAD * images
    fill_mask(side_ref[0], mask_ref, images)
    assemble_taps((small_ref, middle_ref, large_ref), crpe_work_ref, crpe_ref)
    fill_taps(cpe_ref[...].astype(F32), cpe_taps_ref, 9, blocks)
    fill_taps(crpe_ref, crpe_taps_ref, 49, blocks)
    spread(tokens_ref, work_ref, blocks)

    def arrange(slot):
        at = rows_at(slot * images, images)
        mask = mask_ref[at, :]
        for block in range(blocks):
            values = work_ref[block, pl.ds(natural_slot(slot), images, stride=SLOT), :]
            input_ref[block, at, :] = values * mask

    out.start(mask_ref, mask_out)
    loop(SLOT, arrange, unroll=2)
    for ref in (input_ref, position_ref, convolved_ref):
        ref[:, rows:padded, :] = jnp.zeros((blocks, padded - rows, LANES), F32)
    position_ref[:, CELLS * images : rows, :] = input_ref[:, CELLS * images : rows, :]
    convolved_ref[:, CELLS * images : rows, :] = jnp.zeros((blocks, images, LANES), F32)

    subs = images // 8

    def position(index):
        block, sub = index // subs, index % subs
        bias = table_row(table_ref, CPE_B, block)

        def emit(cell, total):
            at = rows_at(cell * images + sub * 8, 8)
            position_ref[block, at, :] = input_ref[block, at, :] + mask_ref[at, :] * (total + bias)

        correlate(input_ref, cpe_taps_ref, 3, 3, images, block, sub, emit)

    loop(blocks * subs, position)
    out.start(input_ref, input_out)
    norm_forward(
        position_ref, table_ref, GAIN1, SHIFT1, normed_ref, normed_t_ref, second_ref, inverse_ref
    )
    sent_parts = out.start(second_ref, parts_out)
    out.start(inverse_ref, inverse_out)
    normed_t_ref[channels:, :] = jnp.ones_like(normed_t_ref[channels:, :])
    out.start(normed_t_ref, normed_t_out)

    def project(step):
        at = rows_at(step * TILE, TILE, TILE)
        normed = normed_ref[at, :]
        mask = mask_ref[at, :]
        query = dot(normed, qkv_ref[:, :channels]) + table_ref[QUERY_B : QUERY_B + 1, :]
        for block in range(blocks):
            query_ref[block, at, :] = query[:, lanes_of(block)]
        key = dot(normed, qkv_ref[:, channels : 2 * channels])
        for block in range(blocks):
            weight_ref[block, at, :] = key[:, lanes_of(block)]
        value = dot(normed, qkv_ref[:, 2 * channels :]) + table_ref[VALUE_B : VALUE_B + 1, :]
        for block in range(blocks):
            value_ref[block, at, :] = value[:, lanes_of(block)] * mask

    loop(padded // TILE, project)
    for ref in (query_ref, value_ref):
        ref[:, padded:held, :] = jnp.zeros((blocks, held - padded, LANES), F32)
    weight_ref[:, rows:held, :] = jnp.zeros((blocks, held - rows, LANES), F32)
    out.start(query_ref, query_out)
    out.start(value_ref, value_out)

    def soften(index):
        block, sub = index // subs, index % subs
        top = None
        for slot in range(SLOT):
            at = rows_at(slot * images + sub * 8, 8)
            key = jnp.where(mask_ref[at, :] > 0, weight_ref[block, at, :], -1e30)
            top = key if top is None else jnp.maximum(top, key)
        total = None
        for slot in range(SLOT):
            at = rows_at(slot * images + sub * 8, 8)
            mask = mask_ref[at, :]
            key = jnp.where(mask > 0, weight_ref[block, at, :], -1e30)
            level = jnp.exp(key - top) * mask
            weight_ref[block, at, :] = level
            total = level if total is None else total + level
        inverse = 1.0 / total
        for slot in range(SLOT):
            at = rows_at(slot * images + sub * 8, 8)
            weight_ref[block, at, :] = weight_ref[block, at, :] * inverse

    loop(blocks * subs, soften)
    out.start(weight_ref, weight_out)
    heads = head_mask()

    def attend(image):
        at = pl.ds(image, SLOT_PAD, stride=images)
        for block in range(blocks):
            weight = weight_ref[block, at, :].astype(BF16)
            value = value_ref[block, at, :].astype(BF16)
            query = query_ref[block, at, :].astype(BF16)
            context = (dot_tn(weight, value) * heads).astype(BF16)
            context_ref[image, block] = context
            work_ref[block, at, :] = dot(query, context)
            yield

    def convolve(size, block, sub, beside=()):
        bias = table_row(table_ref, CRPE_B, block)

        def emit(cell, total):
            convolved_ref[block, rows_at(cell * images + sub * 8, 8), :] = total + bias

        correlate(value_ref, crpe_taps_ref, size, 7, images, block, sub, emit, beside=beside)

    by_block(images, convolve, beside=attend)
    out.start(convolved_ref, convolved_out)
    out.start(context_ref, context_out)
    out.wait(sent_parts)

    def finish(step):
        at = rows_at(step * TILE, TILE, TILE)
        attended = jnp.concatenate(
            [
                work_ref[block, at, :] + query_ref[block, at, :] * convolved_ref[block, at, :]
                for block in range(blocks)
            ],
            1,
        ).astype(BF16)
        attended_t_ref[:, at] = attended.T
        branch = dot(attended, proj_ref[...]) + table_ref[PROJ_B : PROJ_B + 1, :]
        for block in range(blocks):
            second_ref[block, at, :] = position_ref[block, at, :] + branch[:, lanes_of(block)]

    half = padded // TILE // 2
    loop(half, finish)
    part = slice(0, half * TILE)
    out.start(second_ref.at[:, part], second_out.at[:, part])
    loop(padded // TILE - half, lambda step: finish(step + half))
    part = slice(half * TILE, padded)
    out.start(second_ref.at[:, part], second_out.at[:, part])
    out.start(attended_t_ref, attended_t_out)
    out.finish()


def table_row(table_ref, row, block):
    return table_ref[row : row + 1, pl.ds(pl.multiple_of(block * LANES, LANES), LANES)]


def gelu_parts(value):
    level = 0.5 + 0.5 * lax.erf(value * math.sqrt(0.5))
    return level, jnp.exp2(value * value * (-0.5 / math.log(2.0)) - 0.5 * math.log2(2.0 * math.pi))


def cotangent_kernel(cot_ref, mask_ref, cot_rows_out, cot_t_out, sums_ref, cot_rows_ref, cot_t_ref, work_ref, sems):
    copies = Copies(sems)
    rows, channels = cot_ref.shape
    blocks = channels // LANES
    images = rows // SLOT
    padded = cot_rows_ref.shape[0]
    spread(cot_ref, work_ref, blocks)
    cot_rows_ref[rows:padded, :] = jnp.zeros((padded - rows, channels), BF16)

    def arrange(step, sums):
        at = rows_at(step * (2 * images), 2 * images, 16)
        mask = mask_ref[at, :]
        parts = []
        for block in range(blocks):
            pair = [
                work_ref[block, pl.ds(natural_slot(2 * step + one), images, stride=SLOT), :]
                for one in range(2)
            ]
            parts.append(jnp.concatenate(pair, 0) * mask)
        cot_rows_ref[at, :] = jnp.concatenate(parts, 1).astype(BF16)
        return [sums[block] + fold_rows(parts[block]) for block in range(blocks)]

    zero = [jnp.zeros((8, LANES), F32) for _ in range(blocks)]
    sums_ref[...] = jnp.concatenate(lax.fori_loop(0, SLOT // 2, arrange, zero), 1)
    copies.start(cot_rows_ref, cot_rows_out)
    transpose_rows(cot_rows_ref, cot_t_ref)
    copies.start(cot_t_ref, cot_t_out)
    copies.finish()


def mlp_kernel(
    side_ref, bias_sums_ref, cot_rows_in, cot_t_in, second_in, fc_in, gain_ref, shift_ref, fc2_bias_ref,
    result_out, grad_out, grad_fc_keep, grad_fc_send, small_ref,
    second_ref, fc_ref, grad_ref, grad_fc_ref,
    cot_rows_ref, cot_t_ref, normed_ref, normed_t_ref, hidden_ref, pre_ref, hidden_two_ref, pre_two_ref, mlp_ref, back_ref,
    table_ref, result_ref, inverse_ref, sems,
):
    fill_table((gain_ref, shift_ref, fc2_bias_ref), table_ref)
    copies = Copies(sems)
    got_second = copies.start(second_in, second_ref)
    got_fc = copies.start(fc_in, fc_ref)
    got_cot = [copies.start(cot_rows_in, cot_rows_ref), copies.start(cot_t_in, cot_t_ref)]
    padded, channels = cot_rows_ref.shape
    blocks = channels // LANES
    owners, _, units = fc_ref.shape
    mine, half_x, half_z = side_ref[1], side_ref[2] & 1, (side_ref[2] >> 1) & 1
    got_second.wait()
    fc2_bias = table_ref[FC2_B : FC2_B + 1, :]

    def keep(at, second):
        for block in range(blocks):
            mlp_ref[at, lanes_of(block)] = second[block] + fc2_bias[:, lanes_of(block)]

    norm_forward(
        second_ref, table_ref, GAIN2, SHIFT2, normed_ref, normed_t_ref, second_ref, inverse_ref, keep
    )
    normed_t_ref[channels:, :] = jnp.ones_like(normed_t_ref[channels:, :])
    got_fc.wait()
    for copy in got_cot:
        copy.wait()

    tiles = padded // MLP_TILE

    def weights(slot, held, which, end):
        left_ref, right_ref = (normed_t_ref, held[1]) if which == 0 else (cot_t_ref, held[0])
        last = left_ref.shape[0] if end else PIECE
        grad = dot(left_ref[end * PIECE : last, :], right_ref[...]).astype(BF16)
        place = ((half_x ^ which) << 1) | (half_z ^ end)
        grad_fc_ref[slot, place, 0:PIECE, :] = grad[0:PIECE]
        if last > channels:
            grad_fc_ref[slot, (half_x << 1) | half_z, PIECE:, :] = grad[PIECE:]

    def part(slot, held, before):
        owner = mine ^ ((slot >> 1) | ((slot & 1) << 1))
        hidden_ref, pre_ref = held
        for step in range(tiles):
            at = slice(step * MLP_TILE, (step + 1) * MLP_TILE)
            first = fc_ref[owner, 0:channels, :]
            second = fc_ref[owner, channels : 2 * channels, :]
            bias = fc_ref[owner, 2 * channels :, :].astype(F32)[0:1]
            values, grads = dot(normed_ref[at, :], first) + bias, dot_nt(cot_rows_ref[at, :], second)
            if before is not None and step < 4:
                weights(slot - 1, before, step // 2, step % 2)
            level, density = gelu_parts(values)
            hidden = (values * level).astype(BF16)
            pre = (grads * (level + values * density)).astype(BF16)
            hidden_ref[at, :] = hidden
            pre_ref[at, :] = pre
            mlp, back = dot(hidden, second), dot_nt(pre, first)
            if slot == 0:
                back_ref[at, :] = back
            else:
                back_ref[at, :] += back
            if slot < owners - 1:
                mlp_ref[at, :] += mlp
            else:
                result_ref[at, :] = (mlp_ref[at, :] + mlp).astype(BF16)

    held = (hidden_ref, pre_ref), (hidden_two_ref, pre_two_ref)
    targets = [(grad_fc_keep if slot < owners // 2 else grad_fc_send).at[slot % (owners // 2)] for slot in range(owners)]
    for slot in range(owners + 1):
        if slot < owners:
            part(slot, held[slot % 2], held[(slot - 1) % 2] if slot else None)
        else:
            for step in range(4):
                weights(owners - 1, held[(owners - 1) % 2], step // 2, step % 2)
        if slot:
            copies.start(grad_fc_ref.at[slot - 1], targets[slot - 1])

    def grad_at(block, at):
        return back_ref[at, lanes_of(block)]

    def direct_at(block, at):
        return cot_rows_ref[at, lanes_of(block)].astype(F32)

    def emit(at, out):
        for block in range(blocks):
            grad_ref[block, at, :] = out[block]

    gain_sums, shift_sums = norm_backward(
        second_ref, inverse_ref, grad_at, direct_at, table_ref, GAIN2, emit, blocks, padded
    )
    copies.start(grad_ref, grad_out)
    copies.start(result_ref, result_out)
    small_ref[...] = jnp.zeros_like(small_ref)
    small_ref[0:1, :] = total_row(gain_sums)
    small_ref[1:2, :] = total_row(shift_sums)
    small_ref[2:3, :] = jnp.sum(bias_sums_ref[...], 0, keepdims=True)
    for copy in copies.open[4:]:
        copy.wait()


def result_kernel(result_ref, mask_ref, out_ref, work_ref):
    rows, channels = out_ref.shape
    blocks = channels // LANES
    images = rows // SLOT

    def arrange(step):
        at = rows_at(step * (2 * images), 2 * images, 16)
        values = result_ref[at, :].astype(F32)
        mask = mask_ref[at, :]
        for block in range(blocks):
            masked = values[:, lanes_of(block)] * mask
            for one in range(2):
                to = pl.ds(natural_slot(2 * step + one), images, stride=SLOT)
                work_ref[block, to, :] = masked[one * images : (one + 1) * images]

    loop(SLOT // 2, arrange)
    unspread(work_ref, out_ref, blocks)


def branch_kernel(
    proj_ref, grad_in, attended_t_in,
    back_out, grad_proj_ref, small_ref,
    grad_ref, attended_t_ref, back_ref, branch_ref, sems,
):
    copies = Copies(sems)
    padded, channels = branch_ref.shape
    blocks = channels // LANES
    held = back_ref.shape[1]
    half = padded // 2
    halves = slice(0, half), slice(half, padded)
    got = [copies.start(grad_in.at[:, part], grad_ref.at[:, part]) for part in halves]
    got_attended = copies.start(attended_t_in, attended_t_ref)
    back_ref[:, padded:held, :] = jnp.zeros((blocks, held - padded, LANES), F32)
    sent = [copies.start(back_ref.at[:, padded:held], back_out.at[:, padded:held])]

    total = jnp.zeros((8, channels), F32)
    step = half // 2
    for end, part in enumerate(halves):
        got[end].wait()
        for first in range(end * half, (end + 1) * half, step):
            at = slice(first, first + step)
            low = jnp.concatenate([grad_ref[block, at, :] for block in range(blocks)], 1).astype(BF16)
            branch_ref[at, :] = low
            total += fold_rows(low.astype(F32))
            back = dot_nt(low, proj_ref[...])
            for block in range(blocks):
                back_ref[block, at, :] = back[:, lanes_of(block)]
        sent.append(copies.start(back_ref.at[:, part], back_out.at[:, part]))
    got_attended.wait()
    grad_proj_ref[...] = dot(attended_t_ref[...], branch_ref[...]).astype(BF16)
    small_ref[...] = total
    for copy in sent:
        copy.wait()


def mix_kernel(
    side_ref, small_mlp_ref, small_branch_ref, crpe_ref, grad_proj_ref,
    back_in, query_in, weight_in, value_in, convolved_in, normed_t_in, context_in, mask_in,
    keep_ref, send_ref, projected_out,
    total_ref, back_ref, query_ref, weight_ref, value_ref, convolved_ref, normed_t_ref, context_ref, projected_ref,
    mask_ref, small_ref, edge_ref, turned_ref, crpe_taps_ref, sems,
):
    copies = Copies(sems)
    pairs = (back_in, back_ref), (query_in, query_ref), (convolved_in, convolved_ref)
    first = [
        [copies.start(source.at[block], target.at[block]) for source, target in pairs] for block in range(back_ref.shape[0])
    ]
    pairs = (weight_in, weight_ref), (value_in, value_ref), (context_in, context_ref), (mask_in, mask_ref)
    pairs += ((normed_t_in, normed_t_ref),)
    then = [copies.start(*pair) for pair in pairs]
    blocks, padded, _ = edge_ref.shape
    channels = blocks * LANES
    held = query_ref.shape[1]
    images = held // SLOT_PAD
    rows = images * SLOT
    subs = images // 8
    fill_taps(crpe_ref, crpe_taps_ref, 49, blocks)
    turned_ref[:, CELLS * images :, :] = jnp.zeros((blocks, padded - CELLS * images, LANES), F32)
    bias_sums = []

    def arrived(block):
        for copy in first[block]:
            copy.wait()

        def edges(step, total):
            at = rows_at(step * (9 * images), 9 * images)
            back = back_ref[block, at, :]
            edge = back * query_ref[block, at, :]
            edge_ref[block, at, :] = edge
            convolved_ref[block, at, :] = back * convolved_ref[block, at, :]
            return total + fold_rows(edge)

        bias_sums.append(lax.fori_loop(0, CELLS // 9, edges, jnp.zeros((8, LANES), F32)))

    def convolve(size, block, sub):
        def emit(cell, total):
            turned_ref[block, rows_at(cell * images + sub * 8, 8), :] = total

        correlate(edge_ref, crpe_taps_ref, size, 7, images, block, sub, emit, turned=True)

    by_block(images, convolve, arrived)
    for copy in then:
        copy.wait()
    heads = head_mask()

    def attend(image):
        at = pl.ds(image, SLOT_PAD, stride=images)
        for block in range(blocks):
            weight = weight_ref[block, at, :]
            low = weight.astype(BF16)
            value = value_ref[block, at, :].astype(BF16)
            query = query_ref[block, at, :].astype(BF16)
            back = back_ref[block, at, :].astype(BF16)
            context = context_ref[image, block]
            grad = (dot_tn(query, back) * heads).astype(BF16)
            query_ref[block, at, :] = dot_nt(back, context)
            key = dot_nt(value, grad)
            back_ref[block, at, :] = weight * (key - jnp.sum(weight * key, 0, keepdims=True))
            value_ref[block, at, :] = dot(low, grad)

    loop(images, attend, unroll=4)
    projected_ref[rows:padded, :] = jnp.zeros((padded - rows, 3 * channels), BF16)

    def gather(step):
        at = rows_at(step * (2 * images), 2 * images, 16)
        mask = mask_ref[at, :]
        parts = [[], [], []]
        for block in range(blocks):
            parts[0].append(query_ref[block, at, :] + convolved_ref[block, at, :])
            parts[1].append(back_ref[block, at, :])
            parts[2].append((value_ref[block, at, :] + turned_ref[block, at, :]) * mask)
        for which in range(3):
            cols = slice(which * channels, (which + 1) * channels)
            projected_ref[at, cols] = jnp.concatenate(parts[which], 1).astype(BF16)

    loop(SLOT // 2, gather)
    sent = copies.start(projected_ref, projected_out)
    small_ref[...] = jnp.zeros_like(small_ref)
    index = ((side_ref[1] & 1) << 2) | ((side_ref[2] & 1) << 1) | (side_ref[1] >> 1)

    def place(matrix, grad):
        for end in range(channels // PIECE):
            piece = matrix * (channels // PIECE) + end
            total_ref[piece ^ index, 0:PIECE, :] = grad[end * PIECE : (end + 1) * PIECE]

    for which in range(3):
        cols = slice(which * channels, (which + 1) * channels)
        grad = dot(normed_t_ref[...], projected_ref[:, cols])
        place(which, grad[0:channels].astype(BF16))
        small_ref[56 + which : 57 + which, :] = grad[channels : channels + 1]
    place(3, grad_proj_ref[...])
    small_ref[49:50, :] = total_row(bias_sums)
    small_ref[50:51, :] = jnp.sum(small_branch_ref[...], 0, keepdims=True)
    small_ref[64:72, :] = small_mlp_ref[...]
    for piece in range(total_ref.shape[0]):
        total_ref[piece ^ index, PIECE:, :] = small_ref[piece * 16 : (piece + 1) * 16, :].astype(BF16)
    out = [copies.start(total_ref.at[4:8], send_ref), copies.start(total_ref.at[0:4], keep_ref)]
    for copy in [sent] + out:
        copy.wait()


def taps_kernel(
    back_in, query_in, value_in,
    small_ref,
    back_ref, query_ref, value_ref, sums_ref, sems,
):
    copies = Copies(sems)
    blocks, cells, _ = back_ref.shape
    images = cells // CELLS
    part = slice(0, cells)
    pairs = (back_in, back_ref), (query_in, query_ref), (value_in, value_ref)
    got = [
        [copies.start(source.at[block, part], target.at[block]) for source, target in pairs] for block in range(blocks)
    ]
    sums_ref[...] = jnp.zeros_like(sums_ref)

    def arrived(block):
        for copy in got[block]:
            copy.wait()

        def edges(step):
            at = rows_at(step * (9 * images), 9 * images)
            back_ref[block, at, :] = back_ref[block, at, :] * query_ref[block, at, :]

        loop(CELLS // 9, edges)

    def taps(size, block, sub):
        tap_sums(back_ref, value_ref, sums_ref, size, 7, images, block, sub)

    by_block(images, taps, arrived)
    small_ref[...] = jnp.zeros_like(small_ref)
    for block in range(blocks):
        small_ref[0:49, lanes_of(block)] = jnp.sum(sums_ref[block], 1)


def norm_half(
    copies, first, base, operands, grad_out, projected_ref, parts_ref, inverse_ref, grad_ref, normed_ref, table_ref
):
    qkv_ref, gain_ref, projected_in, parts_in, inverse_in, grad_in = operands
    fill_table((gain_ref,), table_ref)
    padded, channels = normed_ref.shape
    blocks = channels // LANES
    half = padded // 2
    got_halves = [
        copies.start(projected_in.at[pl.ds(first + end * half, half)], projected_ref.at[pl.ds(end * half, half)])
        for end in range(2)
    ]
    source, target = pl.ds(first, padded), pl.ds(base, padded)
    got = [
        copies.start(parts_in.at[:, source], parts_ref),
        copies.start(inverse_in.at[source], inverse_ref),
        copies.start(grad_in.at[:, source], grad_ref.at[:, target]),
    ]

    for end in range(2):
        got_halves[end].wait()
        at = slice(end * half, (end + 1) * half)
        normed_ref[at, :] = dot_nt(projected_ref[at, :], qkv_ref[...])
    for copy in got:
        copy.wait()

    def grad_at(block, at):
        return normed_ref[at, lanes_of(block)]

    def moved(at):
        return rows_at(base + at.start, at.size, BAND)

    def direct_at(block, at):
        return grad_ref[block, moved(at), :]

    def emit_norm(at, out):
        for block in range(blocks):
            grad_ref[block, moved(at), :] = out[block]

    sums = norm_backward(parts_ref, inverse_ref, grad_at, direct_at, table_ref, 0, emit_norm, blocks, padded)
    return copies.start(grad_ref.at[:, target], grad_out), sums


def norm_first_kernel(
    qkv_ref, gain_ref, projected_in, parts_in, inverse_in, grad_in,
    grad_out, small_ref,
    projected_ref, parts_ref, inverse_ref, grad_ref, normed_ref, table_ref, sems,
):
    operands = qkv_ref, gain_ref, projected_in, parts_in, inverse_in, grad_in
    sent, (gain_sums, shift_sums) = norm_half(
        Copies(sems), 0, 0, operands, grad_out, projected_ref, parts_ref, inverse_ref, grad_ref, normed_ref,
        table_ref,
    )
    small_ref[...] = jnp.zeros_like(small_ref)
    small_ref[0:1, :] = total_row(gain_sums)
    small_ref[1:2, :] = total_row(shift_sums)
    sent.wait()


def norm_last_kernel(
    first, qkv_ref, gain_ref, projected_in, parts_in, inverse_in, grad_in, grad_first_in, input_in, small_first_ref,
    small_taps_ref,
    grad_out, small_ref,
    projected_ref, parts_ref, inverse_ref, grad_ref, normed_ref, table_ref, input_ref, sums_ref, work_ref, sems,
):
    copies = Copies(sems)
    blocks, cells, _ = input_ref.shape
    images = cells // CELLS
    subs = images // 8
    got = copies.start(grad_first_in, grad_ref.at[:, 0:first]), copies.start(input_in.at[:, 0:cells], input_ref)
    operands = qkv_ref, gain_ref, projected_in, parts_in, inverse_in, grad_in
    sent, (gain_sums, shift_sums) = norm_half(
        copies, first, first, operands, grad_out, projected_ref, parts_ref, inverse_ref, grad_ref, normed_ref,
        table_ref,
    )
    sums_ref[...] = jnp.zeros_like(sums_ref)
    work_ref[...] = jnp.zeros_like(work_ref)
    work_ref[0:56, :] = small_taps_ref[...]
    work_ref[57:58, :] = total_row(gain_sums) + small_first_ref[0:1, :]
    work_ref[58:59, :] = total_row(shift_sums) + small_first_ref[1:2, :]
    for copy in got:
        copy.wait()

    def colsum(step, sums):
        at = rows_at(step * (9 * images), 9 * images)
        return [sums[block] + fold_rows(grad_ref[block, at, :]) for block in range(blocks)]

    zero = [jnp.zeros((8, LANES), F32) for _ in range(blocks)]
    work_ref[56:57, :] = total_row(lax.fori_loop(0, GRID, colsum, zero))

    def taps(index):
        tap_sums(grad_ref, input_ref, sums_ref, 3, 3, images, index // subs, index % subs)

    loop(blocks * subs, taps)
    for block in range(blocks):
        work_ref[64:73, lanes_of(block)] = jnp.sum(sums_ref[block], 1)
    small_ref[...] = work_ref[...].astype(BF16)
    sent.wait()


def back_kernel(
    mask_ref, cpe_ref, first_in, second_in,
    tokens_ref,
    grad_ref, work_ref, result_ref, taps_ref, sems,
):
    copies = Copies(sems)
    half = first_in.shape[1]
    got = copies.start(first_in, grad_ref.at[:, 0:half]), copies.start(second_in, grad_ref.at[:, half : 2 * half])
    rows, channels = tokens_ref.shape
    blocks = channels // LANES
    images = rows // SLOT
    subs = images // 8
    fill_taps(cpe_ref[...].astype(F32), taps_ref, 9, blocks)
    for copy in got:
        copy.wait()

    def convolve(index):
        block, sub = index // subs, index % subs

        def emit(cell, total):
            at = rows_at(cell * images + sub * 8, 8)
            result_ref[block, at, :] = (grad_ref[block, at, :] + total) * mask_ref[at, :]

        correlate(grad_ref, taps_ref, 3, 3, images, block, sub, emit, turned=True)

    loop(blocks * subs, convolve)
    result_ref[:, CELLS * images : rows, :] = grad_ref[:, CELLS * images : rows, :]

    def arrange(slot):
        at = rows_at(slot * images, images)
        for block in range(blocks):
            work_ref[block, pl.ds(natural_slot(slot), images, stride=SLOT), :] = result_ref[block, at, :]

    loop(SLOT, arrange, unroll=2)
    unspread(work_ref, tokens_ref, blocks)


def finish_fc_kernel(
    side_ref, first_ref, second_ref, third_ref, fourth_ref,
    fc1_ref, fc2_ref, bias_ref,
    held_ref,
):
    index = ((side_ref[2] & 1) << 1) | ((side_ref[2] >> 1) & 1)
    for place, piece in enumerate((first_ref, second_ref, third_ref, fourth_ref)):
        held_ref[place ^ index] = piece[...]
    for end in range(2):
        fc1_ref[end * PIECE : (end + 1) * PIECE, :] = held_ref[end, 0:PIECE, :].astype(F32)
        fc2_ref[:, end * PIECE : (end + 1) * PIECE] = held_ref[2 + end, 0:PIECE, :].astype(F32).T
    bias_ref[...] = held_ref[0, PIECE:, :].astype(F32)[0:1].reshape(bias_ref.shape)


def finish_small_kernel(
    own_ref, first_ref, second_ref, third_ref,
    cpe_ref, cpe_bias_ref, gain_ref, shift_ref, crpe_small_ref, crpe_middle_ref, crpe_large_ref,
    work_ref,
):
    terms = [ref[...].astype(F32) for ref in (own_ref, first_ref, second_ref, third_ref)]
    small = ((terms[0] + terms[1]) + (terms[2] + terms[3])).astype(BF16)
    work_ref[...] = small.astype(F32)
    cpe_ref[...] = work_ref[64:73, :]
    for row, ref in enumerate((cpe_bias_ref, gain_ref, shift_ref)):
        ref[...] = work_ref[56 + row : 57 + row, :].reshape(ref.shape)
    channels = small.shape[1]
    offset = 0
    for size, ref in zip((3, 5, 7), (crpe_small_ref, crpe_middle_ref, crpe_large_ref)):
        width = ref.shape[1]
        taps = dot_nt(small, lane_picker(width, offset, channels))
        for tap, place in enumerate(centred(size)):
            ref[tap : tap + 1, :] = taps[place : place + 1, :]
        offset += width


def finish_kernel(side_ref, *refs):
    pieces, (qkv_out, proj_out), rows = refs[:8], refs[8:10], refs[10:-5]
    held_ref, small_ref, qkv_ref, proj_ref, sems = refs[-5:]
    copies = Copies(sems)
    index = ((side_ref[1] & 1) << 2) | ((side_ref[2] & 1) << 1) | (side_ref[1] >> 1)
    for place, piece in enumerate(pieces):
        held_ref[place ^ index] = piece[...]
    channels = proj_ref.shape[1]
    for piece in range(8):
        matrix, end = piece // 2, piece % 2
        at = slice(end * PIECE, (end + 1) * PIECE)
        cols = slice(matrix * channels, (matrix + 1) * channels)
        values = held_ref[piece, 0:PIECE, :].astype(F32)
        if matrix < 3:
            qkv_ref[at, cols] = values
            copies.start(qkv_ref.at[at, cols], qkv_out.at[at, cols])
        else:
            proj_ref[at, :] = values
            copies.start(proj_ref.at[at], proj_out.at[at])
        small_ref[piece * 16 : (piece + 1) * 16, :] = held_ref[piece, PIECE:, :].astype(F32)
    for row, ref in zip(SMALL_ROWS, rows):
        ref[...] = small_ref[row : row + 1, :].reshape(ref.shape)
    copies.finish()


def add(*terms):
    return sum(term.astype(F32) for term in terms).astype(BF16)


def exchange(values, across_dp, across_blk):
    owners, parts = lax.axis_size("blk"), lax.axis_size("dp")
    flip = across_dp * owners + across_blk
    return lax.ppermute(values, ("dp", "blk"), [(at, at ^ flip) for at in range(parts * owners)])


def together(*values):
    return lax.optimization_barrier(values)


def shape(dims, dtype):
    return jax.ShapeDtypeStruct(dims, dtype)


def call(body, outs, scratch, cost, *operands):
    vmem, smem, hbm = (pl.BlockSpec(memory_space=space) for space in (pltpu.VMEM, pltpu.SMEM, pl.ANY))

    def place(value):
        return hbm if isinstance(value, Held) else smem if value.dtype == jnp.int32 else vmem

    def plain(values):
        return [value.array if isinstance(value, Held) else value for value in values]

    return pl.pallas_call(
        body,
        out_shape=plain(outs),
        in_specs=[place(value) for value in operands],
        out_specs=[place(value) for value in outs],
        scratch_shapes=[
            pltpu.SemaphoreType.DMA((item,)) if isinstance(item, int) else pltpu.VMEM(*item) for item in scratch
        ],
        compiler_params=pltpu.CompilerParams(vmem_limit_bytes=VMEM_BYTES),
        cost_estimate=pl.CostEstimate(flops=cost, bytes_accessed=cost // 1000, transcendentals=0),
    )(*plain(operands))


class Held:
    def __init__(self, array):
        self.array = array


def shards(
    tokens, sides, cpe_weight, cpe_bias, norm1_gain, norm1_shift, w_qkv, query_bias, value_bias,
    crpe_small, crpe_middle, crpe_large, crpe_bias, w_proj, proj_bias, norm2_gain, norm2_shift,
    w_fc1, fc1_bias, w_fc2, fc2_bias, cotangent,
):
    rows, channels = tokens.shape
    blocks = channels // LANES
    images = rows // SLOT
    padded = -(-rows // TILE) * TILE
    held = SLOT_PAD * images
    units = w_fc1.shape[1]
    owners = lax.axis_size("blk")

    (packed,) = call(
        pack_kernel, [shape((2 * channels + 16, units), BF16)], [], 1_000_000, fc1_bias, w_fc1, w_fc2
    )
    fc_all = lax.all_gather(packed, "blk", axis=0, tiled=False)
    scalars = jnp.stack([sides[0], lax.axis_index("blk"), lax.axis_index("dp")]).astype(jnp.int32)
    block_rows = (blocks, padded, LANES)
    block_held = (blocks, held, LANES)
    block_cells = (blocks, CELLS * images, LANES)
    contexts = (images, blocks, LANES, LANES), BF16
    front = [
        (block_rows, F32), (block_rows, F32), ((padded, LANES), F32), (block_held, F32), (block_held, F32), (block_held, F32),
        (block_rows, F32), ((channels + 16, padded), BF16), contexts, ((channels, padded), BF16), (block_rows, F32),
    ]
    crpe, mask, inputs, parts, inverse, query, weight, value, convolved, normed_t, context, attended_t, second = call(
        front_kernel,
        [shape((56, channels), F32), Held(shape((padded, LANES), F32))] + [Held(shape(*item)) for item in front],
        front[:1] + front[2:] + [
            (block_rows, F32), ((padded, LANES), F32), (block_held, F32), ((padded, channels), BF16),
            ((blocks, 9, 8, LANES), F32), ((blocks, 49, 8, LANES), F32), ((56, channels), F32), ((8, channels), F32), 13,
        ],
        40_000_000_000,
        scalars, tokens, cpe_weight, crpe_small, crpe_middle, crpe_large, w_qkv, w_proj,
        cpe_bias, norm1_gain, norm1_shift, query_bias, value_bias, crpe_bias, proj_bias,
    )
    pieces = (owners // 2, 4, PIECE + 16, units)
    cot_shapes = [((padded, channels), BF16), ((channels, padded), BF16)]
    cot_rows, cot_t, cot_sums = call(
        cotangent_kernel,
        [Held(shape(*item)) for item in cot_shapes] + [shape((8, channels), F32)],
        cot_shapes + [((blocks, rows, LANES), F32), 2],
        6_000_000_000,
        cotangent, mask,
    )
    result, grad_second, fc_keep, fc_send, small_mlp = call(
        mlp_kernel,
        [
            Held(shape((padded, channels), BF16)), Held(shape(block_rows, F32)), Held(shape(pieces, BF16)),
            Held(shape(pieces, BF16)),
            shape((8, channels), F32),
        ],
        [
            (block_rows, F32), (fc_all.shape, BF16), (block_rows, F32),
            ((owners, 4, PIECE + 16, units), BF16),
            ((padded, channels), BF16), ((channels, padded), BF16),
            ((padded, channels), BF16), ((channels + 16, padded), BF16),
            ((padded, units), BF16), ((padded, units), BF16), ((padded, units), BF16), ((padded, units), BF16),
            ((padded, channels), F32), ((padded, channels), F32), ((8, channels), F32), ((padded, channels), BF16), ((padded, LANES), F32), 6 + owners,
        ],
        60_000_000_000,
        scalars, cot_sums, Held(cot_rows), Held(cot_t), Held(second), Held(fc_all), norm2_gain, norm2_shift, fc2_bias,
    )
    fc_far = exchange(fc_send, 0, 1)
    back, grad_proj, small_branch = call(
        branch_kernel,
        [Held(shape(block_held, F32)), shape((channels, channels), BF16), shape((8, channels), F32)],
        [(block_rows, F32), ((channels, padded), BF16), (block_held, F32), ((padded, channels), BF16), 6],
        10_000_000_000,
        w_proj, Held(grad_second), Held(attended_t),
    )

    def half_of(side, end):
        part = slice(2 * end, 2 * end + 2)
        return add(fc_keep[side, part], fc_far[side, part])

    back, fc_y, fc_x, fc_yx, fc_own = together(back, half_of(1, 0), half_of(0, 1), half_of(1, 1), half_of(0, 0))
    fc_far = exchange(fc_y, 0, 2), exchange(fc_x, 1, 0), exchange(fc_yx, 1, 2)
    total_keep, total_send, projected = call(
        mix_kernel,
        [Held(shape((4, PIECE + 16, channels), BF16))] * 2 + [Held(shape((padded, 3 * channels), BF16))],
        [
            ((8, PIECE + 16, channels), BF16),
            (block_held, F32), (block_held, F32), (block_held, F32), (block_held, F32), (block_rows, F32),
            ((channels + 16, padded), BF16), contexts, ((padded, 3 * channels), BF16),
            ((padded, LANES), F32), ((128, channels), F32), (block_rows, F32), (block_rows, F32),
            ((blocks, 49, 8, LANES), F32), 8 + 3 * blocks,
        ],
        50_000_000_000,
        scalars, small_mlp, small_branch, crpe, grad_proj,
        Held(back), Held(query), Held(weight), Held(value), Held(convolved), Held(normed_t), Held(context),
        Held(mask),
    )
    projected, total_keep, total_send, *fc_far = together(projected, total_keep, total_send, *fc_far)
    total_far = exchange(total_send, 0, 1)
    bits = [1 << bit for bit in range(1, lax.axis_size("dp").bit_length() - 1)]
    fc_bits = [bit for bit in bits if bit > 2]

    def end_of(end):
        return add(fc_own[end], *(far[end] for far in fc_far))

    fc_other, fc_own = end_of(1), end_of(0)
    sums = [add(total_keep[piece], total_far[piece]) for piece in range(4)]
    projected, fc_own, fc_other, *sums = together(projected, fc_own, fc_other, *sums)
    fc_far = exchange(fc_other, 2, 0)
    total_far = exchange(sums[1], 0, 2), exchange(sums[2], 1, 0), exchange(sums[3], 1, 2)
    block_half = (blocks, padded // 2, LANES)
    norm_outs = [Held(shape(block_half, F32)), shape((8, channels), F32)]
    norm_scratch = [((padded // 2, 3 * channels), BF16), (block_half, F32), ((padded // 2, LANES), F32)]
    norm_more = [((padded // 2, channels), F32), ((8, channels), F32)]
    grad_first, small_first = call(
        norm_first_kernel, norm_outs, norm_scratch + [(block_half, F32)] + norm_more + [6], 8_000_000_000,
        w_qkv, norm1_gain, Held(projected), Held(parts), Held(inverse), Held(grad_second),
    )
    back, grad_first, fc_own, own = together(back, grad_first, add(fc_own, fc_far), add(sums[0], *total_far))
    total_far = exchange(own, bits[0], 0)
    fc_far = exchange(fc_own, fc_bits[0], 0)
    (small_taps,) = call(
        taps_kernel,
        [shape((56, channels), F32)],
        [(block_cells, F32), (block_cells, F32), (block_cells, F32), ((blocks, 49, 8, LANES), F32), 3 * blocks],
        15_000_000_000,
        Held(back), Held(query), Held(value),
    )
    fc_own = add(fc_own, fc_far)
    for bit in fc_bits[1:]:
        fc_own = add(fc_own, exchange(fc_own, bit, 0))
    projected, small_taps, fc_own, own = together(projected, small_taps, fc_own, add(own, total_far))
    total_far = exchange(own, bits[1], 0)
    fc_other, fc_third = exchange(fc_own, 2, 0), exchange(fc_own, 1, 0)
    grad_last, small_back = call(
        functools.partial(norm_last_kernel, padded // 2),
        [norm_outs[0], shape((80, channels), BF16)],
        norm_scratch + [(block_rows, F32)] + norm_more
        + [(block_cells, F32), ((blocks, 9, 8, LANES), F32), ((80, channels), F32), 8],
        12_000_000_000,
        w_qkv, norm1_gain, Held(projected), Held(parts), Held(inverse), Held(grad_second), Held(grad_first), Held(inputs),
        small_first, small_taps,
    )
    own = add(own, total_far)
    for bit in bits[2:]:
        own = add(own, exchange(own, bit, 0))
    grad_last, small_back, result, fc_other, fc_third, own = together(
        grad_last, small_back, result, fc_other, fc_third, own
    )
    near = [own, exchange(own, 0, 2), exchange(own, 1, 0), exchange(own, 1, 2)]
    small_far, fc_fourth = exchange(small_back, 0, 1), exchange(fc_other, 1, 0)
    (output,) = call(
        result_kernel, [shape((rows, channels), BF16)], [((blocks, rows, LANES), F32)], 1_000_000,
        result, mask,
    )
    output, small, small_far, fc_fourth = together(output, small_back, small_far, fc_fourth)
    small, grad_last = together(add(small, small_far), grad_last)
    small_far = exchange(small, 0, 2)
    (grad_tokens,) = call(
        back_kernel,
        [shape((rows, channels), BF16)],
        [
            (block_rows, F32), ((blocks, rows, LANES), F32),
            (block_rows, F32), ((blocks, 9, 8, LANES), F32), 2,
        ],
        1_000_000,
        mask, cpe_weight, Held(grad_first), Held(grad_last),
    )
    grad_tokens, small, small_far, *near = together(grad_tokens, small, small_far, *near)
    total_pieces = near + [exchange(piece, 0, 1) for piece in near]
    small = add(small, small_far)
    small_far = exchange(small, 1, 0)
    small, fc_own = together(small, fc_own)
    fc1, fc2, fc1_sums = call(
        finish_fc_kernel,
        [shape((channels, units), F32), shape((units, channels), F32), shape((units,), F32)],
        [((4, PIECE + 16, units), BF16)],
        1_000_000,
        scalars, fc_own, fc_other, fc_third, fc_fourth,
    )
    fc1, small, small_far, *total_pieces = together(fc1, small, small_far, *total_pieces)
    small = add(small, small_far)
    for bit in bits[2:]:
        small = add(small, exchange(small, bit, 0))
    small_far = [exchange(small, flip, 0) for flip in (bits[0], bits[1], bits[0] | bits[1])]
    row = shape((channels,), F32)
    grad_qkv, grad_proj, query_sums, value_sums, crpe_sums, proj_sums, gain_two, shift_two, fc2_sums = call(
        finish_kernel,
        [Held(shape((channels, 3 * channels), F32)), Held(shape((channels, channels), F32))] + [row] * len(SMALL_ROWS),
        [
            ((8, PIECE + 16, channels), BF16), ((128, channels), F32),
            ((channels, 3 * channels), F32), ((channels, channels), F32), 8,
        ],
        1_000_000,
        scalars, *total_pieces,
    )
    grad_qkv, small, *small_far = together(grad_qkv, small, *small_far)
    cpe, cpe_sums, gain_one, shift_one, taps_small, taps_middle, taps_large = call(
        finish_small_kernel,
        [
            shape(cpe_weight.shape, F32), row, row, row,
            shape(crpe_small.shape, F32), shape(crpe_middle.shape, F32), shape(crpe_large.shape, F32),
        ],
        [((80, channels), F32)],
        1_000_000,
        small, *small_far,
    )
    return (
        output, grad_tokens, cpe, cpe_sums, gain_one, shift_one, grad_qkv, query_sums, value_sums,
        taps_small, taps_middle, taps_large, crpe_sums, grad_proj, proj_sums, gain_two, shift_two,
        fc1, fc1_sums, fc2, fc2_sums,
    )


def solution(mesh):
    split, whole = P(("dp", "blk"), None), P()
    fc1, fc1_bias, fc2 = P(None, "blk"), P("blk"), P("blk", None)
    return jax.shard_map(
        shards,
        mesh=mesh,
        in_specs=(split, P(("dp", "blk"))) + (whole,) * 15 + (fc1, fc1_bias, fc2, whole, split),
        out_specs=(split, split) + (whole,) * 15 + (fc1, fc1_bias, fc2, whole),
        check_vma=False,
    )
```

```python
import functools
import math

import jax
import jax.numpy as jnp
from jax import lax
from jax.experimental import pallas as pl
from jax.experimental.pallas import tpu as pltpu
from jax.sharding import PartitionSpec as P

HEADS = 8
GRID = 9
CELLS = GRID * GRID
SLOT = CELLS + 1
LANES = 128
EPSILON = 1e-6
SLOT_PAD = 96
TILE = 256
BAND = 128
MLP_TILE = 512
KERNEL_SIZES = (3, 5, 7, 7)
PIECE = 256
VMEM_BYTES = 62 * 1024 * 1024

F32 = jnp.float32
BF16 = jnp.bfloat16

SMALL_ROWS = (56, 58, 49, 50, 64, 65, 66)
CPE_B, GAIN1, SHIFT1, QUERY_B, VALUE_B, CRPE_B, PROJ_B = range(7)
GAIN2, SHIFT2, FC2_B = range(3)


def dot(left, right):
    return lax.dot_general(left, right, (((1,), (0,)), ((), ())), preferred_element_type=F32)


def dot_nt(left, right):
    return lax.dot_general(left, right, (((1,), (1,)), ((), ())), preferred_element_type=F32)


def dot_tn(left, right):
    return lax.dot_general(left, right, (((0,), (0,)), ((), ())), preferred_element_type=F32)


class Copies:
    def __init__(self, sems):
        self.sems, self.count, self.open = sems, 0, []

    def start(self, source, target):
        assert self.count < self.sems.shape[0]
        copy = pltpu.make_async_copy(source, target, self.sems.at[self.count])
        self.count += 1
        copy.start()
        self.open.append(copy)
        return copy

    def wait(self, copy):
        copy.wait()
        self.open = [other for other in self.open if other is not copy]

    def finish(self):
        for copy in self.open:
            copy.wait()


def loop(count, body, unroll=1):
    def step(index, carry):
        body(index)
        return carry

    lax.fori_loop(0, count, step, 0, unroll=unroll)


def rows_at(start, count, multiple=8):
    return pl.ds(pl.multiple_of(start, multiple), count)


def lanes_of(block):
    return slice(block * LANES, (block + 1) * LANES)


def fold_rows(values):
    count, lanes = values.shape
    return jnp.sum(values.reshape(count // 8, 8, lanes), 0)


def fill_mask(side, mask_ref, images):
    mask_ref[SLOT * images :, :] = jnp.zeros_like(mask_ref[SLOT * images :, :])

    inside = [jnp.where(place < side, 1.0, 0.0).astype(F32) for place in range(GRID)]
    for slot in range(SLOT):
        level = jnp.float32(1.0) if slot == CELLS else inside[slot // GRID] * inside[slot % GRID]
        mask_ref[slot * images : (slot + 1) * images, :] = jnp.full((images, LANES), level, F32)


def spread(rows_ref, blocks_ref, blocks):
    total = rows_ref.shape[0]

    def body(step):
        at = rows_at(step * 48, 48, 16)
        values = rows_ref[at, :].astype(F32)
        for block in range(blocks):
            blocks_ref[block, at, :] = values[:, lanes_of(block)]

    loop(total // 48, body)


def unspread(blocks_ref, rows_ref, blocks):
    total = rows_ref.shape[0]

    def body(step):
        at = rows_at(step * 48, 48, 16)
        values = [blocks_ref[block, at, :] for block in range(blocks)]
        rows_ref[at, :] = jnp.concatenate(values, 1).astype(BF16)

    loop(total // 48, body)


def natural_slot(slot):
    return jnp.where(slot == CELLS, 0, slot + 1)


def fill_table(vectors, table_ref):
    for row, ref in enumerate(vectors):
        table_ref[row : row + 1, :] = ref[...].astype(F32).reshape(1, -1)


def fill_taps(table, taps_ref, count, blocks):
    for tap in range(count):
        for block in range(blocks):
            taps_ref[block, tap] = jnp.broadcast_to(table[tap : tap + 1, lanes_of(block)], (8, LANES))


def centred(size):
    inset = (7 - size) // 2
    return [(a + inset) * 7 + b + inset for a in range(size) for b in range(size)]


def lane_picker(width, offset, channels):
    lane = lax.broadcasted_iota(jnp.int32, (width, channels), 0)
    channel = lax.broadcasted_iota(jnp.int32, (width, channels), 1)
    return jnp.where(channel == lane + offset, 1.0, 0.0).astype(BF16)


def assemble_taps(kernels, work_ref, table_ref):
    channels = table_ref.shape[1]
    table_ref[...] = jnp.zeros_like(table_ref)
    offset = 0
    for size, kernel_ref in zip((3, 5, 7), kernels):
        width = kernel_ref.shape[1]
        work_ref[0 : size * size, :] = dot(kernel_ref[...], lane_picker(width, offset, channels))
        for tap, place in enumerate(centred(size)):
            table_ref[place : place + 1, :] += work_ref[tap : tap + 1, :]
        offset += width


def correlate(source_ref, taps_ref, size, span, images, block, sub, emit, turned=False, beside=()):
    margin, inset = size // 2, (span - size) // 2
    beside = iter(beside)

    def load(cell):
        return source_ref[block, rows_at(cell * images + sub * 8, 8), :]

    for row in range(GRID):
        totals = [None] * GRID
        for a in range(size):
            from_row = row + a - margin
            if not 0 <= from_row < GRID:
                continue
            cells = [load(from_row * GRID + col) for col in range(GRID)]
            for b in range(size):
                tap = (a + inset) * span + b + inset
                weight = taps_ref[block, span * span - 1 - tap if turned else tap]
                for col in range(GRID):
                    from_col = col + b - margin
                    if 0 <= from_col < GRID:
                        term = cells[from_col] * weight
                        totals[col] = term if totals[col] is None else totals[col] + term
        for col in range(GRID):
            emit(row * GRID + col, totals[col])
        next(beside, None)
        next(beside, None)
    for _ in beside:
        pass


def tap_sums(grad_ref, source_ref, sums_ref, size, span, images, block, sub):
    margin, inset = size // 2, (span - size) // 2

    def load(ref, cell):
        return ref[block, rows_at(cell * images + sub * 8, 8), :]

    for a in range(size):
        totals = [None] * size
        for row in range(GRID):
            from_row = row + a - margin
            if not 0 <= from_row < GRID:
                continue
            grads = [load(grad_ref, row * GRID + col) for col in range(GRID)]
            cells = [load(source_ref, from_row * GRID + col) for col in range(GRID)]
            for b in range(size):
                part = None
                for col in range(GRID):
                    from_col = col + b - margin
                    if 0 <= from_col < GRID:
                        term = grads[col] * cells[from_col]
                        part = term if part is None else part + term
                totals[b] = part if totals[b] is None else totals[b] + part
        for b in range(size):
            tap = (a + inset) * span + b + inset
            sums_ref[block, tap] += totals[b]


def by_block(images, body, before=None, beside=None):
    subs = images // 8
    first = 0
    while first < len(KERNEL_SIZES):
        size = KERNEL_SIZES[first]
        count = 1
        while first + count < len(KERNEL_SIZES) and KERNEL_SIZES[first + count] == size:
            count += 1
        for block in range(first, first + count):
            if before is not None:
                before(block)
        last = beside is not None and first + count == len(KERNEL_SIZES)
        share = images // (count * subs)

        def step(index, first=first, size=size, last=last, share=share):
            if last:
                work = (part for one in range(share) for part in beside(index * share + one))
                body(size, first + index // subs, index % subs, work)
            else:
                body(size, first + index // subs, index % subs)

        loop(count * subs, step)
        first += count


def row_sums(value):
    high = value.astype(BF16)
    low = (value - high.astype(F32)).astype(BF16)
    return dot(jnp.concatenate([high, low], 1), jnp.ones((2 * LANES, LANES), BF16))


def row_means(blocks):
    return row_sums(sum(blocks[1:], blocks[0])) * (1.0 / (len(blocks) * LANES))


def norm_parts(blocks):
    mean = row_means(blocks)
    centered = [value - mean for value in blocks]
    inverse = lax.rsqrt(row_means([value * value for value in centered]) + EPSILON)
    return [value * inverse for value in centered], inverse


def norm_forward(source_ref, table_ref, gain_row, shift_row, normed_ref, turned_ref, parts_ref, inverse_ref, keep=None):
    blocks = source_ref.shape[0]
    gains = table_ref[gain_row : gain_row + 1, :]
    shifts = table_ref[shift_row : shift_row + 1, :]

    def body(step):
        at = rows_at(step * BAND, BAND, BAND)
        source = [source_ref[block, at, :] for block in range(blocks)]
        if keep is not None:
            keep(at, source)
        parts, inverse = norm_parts(source)
        inverse_ref[at, :] = inverse
        for block in range(blocks):
            parts_ref[block, at, :] = parts[block]
        out = [
            parts[block] * gains[:, lanes_of(block)] + shifts[:, lanes_of(block)]
            for block in range(blocks)
        ]
        normed_ref[at, :] = jnp.concatenate(out, 1).astype(BF16)

    loop(source_ref.shape[1] // BAND, body, unroll=2)
    transpose_rows(normed_ref, turned_ref)


def transpose_rows(rows_ref, turned_ref):
    width = rows_ref.shape[1]

    def body(step):
        at = rows_at(step * TILE, TILE, TILE)
        turned_ref[0:width, at] = rows_ref[at, :].T

    loop(rows_ref.shape[0] // TILE, body)


def norm_backward(parts_ref, inverse_ref, grad_at, direct_at, table_ref, gain_row, emit, blocks, total):
    gains = table_ref[gain_row : gain_row + 1, :]

    def body(step, sums):
        at = rows_at(step * BAND, BAND, BAND)
        parts, inverse = [parts_ref[block, at, :] for block in range(blocks)], inverse_ref[at, :]
        grads = [grad_at(block, at) for block in range(blocks)]
        scaled = [grads[block] * gains[:, lanes_of(block)] for block in range(blocks)]
        product = [grads[block] * parts[block] for block in range(blocks)]
        crossed = [product[block] * gains[:, lanes_of(block)] for block in range(blocks)]
        mean, cross = row_means(scaled), row_means(crossed)
        out = [
            direct_at(block, at) + inverse * (scaled[block] - mean - parts[block] * cross)
            for block in range(blocks)
        ]
        emit(at, out)
        gain_sums = [sums[0][block] + fold_rows(product[block]) for block in range(blocks)]
        shift_sums = [sums[1][block] + fold_rows(grads[block]) for block in range(blocks)]
        return (gain_sums, shift_sums)

    zero = [jnp.zeros((8, LANES), F32) for _ in range(blocks)]
    return lax.fori_loop(0, total // BAND, body, (zero, zero), unroll=2)


def total_row(parts):
    return jnp.concatenate([jnp.sum(part, 0, keepdims=True) for part in parts], 1)


def head_mask():
    row = lax.broadcasted_iota(jnp.int32, (LANES, LANES), 0)
    col = lax.broadcasted_iota(jnp.int32, (LANES, LANES), 1)
    size = LANES // 2
    return jnp.where((row < size) == (col < size), size ** (-0.5), 0.0).astype(F32)


def pack_kernel(bias_ref, fc1_ref, fc2_ref, packed_ref):
    channels = fc1_ref.shape[0]
    packed_ref[0:channels, :] = fc1_ref[...]
    packed_ref[channels : 2 * channels, :] = fc2_ref[...]
    rest = packed_ref.at[2 * channels :, :]
    rest[...] = jnp.broadcast_to(bias_ref[...].reshape(1, -1), rest.shape)


def front_kernel(
    side_ref, tokens_ref, cpe_ref, small_ref, middle_ref, large_ref, qkv_ref, proj_ref,
    cpe_bias_ref, gain_ref, shift_ref, query_bias_ref, value_bias_ref, crpe_bias_ref, proj_bias_ref,
    crpe_ref, mask_out, input_out, parts_out, inverse_out, query_out, weight_out, value_out, convolved_out, normed_t_out, context_out, attended_t_out, second_out,
    input_ref, inverse_ref, query_ref, weight_ref, value_ref, convolved_ref, normed_t_ref, context_ref, attended_t_ref,
    second_ref, position_ref, mask_ref, work_ref, normed_ref, cpe_taps_ref, crpe_taps_ref, crpe_work_ref, table_ref, sems,
):
    fill_table(
        (cpe_bias_ref, gain_ref, shift_ref, query_bias_ref, value_bias_ref, crpe_bias_ref, proj_bias_ref), table_ref
    )
    out = Copies(sems)
    rows, channels = tokens_ref.shape
    blocks = channels // LANES
    images = rows // SLOT
    padded = normed_ref.shape[0]
    held = SLOT_PAD * images
    fill_mask(side_ref[0], mask_ref, images)
    assemble_taps((small_ref, middle_ref, large_ref), crpe_work_ref, crpe_ref)
    fill_taps(cpe_ref[...].astype(F32), cpe_taps_ref, 9, blocks)
    fill_taps(crpe_ref, crpe_taps_ref, 49, blocks)
    spread(tokens_ref, work_ref, blocks)

    def arrange(slot):
        at = rows_at(slot * images, images)
        mask = mask_ref[at, :]
        for block in range(blocks):
            values = work_ref[block, pl.ds(natural_slot(slot), images, stride=SLOT), :]
            input_ref[block, at, :] = values * mask

    out.start(mask_ref, mask_out)
    loop(SLOT, arrange, unroll=2)
    for ref in (input_ref, position_ref, convolved_ref):
        ref[:, rows:padded, :] = jnp.zeros((blocks, padded - rows, LANES), F32)
    position_ref[:, CELLS * images : rows, :] = input_ref[:, CELLS * images : rows, :]
    convolved_ref[:, CELLS * images : rows, :] = jnp.zeros((blocks, images, LANES), F32)

    subs = images // 8

    def position(index):
        block, sub = index // subs, index % subs
        bias = table_row(table_ref, CPE_B, block)

        def emit(cell, total):
            at = rows_at(cell * images + sub * 8, 8)
            position_ref[block, at, :] = input_ref[block, at, :] + mask_ref[at, :] * (total + bias)

        correlate(input_ref, cpe_taps_ref, 3, 3, images, block, sub, emit)

    loop(blocks * subs, position)
    out.start(input_ref, input_out)
    norm_forward(
        position_ref, table_ref, GAIN1, SHIFT1, normed_ref, normed_t_ref, second_ref, inverse_ref
    )
    sent_parts = out.start(second_ref, parts_out)
    out.start(inverse_ref, inverse_out)
    normed_t_ref[channels:, :] = jnp.ones_like(normed_t_ref[channels:, :])
    out.start(normed_t_ref, normed_t_out)

    def project(step):
        at = rows_at(step * TILE, TILE, TILE)
        normed = normed_ref[at, :]
        mask = mask_ref[at, :]
        query = dot(normed, qkv_ref[:, :channels]) + table_ref[QUERY_B : QUERY_B + 1, :]
        for block in range(blocks):
            query_ref[block, at, :] = query[:, lanes_of(block)]
        key = dot(normed, qkv_ref[:, channels : 2 * channels])
        for block in range(blocks):
            weight_ref[block, at, :] = key[:, lanes_of(block)]
        value = dot(normed, qkv_ref[:, 2 * channels :]) + table_ref[VALUE_B : VALUE_B + 1, :]
        for block in range(blocks):
            value_ref[block, at, :] = value[:, lanes_of(block)] * mask

    loop(padded // TILE, project)
    for ref in (query_ref, value_ref):
        ref[:, padded:held, :] = jnp.zeros((blocks, held - padded, LANES), F32)
    weight_ref[:, rows:held, :] = jnp.zeros((blocks, held - rows, LANES), F32)
    out.start(query_ref, query_out)
    out.start(value_ref, value_out)

    def soften(index):
        block, sub = index // subs, index % subs
        top = None
        for slot in range(SLOT):
            at = rows_at(slot * images + sub * 8, 8)
            key = jnp.where(mask_ref[at, :] > 0, weight_ref[block, at, :], -1e30)
            top = key if top is None else jnp.maximum(top, key)
        total = None
        for slot in range(SLOT):
            at = rows_at(slot * images + sub * 8, 8)
            mask = mask_ref[at, :]
            key = jnp.where(mask > 0, weight_ref[block, at, :], -1e30)
            level = jnp.exp(key - top) * mask
            weight_ref[block, at, :] = level
            total = level if total is None else total + level
        inverse = 1.0 / total
        for slot in range(SLOT):
            at = rows_at(slot * images + sub * 8, 8)
            weight_ref[block, at, :] = weight_ref[block, at, :] * inverse

    loop(blocks * subs, soften)
    out.start(weight_ref, weight_out)
    heads = head_mask()

    def attend(image):
        at = pl.ds(image, SLOT_PAD, stride=images)
        for block in range(blocks):
            weight = weight_ref[block, at, :].astype(BF16)
            value = value_ref[block, at, :].astype(BF16)
            query = query_ref[block, at, :].astype(BF16)
            context = (dot_tn(weight, value) * heads).astype(BF16)
            context_ref[image, block] = context
            work_ref[block, at, :] = dot(query, context)
            yield

    def convolve(size, block, sub, beside=()):
        bias = table_row(table_ref, CRPE_B, block)

        def emit(cell, total):
            convolved_ref[block, rows_at(cell * images + sub * 8, 8), :] = total + bias

        correlate(value_ref, crpe_taps_ref, size, 7, images, block, sub, emit, beside=beside)

    by_block(images, convolve, beside=attend)
    out.start(convolved_ref, convolved_out)
    out.start(context_ref, context_out)
    out.wait(sent_parts)

    def finish(step):
        at = rows_at(step * TILE, TILE, TILE)
        attended = jnp.concatenate(
            [
                work_ref[block, at, :] + query_ref[block, at, :] * convolved_ref[block, at, :]
                for block in range(blocks)
            ],
            1,
        ).astype(BF16)
        attended_t_ref[:, at] = attended.T
        branch = dot(attended, proj_ref[...]) + table_ref[PROJ_B : PROJ_B + 1, :]
        for block in range(blocks):
            second_ref[block, at, :] = position_ref[block, at, :] + branch[:, lanes_of(block)]

    half = padded // TILE // 2
    loop(half, finish)
    part = slice(0, half * TILE)
    out.start(second_ref.at[:, part], second_out.at[:, part])
    loop(padded // TILE - half, lambda step: finish(step + half))
    part = slice(half * TILE, padded)
    out.start(second_ref.at[:, part], second_out.at[:, part])
    out.start(attended_t_ref, attended_t_out)
    out.finish()


def table_row(table_ref, row, block):
    return table_ref[row : row + 1, pl.ds(pl.multiple_of(block * LANES, LANES), LANES)]


def gelu_parts(value):
    level = 0.5 + 0.5 * lax.erf(value * math.sqrt(0.5))
    return level, jnp.exp2(value * value * (-0.5 / math.log(2.0)) - 0.5 * math.log2(2.0 * math.pi))


def cotangent_kernel(cot_ref, mask_ref, cot_rows_out, cot_t_out, sums_ref, cot_rows_ref, cot_t_ref, work_ref, sems):
    copies = Copies(sems)
    rows, channels = cot_ref.shape
    blocks = channels // LANES
    images = rows // SLOT
    padded = cot_rows_ref.shape[0]
    spread(cot_ref, work_ref, blocks)
    cot_rows_ref[rows:padded, :] = jnp.zeros((padded - rows, channels), BF16)

    def arrange(step, sums):
        at = rows_at(step * (2 * images), 2 * images, 16)
        mask = mask_ref[at, :]
        parts = []
        for block in range(blocks):
            pair = [
                work_ref[block, pl.ds(natural_slot(2 * step + one), images, stride=SLOT), :]
                for one in range(2)
            ]
            parts.append(jnp.concatenate(pair, 0) * mask)
        cot_rows_ref[at, :] = jnp.concatenate(parts, 1).astype(BF16)
        return [sums[block] + fold_rows(parts[block]) for block in range(blocks)]

    zero = [jnp.zeros((8, LANES), F32) for _ in range(blocks)]
    sums_ref[...] = jnp.concatenate(lax.fori_loop(0, SLOT // 2, arrange, zero), 1)
    copies.start(cot_rows_ref, cot_rows_out)
    transpose_rows(cot_rows_ref, cot_t_ref)
    copies.start(cot_t_ref, cot_t_out)
    copies.finish()


def mlp_kernel(
    side_ref, bias_sums_ref, cot_rows_in, cot_t_in, second_in, fc_in, gain_ref, shift_ref, fc2_bias_ref,
    result_out, grad_out, grad_fc_keep, grad_fc_send, small_ref,
    second_ref, fc_ref, grad_ref, grad_fc_ref,
    cot_rows_ref, cot_t_ref, normed_ref, normed_t_ref, hidden_ref, pre_ref, hidden_two_ref, pre_two_ref, mlp_ref, back_ref,
    table_ref, result_ref, inverse_ref, sems,
):
    fill_table((gain_ref, shift_ref, fc2_bias_ref), table_ref)
    copies = Copies(sems)
    got_second = copies.start(second_in, second_ref)
    got_fc = copies.start(fc_in, fc_ref)
    got_cot = [copies.start(cot_rows_in, cot_rows_ref), copies.start(cot_t_in, cot_t_ref)]
    padded, channels = cot_rows_ref.shape
    blocks = channels // LANES
    owners, _, units = fc_ref.shape
    mine, half_x, half_z = side_ref[1], side_ref[2] & 1, (side_ref[2] >> 1) & 1
    got_second.wait()
    fc2_bias = table_ref[FC2_B : FC2_B + 1, :]

    def keep(at, second):
        for block in range(blocks):
            mlp_ref[at, lanes_of(block)] = second[block] + fc2_bias[:, lanes_of(block)]

    norm_forward(
        second_ref, table_ref, GAIN2, SHIFT2, normed_ref, normed_t_ref, second_ref, inverse_ref, keep
    )
    normed_t_ref[channels:, :] = jnp.ones_like(normed_t_ref[channels:, :])
    got_fc.wait()
    for copy in got_cot:
        copy.wait()

    tiles = padded // MLP_TILE

    def weights(slot, held, which, end):
        left_ref, right_ref = (normed_t_ref, held[1]) if which == 0 else (cot_t_ref, held[0])
        last = left_ref.shape[0] if end else PIECE
        grad = dot(left_ref[end * PIECE : last, :], right_ref[...]).astype(BF16)
        place = ((half_x ^ which) << 1) | (half_z ^ end)
        grad_fc_ref[slot, place, 0:PIECE, :] = grad[0:PIECE]
        if last > channels:
            grad_fc_ref[slot, (half_x << 1) | half_z, PIECE:, :] = grad[PIECE:]

    def part(slot, held, before):
        owner = mine ^ ((slot >> 1) | ((slot & 1) << 1))
        hidden_ref, pre_ref = held
        for step in range(tiles):
            at = slice(step * MLP_TILE, (step + 1) * MLP_TILE)
            first = fc_ref[owner, 0:channels, :]
            second = fc_ref[owner, channels : 2 * channels, :]
            bias = fc_ref[owner, 2 * channels :, :].astype(F32)[0:1]
            values, grads = dot(normed_ref[at, :], first) + bias, dot_nt(cot_rows_ref[at, :], second)
            if before is not None and step < 4:
                weights(slot - 1, before, step // 2, step % 2)
            level, density = gelu_parts(values)
            hidden = (values * level).astype(BF16)
            pre = (grads * (level + values * density)).astype(BF16)
            hidden_ref[at, :] = hidden
            pre_ref[at, :] = pre
            mlp, back = dot(hidden, second), dot_nt(pre, first)
            if slot == 0:
                back_ref[at, :] = back
            else:
                back_ref[at, :] += back
            if slot < owners - 1:
                mlp_ref[at, :] += mlp
            else:
                result_ref[at, :] = (mlp_ref[at, :] + mlp).astype(BF16)

    held = (hidden_ref, pre_ref), (hidden_two_ref, pre_two_ref)
    targets = [(grad_fc_keep if slot < owners // 2 else grad_fc_send).at[slot % (owners // 2)] for slot in range(owners)]
    for slot in range(owners + 1):
        if slot < owners:
            part(slot, held[slot % 2], held[(slot - 1) % 2] if slot else None)
        else:
            for step in range(4):
                weights(owners - 1, held[(owners - 1) % 2], step // 2, step % 2)
        if slot:
            copies.start(grad_fc_ref.at[slot - 1], targets[slot - 1])

    def grad_at(block, at):
        return back_ref[at, lanes_of(block)]

    def direct_at(block, at):
        return cot_rows_ref[at, lanes_of(block)].astype(F32)

    def emit(at, out):
        for block in range(blocks):
            grad_ref[block, at, :] = out[block]

    gain_sums, shift_sums = norm_backward(
        second_ref, inverse_ref, grad_at, direct_at, table_ref, GAIN2, emit, blocks, padded
    )
    copies.start(grad_ref, grad_out)
    copies.start(result_ref, result_out)
    small_ref[...] = jnp.zeros_like(small_ref)
    small_ref[0:1, :] = total_row(gain_sums)
    small_ref[1:2, :] = total_row(shift_sums)
    small_ref[2:3, :] = jnp.sum(bias_sums_ref[...], 0, keepdims=True)
    for copy in copies.open[4:]:
        copy.wait()


def result_kernel(result_ref, mask_ref, out_ref, work_ref):
    rows, channels = out_ref.shape
    blocks = channels // LANES
    images = rows // SLOT

    def arrange(step):
        at = rows_at(step * (2 * images), 2 * images, 16)
        values = result_ref[at, :].astype(F32)
        mask = mask_ref[at, :]
        for block in range(blocks):
            masked = values[:, lanes_of(block)] * mask
            for one in range(2):
                to = pl.ds(natural_slot(2 * step + one), images, stride=SLOT)
                work_ref[block, to, :] = masked[one * images : (one + 1) * images]

    loop(SLOT // 2, arrange)
    unspread(work_ref, out_ref, blocks)


def branch_kernel(
    proj_ref, grad_in, attended_t_in,
    back_out, grad_proj_ref, small_ref,
    grad_ref, attended_t_ref, back_ref, branch_ref, sems,
):
    copies = Copies(sems)
    padded, channels = branch_ref.shape
    blocks = channels // LANES
    held = back_ref.shape[1]
    half = padded // 2
    halves = slice(0, half), slice(half, padded)
    got = [copies.start(grad_in.at[:, part], grad_ref.at[:, part]) for part in halves]
    got_attended = copies.start(attended_t_in, attended_t_ref)
    back_ref[:, padded:held, :] = jnp.zeros((blocks, held - padded, LANES), F32)
    sent = [copies.start(back_ref.at[:, padded:held], back_out.at[:, padded:held])]

    total = jnp.zeros((8, channels), F32)
    step = half // 2
    for end, part in enumerate(halves):
        got[end].wait()
        for first in range(end * half, (end + 1) * half, step):
            at = slice(first, first + step)
            low = jnp.concatenate([grad_ref[block, at, :] for block in range(blocks)], 1).astype(BF16)
            branch_ref[at, :] = low
            total += fold_rows(low.astype(F32))
            back = dot_nt(low, proj_ref[...])
            for block in range(blocks):
                back_ref[block, at, :] = back[:, lanes_of(block)]
        sent.append(copies.start(back_ref.at[:, part], back_out.at[:, part]))
    got_attended.wait()
    grad_proj_ref[...] = dot(attended_t_ref[...], branch_ref[...]).astype(BF16)
    small_ref[...] = total
    for copy in sent:
        copy.wait()


def mix_kernel(
    side_ref, small_mlp_ref, small_branch_ref, crpe_ref, grad_proj_ref,
    back_in, query_in, weight_in, value_in, convolved_in, normed_t_in, context_in, mask_in,
    keep_ref, send_ref, projected_out,
    total_ref, back_ref, query_ref, weight_ref, value_ref, convolved_ref, normed_t_ref, context_ref, projected_ref,
    mask_ref, small_ref, edge_ref, turned_ref, crpe_taps_ref, sems,
):
    copies = Copies(sems)
    pairs = (back_in, back_ref), (query_in, query_ref), (convolved_in, convolved_ref)
    first = [
        [copies.start(source.at[block], target.at[block]) for source, target in pairs] for block in range(back_ref.shape[0])
    ]
    pairs = (weight_in, weight_ref), (value_in, value_ref), (context_in, context_ref), (mask_in, mask_ref)
    pairs += ((normed_t_in, normed_t_ref),)
    then = [copies.start(*pair) for pair in pairs]
    blocks, padded, _ = edge_ref.shape
    channels = blocks * LANES
    held = query_ref.shape[1]
    images = held // SLOT_PAD
    rows = images * SLOT
    subs = images // 8
    fill_taps(crpe_ref, crpe_taps_ref, 49, blocks)
    turned_ref[:, CELLS * images :, :] = jnp.zeros((blocks, padded - CELLS * images, LANES), F32)
    bias_sums = []

    def arrived(block):
        for copy in first[block]:
            copy.wait()

        def edges(step, total):
            at = rows_at(step * (9 * images), 9 * images)
            back = back_ref[block, at, :]
            edge = back * query_ref[block, at, :]
            edge_ref[block, at, :] = edge
            convolved_ref[block, at, :] = back * convolved_ref[block, at, :]
            return total + fold_rows(edge)

        bias_sums.append(lax.fori_loop(0, CELLS // 9, edges, jnp.zeros((8, LANES), F32)))

    def convolve(size, block, sub):
        def emit(cell, total):
            turned_ref[block, rows_at(cell * images + sub * 8, 8), :] = total

        correlate(edge_ref, crpe_taps_ref, size, 7, images, block, sub, emit, turned=True)

    by_block(images, convolve, arrived)
    for copy in then:
        copy.wait()
    heads = head_mask()

    def attend(image):
        at = pl.ds(image, SLOT_PAD, stride=images)
        for block in range(blocks):
            weight = weight_ref[block, at, :]
            low = weight.astype(BF16)
            value = value_ref[block, at, :].astype(BF16)
            query = query_ref[block, at, :].astype(BF16)
            back = back_ref[block, at, :].astype(BF16)
            context = context_ref[image, block]
            grad = (dot_tn(query, back) * heads).astype(BF16)
            query_ref[block, at, :] = dot_nt(back, context)
            key = dot_nt(value, grad)
            back_ref[block, at, :] = weight * (key - jnp.sum(weight * key, 0, keepdims=True))
            value_ref[block, at, :] = dot(low, grad)

    loop(images, attend, unroll=4)
    projected_ref[rows:padded, :] = jnp.zeros((padded - rows, 3 * channels), BF16)

    def gather(step):
        at = rows_at(step * (2 * images), 2 * images, 16)
        mask = mask_ref[at, :]
        parts = [[], [], []]
        for block in range(blocks):
            parts[0].append(query_ref[block, at, :] + convolved_ref[block, at, :])
            parts[1].append(back_ref[block, at, :])
            parts[2].append((value_ref[block, at, :] + turned_ref[block, at, :]) * mask)
        for which in range(3):
            cols = slice(which * channels, (which + 1) * channels)
            projected_ref[at, cols] = jnp.concatenate(parts[which], 1).astype(BF16)

    loop(SLOT // 2, gather)
    sent = copies.start(projected_ref, projected_out)
    small_ref[...] = jnp.zeros_like(small_ref)
    index = ((side_ref[1] & 1) << 2) | ((side_ref[2] & 1) << 1) | (side_ref[1] >> 1)

    def place(matrix, grad):
        for end in range(channels // PIECE):
            piece = matrix * (channels // PIECE) + end
            total_ref[piece ^ index, 0:PIECE, :] = grad[end * PIECE : (end + 1) * PIECE]

    for which in range(3):
        cols = slice(which * channels, (which + 1) * channels)
        grad = dot(normed_t_ref[...], projected_ref[:, cols])
        place(which, grad[0:channels].astype(BF16))
        small_ref[56 + which : 57 + which, :] = grad[channels : channels + 1]
    place(3, grad_proj_ref[...])
    small_ref[49:50, :] = total_row(bias_sums)
    small_ref[50:51, :] = jnp.sum(small_branch_ref[...], 0, keepdims=True)
    small_ref[64:72, :] = small_mlp_ref[...]
    for piece in range(total_ref.shape[0]):
        total_ref[piece ^ index, PIECE:, :] = small_ref[piece * 16 : (piece + 1) * 16, :].astype(BF16)
    out = [copies.start(total_ref.at[4:8], send_ref), copies.start(total_ref.at[0:4], keep_ref)]
    for copy in [sent] + out:
        copy.wait()


def taps_kernel(
    back_in, query_in, value_in,
    small_ref,
    back_ref, query_ref, value_ref, sums_ref, sems,
):
    copies = Copies(sems)
    blocks, cells, _ = back_ref.shape
    images = cells // CELLS
    part = slice(0, cells)
    pairs = (back_in, back_ref), (query_in, query_ref), (value_in, value_ref)
    got = [
        [copies.start(source.at[block, part], target.at[block]) for source, target in pairs] for block in range(blocks)
    ]
    sums_ref[...] = jnp.zeros_like(sums_ref)

    def arrived(block):
        for copy in got[block]:
            copy.wait()

        def edges(step):
            at = rows_at(step * (9 * images), 9 * images)
            back_ref[block, at, :] = back_ref[block, at, :] * query_ref[block, at, :]

        loop(CELLS // 9, edges)

    def taps(size, block, sub):
        tap_sums(back_ref, value_ref, sums_ref, size, 7, images, block, sub)

    by_block(images, taps, arrived)
    small_ref[...] = jnp.zeros_like(small_ref)
    for block in range(blocks):
        small_ref[0:49, lanes_of(block)] = jnp.sum(sums_ref[block], 1)


def norm_half(
    copies, first, base, operands, grad_out, projected_ref, parts_ref, inverse_ref, grad_ref, normed_ref, table_ref
):
    qkv_ref, gain_ref, projected_in, parts_in, inverse_in, grad_in = operands
    fill_table((gain_ref,), table_ref)
    padded, channels = normed_ref.shape
    blocks = channels // LANES
    half = padded // 2
    got_halves = [
        copies.start(projected_in.at[pl.ds(first + end * half, half)], projected_ref.at[pl.ds(end * half, half)])
        for end in range(2)
    ]
    source, target = pl.ds(first, padded), pl.ds(base, padded)
    got = [
        copies.start(parts_in.at[:, source], parts_ref),
        copies.start(inverse_in.at[source], inverse_ref),
        copies.start(grad_in.at[:, source], grad_ref.at[:, target]),
    ]

    for end in range(2):
        got_halves[end].wait()
        at = slice(end * half, (end + 1) * half)
        normed_ref[at, :] = dot_nt(projected_ref[at, :], qkv_ref[...])
    for copy in got:
        copy.wait()

    def grad_at(block, at):
        return normed_ref[at, lanes_of(block)]

    def moved(at):
        return rows_at(base + at.start, at.size, BAND)

    def direct_at(block, at):
        return grad_ref[block, moved(at), :]

    def emit_norm(at, out):
        for block in range(blocks):
            grad_ref[block, moved(at), :] = out[block]

    sums = norm_backward(parts_ref, inverse_ref, grad_at, direct_at, table_ref, 0, emit_norm, blocks, padded)
    return copies.start(grad_ref.at[:, target], grad_out), sums


def norm_first_kernel(
    qkv_ref, gain_ref, projected_in, parts_in, inverse_in, grad_in,
    grad_out, small_ref,
    projected_ref, parts_ref, inverse_ref, grad_ref, normed_ref, table_ref, sems,
):
    operands = qkv_ref, gain_ref, projected_in, parts_in, inverse_in, grad_in
    sent, (gain_sums, shift_sums) = norm_half(
        Copies(sems), 0, 0, operands, grad_out, projected_ref, parts_ref, inverse_ref, grad_ref, normed_ref,
        table_ref,
    )
    small_ref[...] = jnp.zeros_like(small_ref)
    small_ref[0:1, :] = total_row(gain_sums)
    small_ref[1:2, :] = total_row(shift_sums)
    sent.wait()


def norm_last_kernel(
    first, qkv_ref, gain_ref, projected_in, parts_in, inverse_in, grad_in, grad_first_in, input_in, small_first_ref,
    small_taps_ref,
    grad_out, small_ref,
    projected_ref, parts_ref, inverse_ref, grad_ref, normed_ref, table_ref, input_ref, sums_ref, work_ref, sems,
):
    copies = Copies(sems)
    blocks, cells, _ = input_ref.shape
    images = cells // CELLS
    subs = images // 8
    got = copies.start(grad_first_in, grad_ref.at[:, 0:first]), copies.start(input_in.at[:, 0:cells], input_ref)
    operands = qkv_ref, gain_ref, projected_in, parts_in, inverse_in, grad_in
    sent, (gain_sums, shift_sums) = norm_half(
        copies, first, first, operands, grad_out, projected_ref, parts_ref, inverse_ref, grad_ref, normed_ref,
        table_ref,
    )
    sums_ref[...] = jnp.zeros_like(sums_ref)
    work_ref[...] = jnp.zeros_like(work_ref)
    work_ref[0:56, :] = small_taps_ref[...]
    work_ref[57:58, :] = total_row(gain_sums) + small_first_ref[0:1, :]
    work_ref[58:59, :] = total_row(shift_sums) + small_first_ref[1:2, :]
    for copy in got:
        copy.wait()

    def colsum(step, sums):
        at = rows_at(step * (9 * images), 9 * images)
        return [sums[block] + fold_rows(grad_ref[block, at, :]) for block in range(blocks)]

    zero = [jnp.zeros((8, LANES), F32) for _ in range(blocks)]
    work_ref[56:57, :] = total_row(lax.fori_loop(0, GRID, colsum, zero))

    def taps(index):
        tap_sums(grad_ref, input_ref, sums_ref, 3, 3, images, index // subs, index % subs)

    loop(blocks * subs, taps)
    for block in range(blocks):
        work_ref[64:73, lanes_of(block)] = jnp.sum(sums_ref[block], 1)
    small_ref[...] = work_ref[...].astype(BF16)
    sent.wait()


def back_kernel(
    mask_ref, cpe_ref, first_in, second_in,
    tokens_ref,
    grad_ref, work_ref, result_ref, taps_ref, sems,
):
    copies = Copies(sems)
    half = first_in.shape[1]
    got = copies.start(first_in, grad_ref.at[:, 0:half]), copies.start(second_in, grad_ref.at[:, half : 2 * half])
    rows, channels = tokens_ref.shape
    blocks = channels // LANES
    images = rows // SLOT
    subs = images // 8
    fill_taps(cpe_ref[...].astype(F32), taps_ref, 9, blocks)
    for copy in got:
        copy.wait()

    def convolve(index):
        block, sub = index // subs, index % subs

        def emit(cell, total):
            at = rows_at(cell * images + sub * 8, 8)
            result_ref[block, at, :] = (grad_ref[block, at, :] + total) * mask_ref[at, :]

        correlate(grad_ref, taps_ref, 3, 3, images, block, sub, emit, turned=True)

    loop(blocks * subs, convolve)
    result_ref[:, CELLS * images : rows, :] = grad_ref[:, CELLS * images : rows, :]

    def arrange(slot):
        at = rows_at(slot * images, images)
        for block in range(blocks):
            work_ref[block, pl.ds(natural_slot(slot), images, stride=SLOT), :] = result_ref[block, at, :]

    loop(SLOT, arrange, unroll=2)
    unspread(work_ref, tokens_ref, blocks)


def finish_fc_kernel(
    side_ref, first_ref, second_ref, third_ref, fourth_ref,
    fc1_ref, fc2_ref, bias_ref,
    held_ref,
):
    index = ((side_ref[2] & 1) << 1) | ((side_ref[2] >> 1) & 1)
    for place, piece in enumerate((first_ref, second_ref, third_ref, fourth_ref)):
        held_ref[place ^ index] = piece[...]
    for end in range(2):
        fc1_ref[end * PIECE : (end + 1) * PIECE, :] = held_ref[end, 0:PIECE, :].astype(F32)
        fc2_ref[:, end * PIECE : (end + 1) * PIECE] = held_ref[2 + end, 0:PIECE, :].astype(F32).T
    bias_ref[...] = held_ref[0, PIECE:, :].astype(F32)[0:1].reshape(bias_ref.shape)


def finish_small_kernel(
    own_ref, first_ref, second_ref, third_ref,
    cpe_ref, cpe_bias_ref, gain_ref, shift_ref, crpe_small_ref, crpe_middle_ref, crpe_large_ref,
    work_ref,
):
    terms = [ref[...].astype(F32) for ref in (own_ref, first_ref, second_ref, third_ref)]
    small = ((terms[0] + terms[1]) + (terms[2] + terms[3])).astype(BF16)
    work_ref[...] = small.astype(F32)
    cpe_ref[...] = work_ref[64:73, :]
    for row, ref in enumerate((cpe_bias_ref, gain_ref, shift_ref)):
        ref[...] = work_ref[56 + row : 57 + row, :].reshape(ref.shape)
    channels = small.shape[1]
    offset = 0
    for size, ref in zip((3, 5, 7), (crpe_small_ref, crpe_middle_ref, crpe_large_ref)):
        width = ref.shape[1]
        taps = dot_nt(small, lane_picker(width, offset, channels))
        for tap, place in enumerate(centred(size)):
            ref[tap : tap + 1, :] = taps[place : place + 1, :]
        offset += width


def finish_kernel(side_ref, *refs):
    pieces, (qkv_ref, proj_ref), rows, (held_ref, small_ref) = refs[:8], refs[8:10], refs[10:-2], refs[-2:]
    index = ((side_ref[1] & 1) << 2) | ((side_ref[2] & 1) << 1) | (side_ref[1] >> 1)
    for place, piece in enumerate(pieces):
        held_ref[place ^ index] = piece[...]
    channels = proj_ref.shape[1]
    for piece in range(8):
        matrix, end = piece // 2, piece % 2
        at = slice(end * PIECE, (end + 1) * PIECE)
        values = held_ref[piece, 0:PIECE, :].astype(F32)
        if matrix < 3:
            qkv_ref[at, matrix * channels : (matrix + 1) * channels] = values
        else:
            proj_ref[at, :] = values
        small_ref[piece * 16 : (piece + 1) * 16, :] = held_ref[piece, PIECE:, :].astype(F32)
    for row, ref in zip(SMALL_ROWS, rows):
        ref[...] = small_ref[row : row + 1, :].reshape(ref.shape)


def add(*terms):
    return sum(term.astype(F32) for term in terms).astype(BF16)


def exchange(values, across_dp, across_blk):
    owners, parts = lax.axis_size("blk"), lax.axis_size("dp")
    flip = across_dp * owners + across_blk
    return lax.ppermute(values, ("dp", "blk"), [(at, at ^ flip) for at in range(parts * owners)])


def together(*values):
    return lax.optimization_barrier(values)


def shape(dims, dtype):
    return jax.ShapeDtypeStruct(dims, dtype)


def call(body, outs, scratch, cost, *operands):
    vmem, smem, hbm = (pl.BlockSpec(memory_space=space) for space in (pltpu.VMEM, pltpu.SMEM, pl.ANY))

    def place(value):
        return hbm if isinstance(value, Held) else smem if value.dtype == jnp.int32 else vmem

    def plain(values):
        return [value.array if isinstance(value, Held) else value for value in values]

    return pl.pallas_call(
        body,
        out_shape=plain(outs),
        in_specs=[place(value) for value in operands],
        out_specs=[place(value) for value in outs],
        scratch_shapes=[
            pltpu.SemaphoreType.DMA((item,)) if isinstance(item, int) else pltpu.VMEM(*item) for item in scratch
        ],
        compiler_params=pltpu.CompilerParams(vmem_limit_bytes=VMEM_BYTES),
        cost_estimate=pl.CostEstimate(flops=cost, bytes_accessed=cost // 1000, transcendentals=0),
    )(*plain(operands))


class Held:
    def __init__(self, array):
        self.array = array


def shards(
    tokens, sides, cpe_weight, cpe_bias, norm1_gain, norm1_shift, w_qkv, query_bias, value_bias,
    crpe_small, crpe_middle, crpe_large, crpe_bias, w_proj, proj_bias, norm2_gain, norm2_shift,
    w_fc1, fc1_bias, w_fc2, fc2_bias, cotangent,
):
    rows, channels = tokens.shape
    blocks = channels // LANES
    images = rows // SLOT
    padded = -(-rows // TILE) * TILE
    held = SLOT_PAD * images
    units = w_fc1.shape[1]
    owners = lax.axis_size("blk")

    (packed,) = call(
        pack_kernel, [shape((2 * channels + 16, units), BF16)], [], 1_000_000, fc1_bias, w_fc1, w_fc2
    )
    fc_all = lax.all_gather(packed, "blk", axis=0, tiled=False)
    scalars = jnp.stack([sides[0], lax.axis_index("blk"), lax.axis_index("dp")]).astype(jnp.int32)
    block_rows = (blocks, padded, LANES)
    block_held = (blocks, held, LANES)
    block_cells = (blocks, CELLS * images, LANES)
    contexts = (images, blocks, LANES, LANES), BF16
    front = [
        (block_rows, F32), (block_rows, F32), ((padded, LANES), F32), (block_held, F32), (block_held, F32), (block_held, F32),
        (block_rows, F32), ((channels + 16, padded), BF16), contexts, ((channels, padded), BF16), (block_rows, F32),
    ]
    crpe, mask, inputs, parts, inverse, query, weight, value, convolved, normed_t, context, attended_t, second = call(
        front_kernel,
        [shape((56, channels), F32), Held(shape((padded, LANES), F32))] + [Held(shape(*item)) for item in front],
        front[:1] + front[2:] + [
            (block_rows, F32), ((padded, LANES), F32), (block_held, F32), ((padded, channels), BF16),
            ((blocks, 9, 8, LANES), F32), ((blocks, 49, 8, LANES), F32), ((56, channels), F32), ((8, channels), F32), 13,
        ],
        40_000_000_000,
        scalars, tokens, cpe_weight, crpe_small, crpe_middle, crpe_large, w_qkv, w_proj,
        cpe_bias, norm1_gain, norm1_shift, query_bias, value_bias, crpe_bias, proj_bias,
    )
    pieces = (owners // 2, 4, PIECE + 16, units)
    cot_shapes = [((padded, channels), BF16), ((channels, padded), BF16)]
    cot_rows, cot_t, cot_sums = call(
        cotangent_kernel,
        [Held(shape(*item)) for item in cot_shapes] + [shape((8, channels), F32)],
        cot_shapes + [((blocks, rows, LANES), F32), 2],
        6_000_000_000,
        cotangent, mask,
    )
    result, grad_second, fc_keep, fc_send, small_mlp = call(
        mlp_kernel,
        [
            Held(shape((padded, channels), BF16)), Held(shape(block_rows, F32)), Held(shape(pieces, BF16)),
            Held(shape(pieces, BF16)),
            shape((8, channels), F32),
        ],
        [
            (block_rows, F32), (fc_all.shape, BF16), (block_rows, F32),
            ((owners, 4, PIECE + 16, units), BF16),
            ((padded, channels), BF16), ((channels, padded), BF16),
            ((padded, channels), BF16), ((channels + 16, padded), BF16),
            ((padded, units), BF16), ((padded, units), BF16), ((padded, units), BF16), ((padded, units), BF16),
            ((padded, channels), F32), ((padded, channels), F32), ((8, channels), F32), ((padded, channels), BF16), ((padded, LANES), F32), 6 + owners,
        ],
        60_000_000_000,
        scalars, cot_sums, Held(cot_rows), Held(cot_t), Held(second), Held(fc_all), norm2_gain, norm2_shift, fc2_bias,
    )
    fc_far = exchange(fc_send, 0, 1)
    back, grad_proj, small_branch = call(
        branch_kernel,
        [Held(shape(block_held, F32)), shape((channels, channels), BF16), shape((8, channels), F32)],
        [(block_rows, F32), ((channels, padded), BF16), (block_held, F32), ((padded, channels), BF16), 6],
        10_000_000_000,
        w_proj, Held(grad_second), Held(attended_t),
    )

    def half_of(side, end):
        part = slice(2 * end, 2 * end + 2)
        return add(fc_keep[side, part], fc_far[side, part])

    back, fc_y, fc_x, fc_yx = together(back, half_of(1, 0), half_of(0, 1), half_of(1, 1))
    fc_core = fc_far
    fc_far = exchange(fc_y, 0, 2), exchange(fc_x, 1, 0), exchange(fc_yx, 1, 2)
    total_keep, total_send, projected = call(
        mix_kernel,
        [Held(shape((4, PIECE + 16, channels), BF16))] * 2 + [Held(shape((padded, 3 * channels), BF16))],
        [
            ((8, PIECE + 16, channels), BF16),
            (block_held, F32), (block_held, F32), (block_held, F32), (block_held, F32), (block_rows, F32),
            ((channels + 16, padded), BF16), contexts, ((padded, 3 * channels), BF16),
            ((padded, LANES), F32), ((128, channels), F32), (block_rows, F32), (block_rows, F32),
            ((blocks, 49, 8, LANES), F32), 8 + 3 * blocks,
        ],
        50_000_000_000,
        scalars, small_mlp, small_branch, crpe, grad_proj,
        Held(back), Held(query), Held(weight), Held(value), Held(convolved), Held(normed_t), Held(context),
        Held(mask),
    )
    projected, total_keep, total_send, *fc_far = together(projected, total_keep, total_send, *fc_far)
    total_far = exchange(total_send, 0, 1)
    bits = [1 << bit for bit in range(1, lax.axis_size("dp").bit_length() - 1)]
    fc_bits = [bit for bit in bits if bit > 2]

    def end_of(end):
        return add(fc_keep[0, end], fc_core[0, end], *(far[end] for far in fc_far))

    fc_other, fc_own = end_of(1), end_of(0)
    sums = [add(total_keep[piece], total_far[piece]) for piece in range(4)]
    projected, fc_own, fc_other, *sums = together(projected, fc_own, fc_other, *sums)
    fc_far = exchange(fc_other, 2, 0)
    total_far = exchange(sums[1], 0, 2), exchange(sums[2], 1, 0), exchange(sums[3], 1, 2)
    block_half = (blocks, padded // 2, LANES)
    norm_outs = [Held(shape(block_half, F32)), shape((8, channels), F32)]
    norm_scratch = [((padded // 2, 3 * channels), BF16), (block_half, F32), ((padded // 2, LANES), F32)]
    norm_more = [((padded // 2, channels), F32), ((8, channels), F32)]
    grad_first, small_first = call(
        norm_first_kernel, norm_outs, norm_scratch + [(block_half, F32)] + norm_more + [6], 8_000_000_000,
        w_qkv, norm1_gain, Held(projected), Held(parts), Held(inverse), Held(grad_second),
    )
    back, grad_first, fc_own, own = together(back, grad_first, add(fc_own, fc_far), add(sums[0], *total_far))
    total_far = exchange(own, bits[0], 0)
    fc_far = exchange(fc_own, fc_bits[0], 0)
    (small_taps,) = call(
        taps_kernel,
        [shape((56, channels), F32)],
        [(block_cells, F32), (block_cells, F32), (block_cells, F32), ((blocks, 49, 8, LANES), F32), 3 * blocks],
        15_000_000_000,
        Held(back), Held(query), Held(value),
    )
    fc_own = add(fc_own, fc_far)
    for bit in fc_bits[1:]:
        fc_own = add(fc_own, exchange(fc_own, bit, 0))
    projected, small_taps, fc_own, own = together(projected, small_taps, fc_own, add(own, total_far))
    total_far = exchange(own, bits[1], 0)
    fc_other, fc_third = exchange(fc_own, 2, 0), exchange(fc_own, 1, 0)
    grad_last, small_back = call(
        functools.partial(norm_last_kernel, padded // 2),
        [norm_outs[0], shape((80, channels), BF16)],
        norm_scratch + [(block_rows, F32)] + norm_more
        + [(block_cells, F32), ((blocks, 9, 8, LANES), F32), ((80, channels), F32), 8],
        12_000_000_000,
        w_qkv, norm1_gain, Held(projected), Held(parts), Held(inverse), Held(grad_second), Held(grad_first), Held(inputs),
        small_first, small_taps,
    )
    own = add(own, total_far)
    for bit in bits[2:]:
        own = add(own, exchange(own, bit, 0))
    grad_last, small_back, result, fc_other, fc_third, own = together(
        grad_last, small_back, result, fc_other, fc_third, own
    )
    near = [own, exchange(own, 0, 2), exchange(own, 1, 0), exchange(own, 1, 2)]
    small_far, fc_fourth = exchange(small_back, 0, 1), exchange(fc_other, 1, 0)
    (output,) = call(
        result_kernel, [shape((rows, channels), BF16)], [((blocks, rows, LANES), F32)], 1_000_000,
        result, mask,
    )
    output, small, small_far, fc_fourth = together(output, small_back, small_far, fc_fourth)
    small, grad_last = together(add(small, small_far), grad_last)
    small_far = exchange(small, 0, 2)
    (grad_tokens,) = call(
        back_kernel,
        [shape((rows, channels), BF16)],
        [
            (block_rows, F32), ((blocks, rows, LANES), F32),
            (block_rows, F32), ((blocks, 9, 8, LANES), F32), 2,
        ],
        1_000_000,
        mask, cpe_weight, Held(grad_first), Held(grad_last),
    )
    grad_tokens, small, small_far, *near = together(grad_tokens, small, small_far, *near)
    total_pieces = near + [exchange(piece, 0, 1) for piece in near]
    small = add(small, small_far)
    small_far = exchange(small, 1, 0)
    small, fc_own = together(small, fc_own)
    fc1, fc2, fc1_sums = call(
        finish_fc_kernel,
        [shape((channels, units), F32), shape((units, channels), F32), shape((units,), F32)],
        [((4, PIECE + 16, units), BF16)],
        1_000_000,
        scalars, fc_own, fc_other, fc_third, fc_fourth,
    )
    fc1, small, small_far, *total_pieces = together(fc1, small, small_far, *total_pieces)
    small = add(small, small_far)
    for bit in bits[2:]:
        small = add(small, exchange(small, bit, 0))
    small_far = [exchange(small, flip, 0) for flip in (bits[0], bits[1], bits[0] | bits[1])]
    row = shape((channels,), F32)
    grad_qkv, grad_proj, query_sums, value_sums, crpe_sums, proj_sums, gain_two, shift_two, fc2_sums = call(
        finish_kernel,
        [shape((channels, 3 * channels), F32), shape((channels, channels), F32)] + [row] * len(SMALL_ROWS),
        [((8, PIECE + 16, channels), BF16), ((128, channels), F32)],
        1_000_000,
        scalars, *total_pieces,
    )
    grad_qkv, small, *small_far = together(grad_qkv, small, *small_far)
    cpe, cpe_sums, gain_one, shift_one, taps_small, taps_middle, taps_large = call(
        finish_small_kernel,
        [
            shape(cpe_weight.shape, F32), row, row, row,
            shape(crpe_small.shape, F32), shape(crpe_middle.shape, F32), shape(crpe_large.shape, F32),
        ],
        [((80, channels), F32)],
        1_000_000,
        small, *small_far,
    )
    return (
        output, grad_tokens, cpe, cpe_sums, gain_one, shift_one, grad_qkv, query_sums, value_sums,
        taps_small, taps_middle, taps_large, crpe_sums, grad_proj, proj_sums, gain_two, shift_two,
        fc1, fc1_sums, fc2, fc2_sums,
    )


def solution(mesh):
    split, whole = P(("dp", "blk"), None), P()
    fc1, fc1_bias, fc2 = P(None, "blk"), P("blk"), P("blk", None)
    return jax.shard_map(
        shards,
        mesh=mesh,
        in_specs=(split, P(("dp", "blk"))) + (whole,) * 15 + (fc1, fc1_bias, fc2, whole, split),
        out_specs=(split, split) + (whole,) * 15 + (fc1, fc1_bias, fc2, whole),
        check_vma=False,
    )
```
